256 devices in a mesh: filt: 8 (over x_lo, y), sx: 4 (over x_hi, core), sy: 8 (over z).
Axes of the slice: x: 4 (x_hi: 2, x_lo: 2; x = x_hi * 2 + x_lo), y: 4, z: 8, core: 2. Of those that a mesh axis runs over, the one named last changes fastest.
Arguments:
- activations: bfloat16 [8, 1, 32, 32, 2048], P('filt', None, 'sx', 'sy'), may hold values from -6 to 6
- weights: bfloat16 [8, 27, 32768], P('filt'), may hold values from -0.0546875 to 0.0546875
- out_grad: bfloat16 [8, 1, 32, 32, 2048], P('filt', None, 'sx', 'sy'), may hold values from -6 to 6
Outputs:
- outputs: bfloat16 [8, 1, 32, 32, 2048], P('filt', None, 'sx', 'sy')
- input_grad: bfloat16 [8, 1, 32, 32, 2048], P('filt', None, 'sx', 'sy')
- weight_grad: float32 [8, 27, 32768], P('filt', None, ('sx', 'sy'))
The draws below stay inside these ranges and needn't reach their ends.
All inputs are finite; a program needn't handle non-finite values.
Results may differ from the reference program's by a relative error of at most 0.02.
Values may be sent and summed in bfloat16 or wider, within the bound.
No kernel may reach another device: no remote copies, remote signals or barrier semaphores. Data moves between devices by JAX's collectives and lax.ppermute only.
A program may use at most 128 MiB of HBM per device.

```python
import math
import jax
import jax.numpy as jnp
from jax import lax

CIN = 512
COUT = 512
BATCH = 1
NZ = 32
CB = 64
NX = 32
NY = 32
N_FILT = 8


def levels(own_key, dims, cuts, low, high):
    loudness, own = 1.0, jax.random.fold_in(own_key, 6)
    for axis_at, blocks in cuts:
        heights = jnp.exp(jax.random.uniform(jax.random.fold_in(own, axis_at), (blocks,), jnp.float32, low / len(cuts), high / len(cuts)))
        loudness = loudness * jnp.repeat(heights, dims[axis_at] // blocks).reshape([-1 if axis == axis_at else 1 for axis in range(len(dims))])
    return loudness


def scatter_about(key, shape, width, reach, pieces=(), held_as=jnp.bfloat16):
    level = levels(key, shape, pieces, -0.22, 0.18) if pieces else 1.0
    entries = jax.random.normal(key, shape, jnp.float32) * width * level
    return jnp.minimum(jnp.maximum(entries, -reach), reach).astype(held_as)


def setup_inputs(seed: int = 0) -> dict:
    keys = jax.random.split(jax.random.key(seed), 4)
    return {
        "activations": scatter_about(keys[0], (N_FILT, BATCH, NX, NY, NZ * CB), 1.0, 6.0, ((0, 8), (2, 4), (3, 8))),
        "weights": scatter_about(keys[1], (N_FILT, 27, CIN * CB), (27 * CIN) ** -0.5, 0.0546875, ((0, 8),)),
        "out_grad": scatter_about(keys[2], (N_FILT, BATCH, NX, NY, NZ * CB), 1.0, 6.0, ((0, 8), (2, 4), (3, 8))),
    }


LEAK = 0.2
LAYOUT = ('NDHWC', 'DHWIO', 'NDHWC')

def activate(pre_act):
    return LEAK * pre_act + (1.0 - LEAK) * (jax.nn.softplus(pre_act) - math.log(2.0))

def slope_of(pre_act):
    return LEAK + (1.0 - LEAK) * jax.nn.sigmoid(pre_act)

def convolve(field, kernel):
    return lax.conv_general_dilated(field.astype(jnp.float32), kernel.astype(jnp.float32), (1, 1, 1), ((1, 1), (1, 1), (1, 1)), dimension_numbers=LAYOUT, precision=lax.Precision.HIGHEST)

def to_plain(field):
    moved = field.reshape(N_FILT, BATCH, NX, NY, NZ, CB).transpose(1, 2, 3, 4, 0, 5)
    return moved.reshape(BATCH, NX, NY, NZ, CIN)

def from_plain(field):
    moved = field.reshape(BATCH, NX, NY, NZ, N_FILT, CB).transpose(4, 0, 1, 2, 3, 5)
    return moved.reshape(N_FILT, BATCH, NX, NY, NZ * CB)

def reference(activations, weights, out_grad):
    act_plain = to_plain(activations)
    grad_plain = to_plain(out_grad)
    filters = weights.reshape(N_FILT, 27, CIN, CB).transpose(2, 1, 0, 3).reshape(CIN, 3, 3, 3, COUT)
    forward_kernel = jnp.transpose(filters, (1, 2, 3, 0, 4))
    pre_act = convolve(act_plain, forward_kernel)
    outputs = activate(pre_act).astype(jnp.bfloat16)
    pre_grad = (grad_plain.astype(jnp.float32) * slope_of(pre_act)).astype(jnp.bfloat16)
    back_kernel = jnp.transpose(filters, (1, 2, 3, 4, 0))[::-1, ::-1, ::-1]
    input_grad = convolve(pre_grad, back_kernel).astype(jnp.bfloat16)
    padded = jnp.pad(act_plain.astype(jnp.float32), ((0, 0), (1, 1), (1, 1), (1, 1), (0, 0)))
    grad_wide = pre_grad.astype(jnp.float32)
    collected = []
    for step_x in range(3):
        for step_y in range(3):
            for step_z in range(3):
                window = padded[:, step_x:step_x + NX, step_y:step_y + NY, step_z:step_z + NZ]
                collected.append(jnp.einsum('bxyzc,bxyzo->co', window, grad_wide, precision=lax.Precision.HIGHEST))
    scale = 1.0 / math.sqrt(BATCH * NX * NY * NZ)
    stacked = jnp.stack(collected, 1) * scale
    weight_grad = stacked.reshape(CIN, 27, N_FILT, CB).transpose(2, 1, 0, 3).reshape(N_FILT, 27, CIN * CB)
    return (from_plain(outputs), from_plain(input_grad), weight_grad)
```

```python
import math

import jax
import jax.numpy as jnp
from jax import lax
from jax.experimental import pallas as pl
from jax.experimental.pallas import tpu as pltpu
from jax.sharding import PartitionSpec as P

BF = jnp.bfloat16
F32 = jnp.float32
LEAK = 0.2
SCALE = 1.0 / math.sqrt(32768.0)
PIECE = (8, 4, 16, 128)


def call(kernel, outs, ins, scratch=(), flops=0, nbytes=0):
    return pl.pallas_call(
        kernel,
        out_shape=outs,
        in_specs=[
            pl.BlockSpec(memory_space=pltpu.VMEM if space is None else space)
            for _, space in ins
        ],
        out_specs=jax.tree.map(lambda _: pl.BlockSpec(memory_space=pltpu.VMEM), outs),
        scratch_shapes=list(scratch),
        compiler_params=pltpu.CompilerParams(vmem_limit_bytes=48 << 20),
        cost_estimate=pl.CostEstimate(flops=flops, bytes_accessed=nbytes, transcendentals=0),
    )(*[array for array, _ in ins])


def shape(dims, dtype=BF):
    return jax.ShapeDtypeStruct(dims, dtype)


def down(v):
    rows = lax.broadcasted_iota(jnp.int32, v.shape, 0)
    return jnp.where(rows == 0, 0.0, pltpu.roll(v, 1, 0))


def up(v):
    rows = lax.broadcasted_iota(jnp.int32, v.shape, 0)
    return jnp.where(rows == v.shape[0] - 1, 0.0, pltpu.roll(v, v.shape[0] - 1, 0))


def to_pairs(field_ref, pair_ref, wide):
    for x in range(8):
        rows = field_ref[x].astype(F32)
        for t in range(16):
            wide[pl.ds(x * 64 + t, 4, stride=16), :] = rows[:, t * 128 : (t + 1) * 128]
    pair_ref[...] = wide[...].reshape(PIECE).astype(BF)


def from_pairs(wide, field_ref):
    for x in range(8):
        parts = [wide[pl.ds(x * 64 + t, 4, stride=16), :] for t in range(16)]
        field_ref[x] = jnp.concatenate(parts, axis=1).astype(BF)


def prepare_field(field):
    def kernel(field_ref, pair_ref, wide):
        to_pairs(field_ref, pair_ref, wide)

    return call(
        kernel, shape(PIECE), [(field, None)], [pltpu.VMEM((512, 128), F32)], 0, 400_000
    )


def prepare_weights(weights):
    def kernel(w_ref, fore_ref, back_ref, tall, even, odd):
        def spread(t, carry):
            lanes = pl.ds(pl.multiple_of(t * 128, 128), 128)
            tall[pl.ds(t, 27, stride=256), :] = w_ref[:, lanes].astype(F32)
            return carry

        lax.fori_loop(0, 256, spread, 0, unroll=8)

        def place(ij, carry):
            taps = [tall[pl.ds(pl.multiple_of((ij * 3 + k) * 256, 256), 256), :] for k in range(3)]
            zero = jnp.zeros((256, 64), F32)
            for par in range(2):
                lanes = slice(par * 64, par * 64 + 64)
                even[pl.ds(par, 256, stride=2), :] = jnp.concatenate(
                    [taps[0][:, lanes], taps[1][:, lanes]], axis=1
                )
                odd[pl.ds(par, 256, stride=2), :] = jnp.concatenate([taps[2][:, lanes], zero], axis=1)
            fore_ref[ij, :, 0:128] = even[...].astype(BF)
            fore_ref[ij, :, 128:256] = odd[...].astype(BF)
            for c in range(4):
                rows = slice(c * 128, c * 128 + 128)
                back_ref[ij, 0:128, rows] = even[rows, :].T.astype(BF)
                back_ref[ij, 128:256, rows] = odd[rows, :].T.astype(BF)
            return carry

        lax.fori_loop(0, 9, place, 0)

    return call(
        kernel,
        (shape((9, 512, 256)), shape((9, 256, 512))),
        [(weights, None)],
        [pltpu.VMEM((27 * 256, 128), F32), pltpu.VMEM((512, 128), F32), pltpu.VMEM((512, 128), F32)],
        0,
        8_000_000,
    )


def forward(coords, pieces, y_before, y_after, x_before, x_after, fore, grad):
    def kernel(
        co, p0, p1, p2, p3, p4, p5, p6, p7, yb, ya, xb, xa, fore_ref, grad_ref,
        field_ref, out_ref, pre_ref, slots, total, wide, sems,
    ):
        col, row = co[0], co[1]
        copies = []
        for s, piece in enumerate((p0, p1, p2, p3, p4, p5, p6, p7)):
            owner = (col ^ (s // 4)) * 4 + ((row - s) & 3)
            copies.append(pltpu.make_async_copy(piece, slots.at[owner], sems.at[s]))
        for copy in copies:
            copy.start()

        def place(x, y, take):
            for q in range(4):
                a, b = take(2 * q), take(2 * q + 1)
                lanes = slice(q * 128, q * 128 + 128)
                field_ref[x, y * 32 : y * 32 + 16, lanes] = jnp.concatenate([a[:, :64], b[:, :64]], axis=1)
                field_ref[x, y * 32 + 16 : y * 32 + 32, lanes] = jnp.concatenate([a[:, 64:], b[:, 64:]], axis=1)

        def slot(owner):
            return ((owner // 4) ^ col) * 4 + ((row - owner) & 3)

        for y in range(6):
            place(0, y, lambda f: xb[slot(f), y])
            place(9, y, lambda f: xa[slot(f), y])
        for copy in copies:
            copy.wait()

        def place_x(x, carry):
            place(x + 1, 0, lambda f: yb[slot(f), x])
            place(x + 1, 5, lambda f: ya[slot(f), x])
            for y in range(4):
                place(x + 1, y + 1, lambda f: slots[f, x, y])
            return carry

        lax.fori_loop(0, 8, place_x, 0)

        def multiply(h, carry):
            acc = jnp.zeros((256, 256), F32)
            for i in range(3):
                for j in range(3):
                    rows = [field_ref[2 * h + u + i, j * 32 : j * 32 + 128, :] for u in range(2)]
                    acc = acc + jnp.dot(
                        jnp.concatenate(rows, axis=0), fore_ref[i * 3 + j], preferred_element_type=F32
                    )
            total[pl.ds(pl.multiple_of(h * 256, 256), 256), :] = acc
            return carry

        lax.fori_loop(0, 4, multiply, 0)

        def finish(x, carry):
            for y in range(4):
                start = pl.multiple_of(x * 128 + y * 32, 32)
                even, odd = total[pl.ds(start, 16), :], total[pl.ds(start + 16, 16), :]
                pre = (
                    jnp.concatenate([down(odd[:, 0:64]), even[:, 0:64]], axis=1)
                    + jnp.concatenate([even[:, 64:128], odd[:, 64:128]], axis=1)
                    + jnp.concatenate([odd[:, 128:192], up(even[:, 128:192])], axis=1)
                )
                e = jnp.exp(-jnp.abs(pre))
                soft = jnp.maximum(pre, 0.0) + jnp.log1p(e)
                slope = jnp.where(pre >= 0, 1.0, e) / (1.0 + e)
                value = LEAK * pre + (1.0 - LEAK) * (soft - math.log(2.0))
                wide[pl.ds(pl.multiple_of(x * 64 + y * 16, 16), 16), :] = value
                g = grad_ref[x, y].astype(F32)
                pre_ref[x, y] = (g * (LEAK + (1.0 - LEAK) * slope)).astype(BF)
            return carry

        lax.fori_loop(0, 8, finish, 0)
        from_pairs(wide, out_ref)

    return call(
        kernel,
        (shape((10, 192, 512)), shape((8, 4, 2048)), shape(PIECE)),
        [(coords, pltpu.SMEM)]
        + [(piece, pl.ANY) for piece in pieces]
        + [(a, None) for a in (y_before, y_after, x_before, x_after, fore, grad)],
        [
            pltpu.VMEM((8,) + PIECE, BF),
            pltpu.VMEM((1024, 256), F32),
            pltpu.VMEM((512, 128), F32),
            pltpu.SemaphoreType.DMA((8,)),
        ],
        5_000_000_000,
        6_000_000,
    )


def stacked_depth(v):
    even, odd = v[:, :64], v[:, 64:]
    zero = jnp.zeros((16, 64), F32)
    return (
        (jnp.concatenate([odd, even], axis=1), jnp.concatenate([down(odd), zero], axis=1)),
        (jnp.concatenate([up(even), odd], axis=1), jnp.concatenate([even, zero], axis=1)),
    )


def filter_grad(coords, field, pre_grad):
    def kernel(co, field_ref, pre_ref, keep_ref, send_ref, first, second, turned):
        core = co[2]

        def place(x, carry):
            for y in range(4):
                low, high = stacked_depth(pre_ref[x, y].astype(F32))
                first[y * 32 : y * 32 + 16, :] = low[0]
                second[y * 32 : y * 32 + 16, :] = low[1]
                first[y * 32 + 16 : y * 32 + 32, :] = high[0]
                second[y * 32 + 16 : y * 32 + 32, :] = high[1]
            lanes = pl.ds(pl.multiple_of(x * 128, 128), 128)
            turned[0:128, lanes] = first[...].T.astype(BF)
            turned[128:192, lanes] = second[...].T[0:64].astype(BF)
            return carry

        lax.fori_loop(0, 8, place, 0)

        def multiply(ij, carry):
            i, j = ij // 3, ij % 3
            start = pl.multiple_of(j * 32, 32)
            for half in range(2):
                lanes = slice(half * 256, half * 256 + 256)
                rows = [field_ref[x + i, pl.ds(start, 128), lanes] for x in range(8)]
                got = jnp.dot(
                    turned[...], jnp.concatenate(rows, axis=0), preferred_element_type=F32
                ) * SCALE
                left, right = got[:, :128], got[:, 128:]
                keep_ref[half, ij] = jnp.where(core == 0, left, right)
                send_ref[half, ij] = jnp.where(core == 0, right, left).astype(BF)
            return carry

        lax.fori_loop(0, 9, multiply, 0)

    return call(
        kernel,
        (shape((2, 9, 192, 128), F32), shape((2, 9, 192, 128))),
        [(coords, pltpu.SMEM), (field, None), (pre_grad, None)],
        [pltpu.VMEM((128, 128), F32), pltpu.VMEM((128, 128), F32), pltpu.VMEM((192, 1024), BF)],
        5_000_000_000,
        6_000_000,
    )


def add_cores(coords, keep, got):
    def kernel(co, keep_ref, got_ref, stay_ref, send_ref):
        far = co[3]
        stay_ref[...] = keep_ref[far] + got_ref[far].astype(F32)
        send_ref[...] = (keep_ref[1 - far] + got_ref[1 - far].astype(F32)).astype(BF)

    return call(
        kernel,
        (shape((9, 192, 128), F32), shape((9, 192, 128))),
        [(coords, pltpu.SMEM), (keep, None), (got, None)],
        (),
        0,
        4_000_000,
    )


def add_far(coords, stay, got):
    def kernel(co, stay_ref, got_ref, *outs):
        out_ref, total, turned = outs
        sy = co[4]
        total[...] = (stay_ref[...] + got_ref[...].astype(F32)).reshape(1728, 128)
        for t in range(14):
            width = min(128, 1728 - t * 128)
            turned[:, t * 128 : t * 128 + width] = total[t * 128 : t * 128 + width, :].T.astype(BF)
        for s in range(8):
            out_ref[(s - sy) & 7] = turned[s * 16 : s * 16 + 16, :]

    return call(
        kernel,
        shape((8, 16, 1728)),
        [(coords, pltpu.SMEM), (stay, None), (got, None)],
        [pltpu.VMEM((1728, 128), F32), pltpu.VMEM((128, 1728), BF)],
        0,
        2_000_000,
    )


def add_regions(parts):
    def kernel(*refs):
        ins, (out_ref, total, pairs) = refs[:8], refs[8:]
        for t in range(14):
            width = min(128, 1728 - t * 128)
            lanes = slice(t * 128, t * 128 + width)
            s = ins[0][:, lanes].astype(F32)
            for ref in ins[1:]:
                s = s + ref[:, lanes].astype(F32)
            total[:, 0:width] = s
            even, odd = total[pl.ds(0, 8, stride=2), :], total[pl.ds(1, 8, stride=2), :]
            for u in range(width // 64):
                pick = slice(u * 64, u * 64 + 64)
                at = (2 * t + u) * 8
                pairs[at : at + 8, :] = jnp.concatenate([even[:, pick], odd[:, pick]], axis=1)
        for cp in range(8):
            out_ref[:, cp * 128 : cp * 128 + 128] = pairs[pl.ds(cp, 27, stride=8), :]

    return call(
        kernel,
        shape((27, 1024), F32),
        [(part, None) for part in parts],
        [pltpu.VMEM((16, 128), F32), pltpu.VMEM((216, 128), F32)],
        0,
        600_000,
    )


def input_grad_parts(coords, pre_grad, y_before, y_after, x_before, x_after, back):
    def kernel(co, pre_ref, yb, ya, xb, xa, back_ref, out_ref, rim, total):
        col, row = co[0], co[1]

        def place(x, y, v):
            low, high = stacked_depth(v.astype(F32))
            for half in range(2):
                lanes = slice(half * 128, half * 128 + 128)
                rim[x, y * 32 : y * 32 + 16, lanes] = low[half].astype(BF)
                rim[x, y * 32 + 16 : y * 32 + 32, lanes] = high[half].astype(BF)

        for y in range(6):
            place(0, y, xb[y])
            place(9, y, xa[y])

        def place_x(x, carry):
            place(x + 1, 0, yb[x])
            place(x + 1, 5, ya[x])
            for y in range(4):
                place(x + 1, y + 1, pre_ref[x, y])
            return carry

        lax.fori_loop(0, 8, place_x, 0)

        def multiply(h, carry):
            for n in range(2):
                lanes = slice(n * 256, n * 256 + 256)
                acc = jnp.zeros((256, 256), F32)
                for i in range(3):
                    for j in range(3):
                        at = (2 - j) * 32
                        rows = [rim[2 * h + u + 2 - i, at : at + 128, :] for u in range(2)]
                        acc = acc + jnp.dot(
                            jnp.concatenate(rows, axis=0),
                            back_ref[i * 3 + j, :, lanes],
                            preferred_element_type=F32,
                        )
                total[:, lanes] = acc
            for u in range(2):
                for y in range(4):
                    at = u * 128 + y * 32
                    for f in range(8):
                        lanes = slice(f * 64, f * 64 + 64)
                        pair = jnp.concatenate(
                            [total[at : at + 16, lanes], total[at + 16 : at + 32, lanes]], axis=1
                        )
                        slot = ((f // 4) ^ col) * 4 + ((f - row) & 3)
                        out_ref[slot, 2 * h + u, y] = pair.astype(BF)
            return carry

        lax.fori_loop(0, 4, multiply, 0)

    return call(
        kernel,
        shape((8,) + PIECE),
        [(coords, pltpu.SMEM)]
        + [(a, None) for a in (pre_grad, y_before, y_after, x_before, x_after, back)],
        [pltpu.VMEM((10, 192, 256), BF), pltpu.VMEM((256, 512), F32)],
        5_000_000_000,
        5_000_000,
    )


def add_blocks(parts):
    def kernel(*refs):
        ins, (out_ref, wide) = refs[:8], refs[8:]
        s = ins[0][...].astype(F32)
        for ref in ins[1:]:
            s = s + ref[...].astype(F32)
        wide[...] = s.reshape(512, 128)
        from_pairs(wide, out_ref)

    return call(
        kernel,
        shape((8, 4, 2048)),
        [(part, None) for part in parts],
        [pltpu.VMEM((512, 128), F32)],
        0,
        1_200_000,
    )


def along_filt(slot):
    return [(f, ((f // 4) ^ (slot // 4)) * 4 + (f + slot) % 4) for f in range(8)]


ORDER = (2, 6, 1, 3, 5, 7, 4)


def rims(field, y_dim, join):
    ups = [(i, i + 1) for i in range(7)]
    downs = [(i + 1, i) for i in range(7)]
    first, last = join(3), join(0)
    y_before = lax.ppermute(first, "sy", ups)
    y_after = lax.ppermute(last, "sy", downs)
    x_last = field(7, y_before, y_after)
    x_first = field(0, y_before, y_after)
    x_before = lax.ppermute(x_last, "sx", ups[:3])
    x_after = lax.ppermute(x_first, "sx", downs[:3])
    return y_before, y_after, x_before, x_after


def per_device(activations, weights, out_grad):
    filt, sx, sy = (lax.axis_index(a) for a in ("filt", "sx", "sy"))
    coords = jnp.stack([filt // 4, filt % 4, sx % 2, sx // 2, sy, 0, 0, 0]).astype(jnp.int32)
    own = prepare_field(activations[0, 0])
    pieces = {0: own}
    for s in ORDER:
        pieces[s] = lax.ppermute(own, "filt", along_filt(s))
    pieces = [pieces[s] for s in range(8)]
    fore, back = prepare_weights(weights[0])
    grad = prepare_field(out_grad[0, 0])

    halos = rims(
        lambda x, yb, ya: jnp.concatenate(
            [yb[:, x : x + 1], jnp.stack([p[x] for p in pieces]), ya[:, x : x + 1]], axis=1
        ),
        1,
        lambda y: jnp.stack([p[:, y] for p in pieces]),
    )
    field, outputs, pre_grad = forward(coords, pieces, *halos, fore, grad)

    grad_halos = rims(
        lambda x, yb, ya: jnp.concatenate([yb[x : x + 1], pre_grad[x], ya[x : x + 1]], axis=0),
        1,
        lambda y: pre_grad[:, y],
    )
    keep, send = filter_grad(coords, field, pre_grad)
    got = lax.ppermute(send, "sx", [(i, i ^ 1) for i in range(4)])
    stay, send = add_cores(coords, keep, got)
    got = lax.ppermute(send, "sx", [(i, i ^ 2) for i in range(4)])

    parts = input_grad_parts(coords, pre_grad, *grad_halos, back)
    sums = {0: parts[0]}
    for s in ORDER:
        sums[s] = lax.ppermute(parts[s], "filt", along_filt(s))

    turned = add_far(coords, stay, got)
    regions = [turned[0]]
    for d in range(1, 8):
        regions.append(lax.ppermute(turned[d], "sy", [(i, (i + d) % 8) for i in range(8)]))

    input_grad = add_blocks([sums[s] for s in range(8)])
    weight_grad = add_regions(regions)
    return outputs[None, None], input_grad[None, None], weight_grad[None]


def solution(mesh):
    in_specs = (
        P("filt", None, "sx", "sy", None),
        P("filt", None, None),
        P("filt", None, "sx", "sy", None),
    )
    out_specs = (
        P("filt", None, "sx", "sy", None),
        P("filt", None, "sx", "sy", None),
        P("filt", None, ("sx", "sy")),
    )
    return jax.shard_map(
        per_device, mesh=mesh, in_specs=in_specs, out_specs=out_specs, check_vma=False
    )
```

```python
import math

import jax
import jax.numpy as jnp
from jax import lax
from jax.experimental import pallas as pl
from jax.experimental.pallas import tpu as pltpu
from jax.sharding import PartitionSpec as P

BF = jnp.bfloat16
F32 = jnp.float32
LEAK = 0.2
SCALE = 1.0 / math.sqrt(32768.0)
PIECE = (8, 4, 16, 128)


def call(kernel, outs, ins, scratch=(), flops=0, nbytes=0):
    return pl.pallas_call(
        kernel,
        out_shape=outs,
        in_specs=[
            pl.BlockSpec(memory_space=pltpu.VMEM if space is None else space)
            for _, space in ins
        ],
        out_specs=jax.tree.map(lambda _: pl.BlockSpec(memory_space=pltpu.VMEM), outs),
        scratch_shapes=list(scratch),
        compiler_params=pltpu.CompilerParams(vmem_limit_bytes=48 << 20),
        cost_estimate=pl.CostEstimate(flops=flops, bytes_accessed=nbytes, transcendentals=0),
    )(*[array for array, _ in ins])


def shape(dims, dtype=BF):
    return jax.ShapeDtypeStruct(dims, dtype)


def down(v):
    rows = lax.broadcasted_iota(jnp.int32, v.shape, 0)
    return jnp.where(rows == 0, 0.0, pltpu.roll(v, 1, 0))


def up(v):
    rows = lax.broadcasted_iota(jnp.int32, v.shape, 0)
    return jnp.where(rows == v.shape[0] - 1, 0.0, pltpu.roll(v, v.shape[0] - 1, 0))


def to_pairs(field_ref, pair_ref, wide):
    for x in range(8):
        rows = field_ref[x].astype(F32)
        for t in range(16):
            wide[pl.ds(x * 64 + t, 4, stride=16), :] = rows[:, t * 128 : (t + 1) * 128]
    pair_ref[...] = wide[...].reshape(PIECE).astype(BF)


def from_pairs(wide, field_ref):
    for x in range(8):
        parts = [wide[pl.ds(x * 64 + t, 4, stride=16), :] for t in range(16)]
        field_ref[x] = jnp.concatenate(parts, axis=1).astype(BF)


def prepare_field(field):
    def kernel(field_ref, pair_ref, wide):
        to_pairs(field_ref, pair_ref, wide)

    return call(
        kernel, shape(PIECE), [(field, None)], [pltpu.VMEM((512, 128), F32)], 0, 400_000
    )


def prepare_gather(field):
    def kernel(field_ref, edge_ref, middle_ref, wide):
        for x in range(8):
            rows = field_ref[x].astype(F32)
            for t in range(16):
                wide[pl.ds(x * 16 + t, 4, stride=128), :] = rows[:, t * 128 : (t + 1) * 128]
        for y, (ref, at) in enumerate(((edge_ref, 0), (middle_ref, 0), (middle_ref, 1), (edge_ref, 1))):
            row = wide[y * 128 : y * 128 + 128, :].reshape(8, 16, 128).astype(BF)
            for f in range(8):
                ref[f, at] = row

    out = shape((8, 2, 8, 16, 128))
    return call(kernel, (out, out), [(field, None)], [pltpu.VMEM((512, 128), F32)], 0, 1_300_000)


def gather_edges(edge, middle, y_before, y_after):
    def kernel(edge_ref, middle_ref, yb, ya, last_ref, first_ref):
        for out_ref, x in ((last_ref, 7), (first_ref, 0)):
            for f in range(8):
                out_ref[f, 0] = yb[f, x]
                out_ref[f, 1] = edge_ref[f, 0, x]
                out_ref[f, 2] = middle_ref[f, 0, x]
                out_ref[f, 3] = middle_ref[f, 1, x]
                out_ref[f, 4] = edge_ref[f, 1, x]
                out_ref[f, 5] = ya[f, x]

    out = shape((8, 6, 16, 128))
    ins = [(a, None) for a in (edge, middle, y_before, y_after)]
    return call(kernel, (out, out), ins, (), 0, 400_000)


def grad_edges(pre_grad, y_before, y_after):
    def kernel(pre_ref, yb, ya, last_ref, first_ref):
        for out_ref, x in ((last_ref, 7), (first_ref, 0)):
            out_ref[0] = yb[x]
            out_ref[1:5] = pre_ref[x]
            out_ref[5] = ya[x]

    out = shape((6, 16, 128))
    ins = [(a, None) for a in (pre_grad, y_before, y_after)]
    return call(kernel, (out, out), ins, (), 0, 50_000)


def prepare_weights(weights):
    def kernel(w_ref, fore_ref, back_ref, tall, even, odd):
        def spread(t, carry):
            lanes = pl.ds(pl.multiple_of(t * 128, 128), 128)
            tall[pl.ds(t, 27, stride=256), :] = w_ref[:, lanes].astype(F32)
            return carry

        lax.fori_loop(0, 256, spread, 0, unroll=8)

        def place(ij, carry):
            taps = [tall[pl.ds(pl.multiple_of((ij * 3 + k) * 256, 256), 256), :] for k in range(3)]
            zero = jnp.zeros((256, 64), F32)
            for par in range(2):
                lanes = slice(par * 64, par * 64 + 64)
                even[pl.ds(par, 256, stride=2), :] = jnp.concatenate(
                    [taps[0][:, lanes], taps[1][:, lanes]], axis=1
                )
                odd[pl.ds(par, 256, stride=2), :] = jnp.concatenate([taps[2][:, lanes], zero], axis=1)
            fore_ref[ij, :, 0:128] = even[...].astype(BF)
            fore_ref[ij, :, 128:256] = odd[...].astype(BF)
            for c in range(4):
                rows = slice(c * 128, c * 128 + 128)
                back_ref[ij, 0:128, rows] = even[rows, :].T.astype(BF)
                back_ref[ij, 128:256, rows] = odd[rows, :].T.astype(BF)
            return carry

        lax.fori_loop(0, 9, place, 0)

    return call(
        kernel,
        (shape((9, 512, 256)), shape((9, 256, 512))),
        [(weights, None)],
        [pltpu.VMEM((27 * 256, 128), F32), pltpu.VMEM((512, 128), F32), pltpu.VMEM((512, 128), F32)],
        0,
        8_000_000,
    )


def masked(v, inside):
    return jnp.where(inside, v, jnp.zeros_like(v))


def forward(coords, edge, middle, y_before, y_after, x_before, x_after, fore, grad):
    def kernel(
        co, edge_ref, middle_ref, yb, ya, xb, xa, fore_ref, grad_ref,
        field_ref, out_ref, pre_ref, first_ref, last_ref, total, wide,
    ):
        y_low, y_high, x_low, x_high = co[4] > 0, co[4] < 7, co[5] > 0, co[5] < 3

        def place(x, y, take):
            for q in range(4):
                a, b = take(2 * q), take(2 * q + 1)
                lanes = slice(q * 128, q * 128 + 128)
                field_ref[x, y * 32 : y * 32 + 16, lanes] = jnp.concatenate([a[:, :64], b[:, :64]], axis=1)
                field_ref[x, y * 32 + 16 : y * 32 + 32, lanes] = jnp.concatenate([a[:, 64:], b[:, 64:]], axis=1)

        for y in range(6):
            beside = {0: y_low, 5: y_high}.get(y, True)
            place(0, y, lambda f: masked(xb[f, y], jnp.logical_and(x_low, beside)))
            place(9, y, lambda f: masked(xa[f, y], jnp.logical_and(x_high, beside)))

        def place_x(x, carry):
            place(x + 1, 0, lambda f: masked(yb[f, x], y_low))
            place(x + 1, 5, lambda f: masked(ya[f, x], y_high))
            place(x + 1, 1, lambda f: edge_ref[f, 0, x])
            place(x + 1, 2, lambda f: middle_ref[f, 0, x])
            place(x + 1, 3, lambda f: middle_ref[f, 1, x])
            place(x + 1, 4, lambda f: edge_ref[f, 1, x])
            return carry

        lax.fori_loop(0, 8, place_x, 0)

        def multiply(h, carry):
            acc = jnp.zeros((256, 256), F32)
            for i in range(3):
                for j in range(3):
                    rows = [field_ref[2 * h + u + i, j * 32 : j * 32 + 128, :] for u in range(2)]
                    acc = acc + jnp.dot(
                        jnp.concatenate(rows, axis=0), fore_ref[i * 3 + j], preferred_element_type=F32
                    )
            total[pl.ds(pl.multiple_of(h * 256, 256), 256), :] = acc
            return carry

        lax.fori_loop(0, 4, multiply, 0)

        def finish(x, carry):
            for y in range(4):
                start = pl.multiple_of(x * 128 + y * 32, 32)
                even, odd = total[pl.ds(start, 16), :], total[pl.ds(start + 16, 16), :]
                pre = (
                    jnp.concatenate([down(odd[:, 0:64]), even[:, 0:64]], axis=1)
                    + jnp.concatenate([even[:, 64:128], odd[:, 64:128]], axis=1)
                    + jnp.concatenate([odd[:, 128:192], up(even[:, 128:192])], axis=1)
                )
                e = jnp.exp(-jnp.abs(pre))
                soft = jnp.maximum(pre, 0.0) + jnp.log1p(e)
                slope = jnp.where(pre >= 0, 1.0, e) / (1.0 + e)
                value = LEAK * pre + (1.0 - LEAK) * (soft - math.log(2.0))
                wide[pl.ds(pl.multiple_of(x * 64 + y * 16, 16), 16), :] = value
                g = grad_ref[x, y].astype(F32)
                turned = (g * (LEAK + (1.0 - LEAK) * slope)).astype(BF)
                pre_ref[x, y] = turned
                if y == 0:
                    first_ref[x] = turned
                if y == 3:
                    last_ref[x] = turned
            return carry

        lax.fori_loop(0, 8, finish, 0)
        from_pairs(wide, out_ref)

    return call(
        kernel,
        (
            shape((10, 192, 512)),
            shape((8, 4, 2048)),
            shape(PIECE),
            shape((8, 16, 128)),
            shape((8, 16, 128)),
        ),
        [(coords, pltpu.SMEM)]
        + [
            (a, None)
            for a in (edge, middle, y_before, y_after, x_before, x_after, fore, grad)
        ],
        [pltpu.VMEM((1024, 256), F32), pltpu.VMEM((512, 128), F32)],
        5_000_000_000,
        6_000_000,
    )


def stacked_depth(v):
    even, odd = v[:, :64], v[:, 64:]
    zero = jnp.zeros((16, 64), F32)
    return (
        (jnp.concatenate([odd, even], axis=1), jnp.concatenate([down(odd), zero], axis=1)),
        (jnp.concatenate([up(even), odd], axis=1), jnp.concatenate([even, zero], axis=1)),
    )


def filter_grad(coords, field, pre_grad):
    def kernel(co, field_ref, pre_ref, keep_ref, send_ref, first, second, turned):
        core = co[2]

        def place(x, carry):
            for y in range(4):
                low, high = stacked_depth(pre_ref[x, y].astype(F32))
                first[y * 32 : y * 32 + 16, :] = low[0]
                second[y * 32 : y * 32 + 16, :] = low[1]
                first[y * 32 + 16 : y * 32 + 32, :] = high[0]
                second[y * 32 + 16 : y * 32 + 32, :] = high[1]
            lanes = pl.ds(pl.multiple_of(x * 128, 128), 128)
            turned[0:128, lanes] = first[...].T.astype(BF)
            turned[128:192, lanes] = second[...].T[0:64].astype(BF)
            return carry

        lax.fori_loop(0, 8, place, 0)

        def multiply(ij, carry):
            i, j = ij // 3, ij % 3
            start = pl.multiple_of(j * 32, 32)
            for half in range(2):
                lanes = slice(half * 256, half * 256 + 256)
                rows = [field_ref[x + i, pl.ds(start, 128), lanes] for x in range(8)]
                got = jnp.dot(
                    turned[...], jnp.concatenate(rows, axis=0), preferred_element_type=F32
                ) * SCALE
                left, right = got[:, :128], got[:, 128:]
                keep_ref[half, ij] = jnp.where(core == 0, left, right)
                send_ref[half, ij] = jnp.where(core == 0, right, left).astype(BF)
            return carry

        lax.fori_loop(0, 9, multiply, 0)

    return call(
        kernel,
        (shape((2, 9, 192, 128), F32), shape((2, 9, 192, 128))),
        [(coords, pltpu.SMEM), (field, None), (pre_grad, None)],
        [pltpu.VMEM((128, 128), F32), pltpu.VMEM((128, 128), F32), pltpu.VMEM((192, 1024), BF)],
        5_000_000_000,
        6_000_000,
    )


def add_cores(coords, keep, got):
    def kernel(co, keep_ref, got_ref, stay_ref, send_ref):
        far = co[3]
        stay_ref[...] = keep_ref[far] + got_ref[far].astype(F32)
        send_ref[...] = (keep_ref[1 - far] + got_ref[1 - far].astype(F32)).astype(BF)

    return call(
        kernel,
        (shape((9, 192, 128), F32), shape((9, 192, 128))),
        [(coords, pltpu.SMEM), (keep, None), (got, None)],
        (),
        0,
        4_000_000,
    )


def add_far(stay, got):
    def kernel(stay_ref, got_ref, out_ref, total, turned):
        total[...] = (stay_ref[...] + got_ref[...].astype(F32)).reshape(1728, 128)
        for t in range(14):
            width = min(128, 1728 - t * 128)
            turned[:, t * 128 : t * 128 + width] = total[t * 128 : t * 128 + width, :].T.astype(BF)
        for s in range(8):
            out_ref[s] = turned[s * 16 : s * 16 + 16, :]

    return call(
        kernel,
        shape((8, 16, 1728)),
        [(stay, None), (got, None)],
        [pltpu.VMEM((1728, 128), F32), pltpu.VMEM((128, 1728), BF)],
        0,
        2_000_000,
    )


def add_regions(parts):
    def kernel(parts_ref, out_ref, total, pairs):
        for t in range(14):
            width = min(128, 1728 - t * 128)
            lanes = slice(t * 128, t * 128 + width)
            s = parts_ref[0, :, lanes].astype(F32)
            for d in range(1, 8):
                s = s + parts_ref[d, :, lanes].astype(F32)
            total[:, 0:width] = s
            even, odd = total[pl.ds(0, 8, stride=2), :], total[pl.ds(1, 8, stride=2), :]
            for u in range(width // 64):
                pick = slice(u * 64, u * 64 + 64)
                at = (2 * t + u) * 8
                pairs[at : at + 8, :] = jnp.concatenate([even[:, pick], odd[:, pick]], axis=1)
        for cp in range(8):
            out_ref[:, cp * 128 : cp * 128 + 128] = pairs[pl.ds(cp, 27, stride=8), :]

    return call(
        kernel,
        shape((27, 1024), F32),
        [(parts, None)],
        [pltpu.VMEM((16, 128), F32), pltpu.VMEM((216, 128), F32)],
        0,
        600_000,
    )


def input_grad_parts(coords, pre_grad, y_before, y_after, x_before, x_after, back):
    def kernel(co, pre_ref, yb, ya, xb, xa, back_ref, out_ref, rim, total):
        y_low, y_high, x_low, x_high = co[4] > 0, co[4] < 7, co[5] > 0, co[5] < 3

        def place(x, y, v):
            low, high = stacked_depth(v.astype(F32))
            for half in range(2):
                lanes = slice(half * 128, half * 128 + 128)
                rim[x, y * 32 : y * 32 + 16, lanes] = low[half].astype(BF)
                rim[x, y * 32 + 16 : y * 32 + 32, lanes] = high[half].astype(BF)

        for y in range(6):
            beside = {0: y_low, 5: y_high}.get(y, True)
            place(0, y, masked(xb[y], jnp.logical_and(x_low, beside)))
            place(9, y, masked(xa[y], jnp.logical_and(x_high, beside)))

        def place_x(x, carry):
            place(x + 1, 0, masked(yb[x], y_low))
            place(x + 1, 5, masked(ya[x], y_high))
            for y in range(4):
                place(x + 1, y + 1, pre_ref[x, y])
            return carry

        lax.fori_loop(0, 8, place_x, 0)

        def multiply(h, carry):
            for n in range(2):
                lanes = slice(n * 256, n * 256 + 256)
                acc = jnp.zeros((256, 256), F32)
                for i in range(3):
                    for j in range(3):
                        at = (2 - j) * 32
                        rows = [rim[2 * h + u + 2 - i, at : at + 128, :] for u in range(2)]
                        acc = acc + jnp.dot(
                            jnp.concatenate(rows, axis=0),
                            back_ref[i * 3 + j, :, lanes],
                            preferred_element_type=F32,
                        )
                total[:, lanes] = acc
            for u in range(2):
                for y in range(4):
                    at = u * 128 + y * 32
                    for f in range(8):
                        lanes = slice(f * 64, f * 64 + 64)
                        pair = jnp.concatenate(
                            [total[at : at + 16, lanes], total[at + 16 : at + 32, lanes]], axis=1
                        )
                        out_ref[f, 2 * h + u, y] = pair.astype(BF)
            return carry

        lax.fori_loop(0, 4, multiply, 0)

    return call(
        kernel,
        shape((8,) + PIECE),
        [(coords, pltpu.SMEM)]
        + [(a, None) for a in (pre_grad, y_before, y_after, x_before, x_after, back)],
        [pltpu.VMEM((10, 192, 256), BF), pltpu.VMEM((256, 512), F32)],
        5_000_000_000,
        5_000_000,
    )


def add_blocks(parts):
    def kernel(parts_ref, out_ref, wide):
        s = parts_ref[0].astype(F32)
        for f in range(1, 8):
            s = s + parts_ref[f].astype(F32)
        wide[...] = s.reshape(512, 128)
        from_pairs(wide, out_ref)

    return call(
        kernel,
        shape((8, 4, 2048)),
        [(parts, None)],
        [pltpu.VMEM((512, 128), F32)],
        0,
        1_200_000,
    )


def both_ways(last, first, axis, size):
    return (
        lax.ppermute(last, axis, [(i, (i + 1) % size) for i in range(size)]),
        lax.ppermute(first, axis, [((i + 1) % size, i) for i in range(size)]),
    )


def exchange(parts, axis):
    return lax.all_to_all(parts, axis, 0, 0)


def per_device(activations, weights, out_grad):
    filt, sx, sy = (lax.axis_index(a) for a in ("filt", "sx", "sy"))
    coords = jnp.stack([filt // 4, filt % 4, sx % 2, sx // 2, sy, sx, 0, 0]).astype(jnp.int32)
    edge, middle = prepare_gather(activations[0, 0])
    edge = exchange(edge, "filt")
    middle, edge = lax.optimization_barrier((middle, edge))
    y_before, y_after = both_ways(edge[:, 1], edge[:, 0], "sy", 8)
    middle = exchange(middle, "filt")
    middle, weights, out_grad = lax.optimization_barrier((middle, weights, out_grad))
    x_last, x_first = gather_edges(edge, middle, y_before, y_after)
    x_before, x_after = both_ways(x_last, x_first, "sx", 4)
    fore, back = prepare_weights(weights[0])
    grad = prepare_field(out_grad[0, 0])
    field, outputs, pre_grad, g_first, g_last = forward(
        coords, edge, middle, y_before, y_after, x_before, x_after, fore, grad
    )

    gy_before, gy_after = both_ways(g_last, g_first, "sy", 8)
    keep, send = filter_grad(coords, field, pre_grad)
    got = lax.ppermute(send, "sx", [(i, i ^ 1) for i in range(4)])
    gx_before, gx_after = both_ways(*grad_edges(pre_grad, gy_before, gy_after), "sx", 4)
    stay, send = add_cores(coords, keep, got)
    send, pre_grad = lax.optimization_barrier((send, pre_grad))
    got = lax.ppermute(send, "sx", [(i, i ^ 2) for i in range(4)])

    parts = input_grad_parts(coords, pre_grad, gy_before, gy_after, gx_before, gx_after, back)
    parts = exchange(parts, "filt")
    regions = exchange(add_far(stay, got), "sy")
    input_grad = add_blocks(parts)
    weight_grad = add_regions(regions)
    return outputs[None, None], input_grad[None, None], weight_grad[None]


def solution(mesh):
    in_specs = (
        P("filt", None, "sx", "sy", None),
        P("filt", None, None),
        P("filt", None, "sx", "sy", None),
    )
    out_specs = (
        P("filt", None, "sx", "sy", None),
        P("filt", None, "sx", "sy", None),
        P("filt", None, ("sx", "sy")),
    )
    return jax.shard_map(
        per_device, mesh=mesh, in_specs=in_specs, out_specs=out_specs, check_vma=False
    )
```

```python
import math

import jax
import jax.numpy as jnp
from jax import lax
from jax.experimental import pallas as pl
from jax.experimental.pallas import tpu as pltpu
from jax.sharding import PartitionSpec as P

BF = jnp.bfloat16
F32 = jnp.float32
LEAK = 0.2
SCALE = 1.0 / math.sqrt(32768.0)
PIECE = (8, 4, 16, 128)


def call(kernel, outs, ins, scratch=(), flops=0, nbytes=0):
    return pl.pallas_call(
        kernel,
        out_shape=outs,
        in_specs=[
            pl.BlockSpec(memory_space=pltpu.VMEM if space is None else space)
            for _, space in ins
        ],
        out_specs=jax.tree.map(lambda _: pl.BlockSpec(memory_space=pltpu.VMEM), outs),
        scratch_shapes=list(scratch),
        compiler_params=pltpu.CompilerParams(vmem_limit_bytes=48 << 20),
        cost_estimate=pl.CostEstimate(flops=flops, bytes_accessed=nbytes, transcendentals=0),
    )(*[array for array, _ in ins])


def shape(dims, dtype=BF):
    return jax.ShapeDtypeStruct(dims, dtype)


def down(v):
    rows = lax.broadcasted_iota(jnp.int32, v.shape, 0)
    return jnp.where(rows == 0, 0.0, pltpu.roll(v, 1, 0))


def up(v):
    rows = lax.broadcasted_iota(jnp.int32, v.shape, 0)
    return jnp.where(rows == v.shape[0] - 1, 0.0, pltpu.roll(v, v.shape[0] - 1, 0))


def to_pairs(field_ref, pair_ref, wide):
    for x in range(8):
        rows = field_ref[x].astype(F32)
        for t in range(16):
            wide[pl.ds(x * 64 + t, 4, stride=16), :] = rows[:, t * 128 : (t + 1) * 128]
    pair_ref[...] = wide[...].reshape(PIECE).astype(BF)


def from_pairs(wide, field_ref):
    for x in range(8):
        parts = [wide[pl.ds(x * 64 + t, 4, stride=16), :] for t in range(16)]
        field_ref[x] = jnp.concatenate(parts, axis=1).astype(BF)


def prepare_field(field):
    def kernel(field_ref, pair_ref, wide):
        to_pairs(field_ref, pair_ref, wide)

    return call(
        kernel, shape(PIECE), [(field, None)], [pltpu.VMEM((512, 128), F32)], 0, 400_000
    )


def prepare_gather(field):
    def kernel(field_ref, out_ref, wide):
        for x in range(8):
            rows = field_ref[x].astype(F32)
            for t in range(16):
                wide[pl.ds(x * 16 + t, 4, stride=128), :] = rows[:, t * 128 : (t + 1) * 128]
        for y in range(4):
            row = wide[y * 128 : y * 128 + 128, :].reshape(8, 16, 128).astype(BF)
            for f in range(8):
                out_ref[f, y] = row

    return call(
        kernel,
        shape((8, 4, 8, 16, 128)),
        [(field, None)],
        [pltpu.VMEM((512, 128), F32)],
        0,
        1_300_000,
    )


def gather_edges(cells, y_before, y_after):
    def kernel(cells_ref, yb, ya, last_ref, first_ref):
        for out_ref, x in ((last_ref, 7), (first_ref, 0)):
            for f in range(8):
                out_ref[f, 0] = yb[f, x]
                out_ref[f, 5] = ya[f, x]
                for y in range(4):
                    out_ref[f, y + 1] = cells_ref[f, y, x]

    out = shape((8, 6, 16, 128))
    ins = [(a, None) for a in (cells, y_before, y_after)]
    return call(kernel, (out, out), ins, (), 0, 400_000)


def grad_edges(pre_grad, y_before, y_after):
    def kernel(pre_ref, yb, ya, last_ref, first_ref):
        for out_ref, x in ((last_ref, 7), (first_ref, 0)):
            out_ref[0] = yb[x]
            out_ref[1:5] = pre_ref[x]
            out_ref[5] = ya[x]

    out = shape((6, 16, 128))
    ins = [(a, None) for a in (pre_grad, y_before, y_after)]
    return call(kernel, (out, out), ins, (), 0, 50_000)


def prepare_weights(weights):
    def kernel(w_ref, fore_ref, back_ref, tall, even, odd):
        def spread(t, carry):
            lanes = pl.ds(pl.multiple_of(t * 128, 128), 128)
            tall[pl.ds(t, 27, stride=256), :] = w_ref[:, lanes].astype(F32)
            return carry

        lax.fori_loop(0, 256, spread, 0, unroll=8)

        def place(ij, carry):
            taps = [tall[pl.ds(pl.multiple_of((ij * 3 + k) * 256, 256), 256), :] for k in range(3)]
            zero = jnp.zeros((256, 64), F32)
            for par in range(2):
                lanes = slice(par * 64, par * 64 + 64)
                even[pl.ds(par, 256, stride=2), :] = jnp.concatenate(
                    [taps[0][:, lanes], taps[1][:, lanes]], axis=1
                )
                odd[pl.ds(par, 256, stride=2), :] = jnp.concatenate([taps[2][:, lanes], zero], axis=1)
            fore_ref[ij, :, 0:128] = even[...].astype(BF)
            fore_ref[ij, :, 128:256] = odd[...].astype(BF)
            for c in range(4):
                rows = slice(c * 128, c * 128 + 128)
                back_ref[ij, 0:128, rows] = even[rows, :].T.astype(BF)
                back_ref[ij, 128:256, rows] = odd[rows, :].T.astype(BF)
            return carry

        lax.fori_loop(0, 9, place, 0)

    return call(
        kernel,
        (shape((9, 512, 256)), shape((9, 256, 512))),
        [(weights, None)],
        [pltpu.VMEM((27 * 256, 128), F32), pltpu.VMEM((512, 128), F32), pltpu.VMEM((512, 128), F32)],
        0,
        8_000_000,
    )


def masked(v, inside):
    return jnp.where(inside, v, jnp.zeros_like(v))


def forward(coords, cells, y_before, y_after, x_before, x_after, fore, grad):
    def kernel(
        co, cells_ref, yb, ya, xb, xa, fore_ref, grad_ref,
        field_ref, out_ref, pre_ref, first_ref, last_ref, total, wide,
    ):
        y_low, y_high, x_low, x_high = co[4] > 0, co[4] < 7, co[5] > 0, co[5] < 3

        def place(x, y, take):
            for q in range(4):
                a, b = take(2 * q), take(2 * q + 1)
                lanes = slice(q * 128, q * 128 + 128)
                field_ref[x, y * 32 : y * 32 + 16, lanes] = jnp.concatenate([a[:, :64], b[:, :64]], axis=1)
                field_ref[x, y * 32 + 16 : y * 32 + 32, lanes] = jnp.concatenate([a[:, 64:], b[:, 64:]], axis=1)

        for y in range(6):
            beside = {0: y_low, 5: y_high}.get(y, True)
            place(0, y, lambda f: masked(xb[f, y], jnp.logical_and(x_low, beside)))
            place(9, y, lambda f: masked(xa[f, y], jnp.logical_and(x_high, beside)))

        def place_x(x, carry):
            place(x + 1, 0, lambda f: masked(yb[f, x], y_low))
            place(x + 1, 5, lambda f: masked(ya[f, x], y_high))
            for y in range(4):
                place(x + 1, y + 1, lambda f: cells_ref[f, y, x])
            return carry

        lax.fori_loop(0, 8, place_x, 0)

        def multiply(h, carry):
            acc = jnp.zeros((256, 256), F32)
            for i in range(3):
                for j in range(3):
                    rows = [field_ref[2 * h + u + i, j * 32 : j * 32 + 128, :] for u in range(2)]
                    acc = acc + jnp.dot(
                        jnp.concatenate(rows, axis=0), fore_ref[i * 3 + j], preferred_element_type=F32
                    )
            total[pl.ds(pl.multiple_of(h * 256, 256), 256), :] = acc
            return carry

        lax.fori_loop(0, 4, multiply, 0)

        def finish(x, carry):
            for y in range(4):
                start = pl.multiple_of(x * 128 + y * 32, 32)
                even, odd = total[pl.ds(start, 16), :], total[pl.ds(start + 16, 16), :]
                pre = (
                    jnp.concatenate([down(odd[:, 0:64]), even[:, 0:64]], axis=1)
                    + jnp.concatenate([even[:, 64:128], odd[:, 64:128]], axis=1)
                    + jnp.concatenate([odd[:, 128:192], up(even[:, 128:192])], axis=1)
                )
                e = jnp.exp(-jnp.abs(pre))
                soft = jnp.maximum(pre, 0.0) + jnp.log1p(e)
                slope = jnp.where(pre >= 0, 1.0, e) / (1.0 + e)
                value = LEAK * pre + (1.0 - LEAK) * (soft - math.log(2.0))
                wide[pl.ds(pl.multiple_of(x * 64 + y * 16, 16), 16), :] = value
                g = grad_ref[x, y].astype(F32)
                turned = (g * (LEAK + (1.0 - LEAK) * slope)).astype(BF)
                pre_ref[x, y] = turned
                if y == 0:
                    first_ref[x] = turned
                if y == 3:
                    last_ref[x] = turned
            return carry

        lax.fori_loop(0, 8, finish, 0)
        from_pairs(wide, out_ref)

    return call(
        kernel,
        (
            shape((10, 192, 512)),
            shape((8, 4, 2048)),
            shape(PIECE),
            shape((8, 16, 128)),
            shape((8, 16, 128)),
        ),
        [(coords, pltpu.SMEM)]
        + [
            (a, None)
            for a in (cells, y_before, y_after, x_before, x_after, fore, grad)
        ],
        [pltpu.VMEM((1024, 256), F32), pltpu.VMEM((512, 128), F32)],
        5_000_000_000,
        6_000_000,
    )


def stacked_depth(v):
    even, odd = v[:, :64], v[:, 64:]
    zero = jnp.zeros((16, 64), F32)
    return (
        (jnp.concatenate([odd, even], axis=1), jnp.concatenate([down(odd), zero], axis=1)),
        (jnp.concatenate([up(even), odd], axis=1), jnp.concatenate([even, zero], axis=1)),
    )


def filter_grad(coords, field, pre_grad):
    def kernel(co, field_ref, pre_ref, keep_ref, send_ref, first, second, turned):
        core = co[2]

        def place(x, carry):
            for y in range(4):
                low, high = stacked_depth(pre_ref[x, y].astype(F32))
                first[y * 32 : y * 32 + 16, :] = low[0]
                second[y * 32 : y * 32 + 16, :] = low[1]
                first[y * 32 + 16 : y * 32 + 32, :] = high[0]
                second[y * 32 + 16 : y * 32 + 32, :] = high[1]
            lanes = pl.ds(pl.multiple_of(x * 128, 128), 128)
            turned[0:128, lanes] = first[...].T.astype(BF)
            turned[128:192, lanes] = second[...].T[0:64].astype(BF)
            return carry

        lax.fori_loop(0, 8, place, 0)

        def multiply(ij, carry):
            i, j = ij // 3, ij % 3
            start = pl.multiple_of(j * 32, 32)
            for half in range(2):
                lanes = slice(half * 256, half * 256 + 256)
                rows = [field_ref[x + i, pl.ds(start, 128), lanes] for x in range(8)]
                got = jnp.dot(
                    turned[...], jnp.concatenate(rows, axis=0), preferred_element_type=F32
                ) * SCALE
                left, right = got[:, :128], got[:, 128:]
                keep_ref[half, ij] = jnp.where(core == 0, left, right)
                send_ref[half, ij] = jnp.where(core == 0, right, left).astype(BF)
            return carry

        lax.fori_loop(0, 9, multiply, 0)

    return call(
        kernel,
        (shape((2, 9, 192, 128), F32), shape((2, 9, 192, 128))),
        [(coords, pltpu.SMEM), (field, None), (pre_grad, None)],
        [pltpu.VMEM((128, 128), F32), pltpu.VMEM((128, 128), F32), pltpu.VMEM((192, 1024), BF)],
        5_000_000_000,
        6_000_000,
    )


def add_cores(coords, keep, got):
    def kernel(co, keep_ref, got_ref, stay_ref, send_ref):
        far = co[3]
        stay_ref[...] = keep_ref[far] + got_ref[far].astype(F32)
        send_ref[...] = (keep_ref[1 - far] + got_ref[1 - far].astype(F32)).astype(BF)

    return call(
        kernel,
        (shape((9, 192, 128), F32), shape((9, 192, 128))),
        [(coords, pltpu.SMEM), (keep, None), (got, None)],
        (),
        0,
        4_000_000,
    )


def add_far(stay, got):
    def kernel(stay_ref, got_ref, out_ref, total, turned):
        total[...] = (stay_ref[...] + got_ref[...].astype(F32)).reshape(1728, 128)
        for t in range(14):
            width = min(128, 1728 - t * 128)
            turned[:, t * 128 : t * 128 + width] = total[t * 128 : t * 128 + width, :].T.astype(BF)
        for s in range(8):
            out_ref[s] = turned[s * 16 : s * 16 + 16, :]

    return call(
        kernel,
        shape((8, 16, 1728)),
        [(stay, None), (got, None)],
        [pltpu.VMEM((1728, 128), F32), pltpu.VMEM((128, 1728), BF)],
        0,
        2_000_000,
    )


def add_regions(parts):
    def kernel(parts_ref, out_ref, total, pairs):
        for t in range(14):
            width = min(128, 1728 - t * 128)
            lanes = slice(t * 128, t * 128 + width)
            s = parts_ref[0, :, lanes].astype(F32)
            for d in range(1, 8):
                s = s + parts_ref[d, :, lanes].astype(F32)
            total[:, 0:width] = s
            even, odd = total[pl.ds(0, 8, stride=2), :], total[pl.ds(1, 8, stride=2), :]
            for u in range(width // 64):
                pick = slice(u * 64, u * 64 + 64)
                at = (2 * t + u) * 8
                pairs[at : at + 8, :] = jnp.concatenate([even[:, pick], odd[:, pick]], axis=1)
        for cp in range(8):
            out_ref[:, cp * 128 : cp * 128 + 128] = pairs[pl.ds(cp, 27, stride=8), :]

    return call(
        kernel,
        shape((27, 1024), F32),
        [(parts, None)],
        [pltpu.VMEM((16, 128), F32), pltpu.VMEM((216, 128), F32)],
        0,
        600_000,
    )


def input_grad_parts(coords, pre_grad, y_before, y_after, x_before, x_after, back):
    def kernel(co, pre_ref, yb, ya, xb, xa, back_ref, out_ref, rim, total):
        y_low, y_high, x_low, x_high = co[4] > 0, co[4] < 7, co[5] > 0, co[5] < 3

        def place(x, y, v):
            low, high = stacked_depth(v.astype(F32))
            for half in range(2):
                lanes = slice(half * 128, half * 128 + 128)
                rim[x, y * 32 : y * 32 + 16, lanes] = low[half].astype(BF)
                rim[x, y * 32 + 16 : y * 32 + 32, lanes] = high[half].astype(BF)

        for y in range(6):
            beside = {0: y_low, 5: y_high}.get(y, True)
            place(0, y, masked(xb[y], jnp.logical_and(x_low, beside)))
            place(9, y, masked(xa[y], jnp.logical_and(x_high, beside)))

        def place_x(x, carry):
            place(x + 1, 0, masked(yb[x], y_low))
            place(x + 1, 5, masked(ya[x], y_high))
            for y in range(4):
                place(x + 1, y + 1, pre_ref[x, y])
            return carry

        lax.fori_loop(0, 8, place_x, 0)

        def multiply(h, carry):
            for n in range(2):
                lanes = slice(n * 256, n * 256 + 256)
                acc = jnp.zeros((256, 256), F32)
                for i in range(3):
                    for j in range(3):
                        at = (2 - j) * 32
                        rows = [rim[2 * h + u + 2 - i, at : at + 128, :] for u in range(2)]
                        acc = acc + jnp.dot(
                            jnp.concatenate(rows, axis=0),
                            back_ref[i * 3 + j, :, lanes],
                            preferred_element_type=F32,
                        )
                total[:, lanes] = acc
            for u in range(2):
                for y in range(4):
                    at = u * 128 + y * 32
                    for f in range(8):
                        lanes = slice(f * 64, f * 64 + 64)
                        pair = jnp.concatenate(
                            [total[at : at + 16, lanes], total[at + 16 : at + 32, lanes]], axis=1
                        )
                        out_ref[f, 2 * h + u, y] = pair.astype(BF)
            return carry

        lax.fori_loop(0, 4, multiply, 0)

    return call(
        kernel,
        shape((8,) + PIECE),
        [(coords, pltpu.SMEM)]
        + [(a, None) for a in (pre_grad, y_before, y_after, x_before, x_after, back)],
        [pltpu.VMEM((10, 192, 256), BF), pltpu.VMEM((256, 512), F32)],
        5_000_000_000,
        5_000_000,
    )


def add_blocks(parts):
    def kernel(parts_ref, out_ref, wide):
        s = parts_ref[0].astype(F32)
        for f in range(1, 8):
            s = s + parts_ref[f].astype(F32)
        wide[...] = s.reshape(512, 128)
        from_pairs(wide, out_ref)

    return call(
        kernel,
        shape((8, 4, 2048)),
        [(parts, None)],
        [pltpu.VMEM((512, 128), F32)],
        0,
        1_200_000,
    )


def both_ways(last, first, axis, size):
    return (
        lax.ppermute(last, axis, [(i, (i + 1) % size) for i in range(size)]),
        lax.ppermute(first, axis, [((i + 1) % size, i) for i in range(size)]),
    )


def exchange(parts, axis):
    return lax.all_to_all(parts, axis, 0, 0)


def per_device(activations, weights, out_grad):
    filt, sx, sy = (lax.axis_index(a) for a in ("filt", "sx", "sy"))
    coords = jnp.stack([filt // 4, filt % 4, sx % 2, sx // 2, sy, sx, 0, 0]).astype(jnp.int32)
    cells = prepare_gather(activations[0, 0])
    cells, weights, out_grad = lax.optimization_barrier((cells, weights, out_grad))
    cells = exchange(cells, "filt")
    fore, back = prepare_weights(weights[0])
    grad = prepare_field(out_grad[0, 0])
    cells, fore, back, grad = lax.optimization_barrier((cells, fore, back, grad))
    y_before, y_after = both_ways(cells[:, 3], cells[:, 0], "sy", 8)
    x_last, x_first = gather_edges(cells, y_before, y_after)
    x_before, x_after = both_ways(x_last, x_first, "sx", 4)
    field, outputs, pre_grad, g_first, g_last = forward(
        coords, cells, y_before, y_after, x_before, x_after, fore, grad
    )

    gy_before, gy_after = both_ways(g_last, g_first, "sy", 8)
    keep, send = filter_grad(coords, field, pre_grad)
    got = lax.ppermute(send, "sx", [(i, i ^ 1) for i in range(4)])
    got, gy_before, gy_after = lax.optimization_barrier((got, gy_before, gy_after))
    stay, send = add_cores(coords, keep, got)
    gx_before, gx_after = both_ways(*grad_edges(pre_grad, gy_before, gy_after), "sx", 4)
    got = lax.ppermute(send, "sx", [(i, i ^ 2) for i in range(4)])

    parts = input_grad_parts(coords, pre_grad, gy_before, gy_after, gx_before, gx_after, back)
    parts, got = lax.optimization_barrier((parts, got))
    parts = exchange(parts, "filt")
    regions = exchange(add_far(stay, got), "sy")
    input_grad = add_blocks(parts)
    weight_grad = add_regions(regions)
    return outputs[None, None], input_grad[None, None], weight_grad[None]


def solution(mesh):
    in_specs = (
        P("filt", None, "sx", "sy", None),
        P("filt", None, None),
        P("filt", None, "sx", "sy", None),
    )
    out_specs = (
        P("filt", None, "sx", "sy", None),
        P("filt", None, "sx", "sy", None),
        P("filt", None, ("sx", "sy")),
    )
    return jax.shard_map(
        per_device, mesh=mesh, in_specs=in_specs, out_specs=out_specs, check_vma=False
    )
```

```python
import math

import jax
import jax.numpy as jnp
from jax import lax
from jax.experimental import pallas as pl
from jax.experimental.pallas import tpu as pltpu
from jax.sharding import PartitionSpec as P

BF = jnp.bfloat16
F32 = jnp.float32
LEAK = 0.2
SCALE = 1.0 / math.sqrt(32768.0)
PIECE = (8, 4, 16, 128)


def call(kernel, outs, ins, scratch=(), flops=0, nbytes=0):
    return pl.pallas_call(
        kernel,
        out_shape=outs,
        in_specs=[
            pl.BlockSpec(memory_space=pltpu.VMEM if space is None else space)
            for _, space in ins
        ],
        out_specs=jax.tree.map(lambda _: pl.BlockSpec(memory_space=pltpu.VMEM), outs),
        scratch_shapes=list(scratch),
        compiler_params=pltpu.CompilerParams(vmem_limit_bytes=48 << 20),
        cost_estimate=pl.CostEstimate(flops=flops, bytes_accessed=nbytes, transcendentals=0),
    )(*[array for array, _ in ins])


def shape(dims, dtype=BF):
    return jax.ShapeDtypeStruct(dims, dtype)


def down(v):
    rows = lax.broadcasted_iota(jnp.int32, v.shape, 0)
    return jnp.where(rows == 0, 0.0, pltpu.roll(v, 1, 0))


def up(v):
    rows = lax.broadcasted_iota(jnp.int32, v.shape, 0)
    return jnp.where(rows == v.shape[0] - 1, 0.0, pltpu.roll(v, v.shape[0] - 1, 0))


def to_pairs(field_ref, pair_ref, wide):
    for x in range(8):
        rows = field_ref[x].astype(F32)
        for t in range(16):
            wide[pl.ds(x * 64 + t, 4, stride=16), :] = rows[:, t * 128 : (t + 1) * 128]
    pair_ref[...] = wide[...].reshape(PIECE).astype(BF)


def from_pairs(wide, field_ref, layers):
    for n, x in enumerate(layers):
        parts = [wide[pl.ds(n * 64 + t, 4, stride=16), :] for t in range(16)]
        field_ref[x] = jnp.concatenate(parts, axis=1).astype(BF)


def prepare_field(field):
    def kernel(field_ref, pair_ref, wide):
        to_pairs(field_ref, pair_ref, wide)

    return call(
        kernel, shape(PIECE), [(field, None)], [pltpu.VMEM((512, 128), F32)], 0, 400_000
    )


def prepare_gather(field):
    def kernel(field_ref, out_ref, wide):
        for x in range(8):
            rows = field_ref[x].astype(F32)
            for t in range(16):
                wide[pl.ds(x * 16 + t, 4, stride=128), :] = rows[:, t * 128 : (t + 1) * 128]
        for y in range(4):
            row = wide[y * 128 : y * 128 + 128, :].reshape(8, 16, 128).astype(BF)
            for f in range(8):
                out_ref[f, y] = row

    return call(
        kernel,
        shape((8, 4, 8, 16, 128)),
        [(field, None)],
        [pltpu.VMEM((512, 128), F32)],
        0,
        1_300_000,
    )


def gather_edges(cells, y_before, y_after):
    def kernel(cells_ref, yb, ya, last_ref, first_ref):
        for out_ref, x in ((last_ref, 7), (first_ref, 0)):
            for f in range(8):
                out_ref[f, 0] = yb[f, x]
                out_ref[f, 5] = ya[f, x]
                for y in range(4):
                    out_ref[f, y + 1] = cells_ref[f, y, x]

    out = shape((8, 6, 16, 128))
    ins = [(a, None) for a in (cells, y_before, y_after)]
    return call(kernel, (out, out), ins, (), 0, 400_000)


def grad_edges(pre_grad, y_before, y_after):
    def kernel(pre_ref, yb, ya, last_ref, first_ref):
        for out_ref, x in ((last_ref, 7), (first_ref, 0)):
            out_ref[0] = yb[x]
            out_ref[1:5] = pre_ref[x]
            out_ref[5] = ya[x]

    out = shape((6, 16, 128))
    ins = [(a, None) for a in (pre_grad, y_before, y_after)]
    return call(kernel, (out, out), ins, (), 0, 50_000)


def prepare_weights(weights):
    def kernel(w_ref, fore_ref, back_ref, tall, even, odd):
        def spread(t, carry):
            lanes = pl.ds(pl.multiple_of(t * 128, 128), 128)
            tall[pl.ds(t, 27, stride=256), :] = w_ref[:, lanes].astype(F32)
            return carry

        lax.fori_loop(0, 256, spread, 0, unroll=8)

        def place(ij, carry):
            taps = [tall[pl.ds(pl.multiple_of((ij * 3 + k) * 256, 256), 256), :] for k in range(3)]
            zero = jnp.zeros((256, 64), F32)
            for par in range(2):
                lanes = slice(par * 64, par * 64 + 64)
                even[pl.ds(par, 256, stride=2), :] = jnp.concatenate(
                    [taps[0][:, lanes], taps[1][:, lanes]], axis=1
                )
                odd[pl.ds(par, 256, stride=2), :] = jnp.concatenate([taps[2][:, lanes], zero], axis=1)
            fore_ref[ij, :, 0:128] = even[...].astype(BF)
            fore_ref[ij, :, 128:256] = odd[...].astype(BF)
            for c in range(4):
                rows = slice(c * 128, c * 128 + 128)
                back_ref[ij, 0:128, rows] = even[rows, :].T.astype(BF)
                back_ref[ij, 128:256, rows] = odd[rows, :].T.astype(BF)
            return carry

        lax.fori_loop(0, 9, place, 0)

    return call(
        kernel,
        (shape((9, 512, 256)), shape((9, 256, 512))),
        [(weights, None)],
        [pltpu.VMEM((27 * 256, 128), F32), pltpu.VMEM((512, 128), F32), pltpu.VMEM((512, 128), F32)],
        0,
        8_000_000,
    )


def masked(v, inside):
    return jnp.where(inside, v, jnp.zeros_like(v))


def place_cell(field_ref, x, y, take):
    for q in range(4):
        a, b = take(2 * q), take(2 * q + 1)
        lanes = slice(q * 128, q * 128 + 128)
        field_ref[x, y * 32 : y * 32 + 16, lanes] = jnp.concatenate([a[:, :64], b[:, :64]], axis=1)
        field_ref[x, y * 32 + 16 : y * 32 + 32, lanes] = jnp.concatenate([a[:, 64:], b[:, 64:]], axis=1)


def convolved(rows, fore_ref):
    acc = jnp.zeros((256, 256), F32)
    for i in range(3):
        for j in range(3):
            acc = acc + jnp.dot(
                jnp.concatenate([rows(u, i, j * 32) for u in range(2)], axis=0),
                fore_ref[i * 3 + j],
                preferred_element_type=F32,
            )
    return acc


def finish_cell(total, start, grad):
    even, odd = total[pl.ds(start, 16), :], total[pl.ds(start + 16, 16), :]
    pre = (
        jnp.concatenate([down(odd[:, 0:64]), even[:, 0:64]], axis=1)
        + jnp.concatenate([even[:, 64:128], odd[:, 64:128]], axis=1)
        + jnp.concatenate([odd[:, 128:192], up(even[:, 128:192])], axis=1)
    )
    e = jnp.exp(-jnp.abs(pre))
    soft = jnp.maximum(pre, 0.0) + jnp.log1p(e)
    slope = jnp.where(pre >= 0, 1.0, e) / (1.0 + e)
    value = LEAK * pre + (1.0 - LEAK) * (soft - math.log(2.0))
    return value, (grad.astype(F32) * (LEAK + (1.0 - LEAK) * slope)).astype(BF)


def forward_inner(coords, cells, y_before, y_after, fore, grad):
    def kernel(co, cells_ref, yb, ya, fore_ref, grad_ref, field_ref, out_ref, pre_ref, total, wide):
        y_low, y_high = co[4] > 0, co[4] < 7

        def place(x, carry):
            place_cell(field_ref, x, 0, lambda f: masked(yb[f, x], y_low))
            place_cell(field_ref, x, 5, lambda f: masked(ya[f, x], y_high))
            for y in range(4):
                place_cell(field_ref, x, y + 1, lambda f: cells_ref[f, y, x])
            return carry

        lax.fori_loop(0, 8, place, 0)

        def multiply(h, carry):
            start = pl.multiple_of(h * 256, 256)
            total[pl.ds(start, 256), :] = convolved(
                lambda u, i, at: field_ref[2 * h + u + i, at : at + 128, :], fore_ref
            )
            return carry

        lax.fori_loop(0, 3, multiply, 0)

        def finish(x, carry):
            for y in range(4):
                start = pl.multiple_of(x * 128 + y * 32, 32)
                value, turned = finish_cell(total, start, grad_ref[x + 1, y])
                wide[pl.ds(pl.multiple_of(x * 64 + y * 16, 16), 16), :] = value
                pre_ref[x, y] = turned
            return carry

        lax.fori_loop(0, 6, finish, 0)
        from_pairs(wide, out_ref, range(6))

    return call(
        kernel,
        (shape((8, 192, 512)), shape((6, 4, 2048)), shape((6, 4, 16, 128))),
        [(coords, pltpu.SMEM)] + [(a, None) for a in (cells, y_before, y_after, fore, grad)],
        [pltpu.VMEM((768, 256), F32), pltpu.VMEM((384, 128), F32)],
        4_000_000_000,
        6_000_000,
    )


def forward_outer(coords, field, x_before, x_after, fore, grad, out_inner, pre_inner):
    def kernel(
        co, field_ref, xb, xa, fore_ref, grad_ref, out_in, pre_in,
        rim_ref, out_ref, pre_ref, first_ref, last_ref, total, wide,
    ):
        y_low, y_high, x_low, x_high = co[4] > 0, co[4] < 7, co[5] > 0, co[5] < 3
        for y in range(6):
            beside = {0: y_low, 5: y_high}.get(y, True)
            place_cell(rim_ref, 0, y, lambda f: masked(xb[f, y], jnp.logical_and(x_low, beside)))
            place_cell(rim_ref, 1, y, lambda f: masked(xa[f, y], jnp.logical_and(x_high, beside)))

        def rows(u, i, at):
            if u == 0:
                return (field_ref[i - 1] if i else rim_ref[0])[at : at + 128, :]
            return (field_ref[6 + i] if i < 2 else rim_ref[1])[at : at + 128, :]

        total[...] = convolved(rows, fore_ref)
        for n, x in enumerate((0, 7)):
            for y in range(4):
                value, turned = finish_cell(total, n * 128 + y * 32, grad_ref[x, y])
                wide[n * 64 + y * 16 : n * 64 + y * 16 + 16, :] = value
                pre_ref[x, y] = turned
        from_pairs(wide, out_ref, (0, 7))
        out_ref[1:7] = out_in[...]
        pre_ref[1:7] = pre_in[...]
        for x in range(8):
            first_ref[x] = pre_ref[x, 0]
            last_ref[x] = pre_ref[x, 3]

    return call(
        kernel,
        (
            shape((2, 192, 512)),
            shape((8, 4, 2048)),
            shape(PIECE),
            shape((8, 16, 128)),
            shape((8, 16, 128)),
        ),
        [(coords, pltpu.SMEM)]
        + [(a, None) for a in (field, x_before, x_after, fore, grad, out_inner, pre_inner)],
        [pltpu.VMEM((256, 256), F32), pltpu.VMEM((128, 128), F32)],
        2_000_000_000,
        6_000_000,
    )


def stacked_depth(v):
    even, odd = v[:, :64], v[:, 64:]
    zero = jnp.zeros((16, 64), F32)
    return (
        (jnp.concatenate([odd, even], axis=1), jnp.concatenate([down(odd), zero], axis=1)),
        (jnp.concatenate([up(even), odd], axis=1), jnp.concatenate([even, zero], axis=1)),
    )


def filter_grad(coords, field, rim, pre_grad):
    def kernel(co, field_ref, rim_ref, pre_ref, keep_ref, send_ref, first, second, turned):
        core = co[2]

        def place(x, carry):
            for y in range(4):
                low, high = stacked_depth(pre_ref[x, y].astype(F32))
                first[y * 32 : y * 32 + 16, :] = low[0]
                second[y * 32 : y * 32 + 16, :] = low[1]
                first[y * 32 + 16 : y * 32 + 32, :] = high[0]
                second[y * 32 + 16 : y * 32 + 32, :] = high[1]
            lanes = pl.ds(pl.multiple_of(x * 128, 128), 128)
            turned[0:128, lanes] = first[...].T.astype(BF)
            turned[128:192, lanes] = second[...].T[0:64].astype(BF)
            return carry

        lax.fori_loop(0, 8, place, 0)

        def layer(x, rows, lanes):
            if x in (0, 9):
                return rim_ref[x // 9, rows, lanes]
            return field_ref[x - 1, rows, lanes]

        def multiply(j, carry):
            rows = pl.ds(pl.multiple_of(j * 32, 32), 128)
            for i in range(3):
                for half in range(2):
                    lanes = slice(half * 256, half * 256 + 256)
                    cells = [layer(x + i, rows, lanes) for x in range(8)]
                    got = jnp.dot(
                        turned[...], jnp.concatenate(cells, axis=0), preferred_element_type=F32
                    ) * SCALE
                    left, right = got[:, :128], got[:, 128:]
                    keep_ref[half, i * 3 + j] = jnp.where(core == 0, left, right)
                    send_ref[half, i * 3 + j] = jnp.where(core == 0, right, left).astype(BF)
            return carry

        lax.fori_loop(0, 3, multiply, 0)

    return call(
        kernel,
        (shape((2, 9, 192, 128), F32), shape((2, 9, 192, 128))),
        [(coords, pltpu.SMEM), (field, None), (rim, None), (pre_grad, None)],
        [pltpu.VMEM((128, 128), F32), pltpu.VMEM((128, 128), F32), pltpu.VMEM((192, 1024), BF)],
        5_000_000_000,
        6_000_000,
    )


def add_cores(coords, keep, got):
    def kernel(co, keep_ref, got_ref, stay_ref, send_ref):
        far = co[3]
        stay_ref[...] = keep_ref[far] + got_ref[far].astype(F32)
        send_ref[...] = (keep_ref[1 - far] + got_ref[1 - far].astype(F32)).astype(BF)

    return call(
        kernel,
        (shape((9, 192, 128), F32), shape((9, 192, 128))),
        [(coords, pltpu.SMEM), (keep, None), (got, None)],
        (),
        0,
        4_000_000,
    )


def add_far(coords, stay, got):
    def kernel(co, stay_ref, got_ref, *refs):
        outs, (total, turned) = refs[:8], refs[8:]
        sy = co[4]
        total[...] = (stay_ref[...] + got_ref[...].astype(F32)).reshape(1728, 128)
        for t in range(14):
            width = min(128, 1728 - t * 128)
            block = total[t * 128 : t * 128 + width, :].T.astype(BF).reshape(8, 16, width)
            turned[:, :, t * 128 : t * 128 + width] = block
        for d in range(8):
            outs[d][...] = turned[(sy + d) & 7]

    return call(
        kernel,
        (shape((16, 1728)),) * 8,
        [(coords, pltpu.SMEM), (stay, None), (got, None)],
        [pltpu.VMEM((1728, 128), F32), pltpu.VMEM((8, 16, 1728), BF)],
        0,
        2_000_000,
    )


def add_regions(parts):
    def kernel(*refs):
        ins, (out_ref, total, pairs) = refs[:8], refs[8:]
        for t in range(14):
            width = min(128, 1728 - t * 128)
            lanes = slice(t * 128, t * 128 + width)
            s = ins[0][:, lanes].astype(F32)
            for ref in ins[1:]:
                s = s + ref[:, lanes].astype(F32)
            total[:, 0:width] = s
            even, odd = total[pl.ds(0, 8, stride=2), :], total[pl.ds(1, 8, stride=2), :]
            for u in range(width // 64):
                pick = slice(u * 64, u * 64 + 64)
                at = (2 * t + u) * 8
                pairs[at : at + 8, :] = jnp.concatenate([even[:, pick], odd[:, pick]], axis=1)
        for cp in range(8):
            out_ref[:, cp * 128 : cp * 128 + 128] = pairs[pl.ds(cp, 27, stride=8), :]

    return call(
        kernel,
        shape((27, 1024), F32),
        [(part, None) for part in parts],
        [pltpu.VMEM((16, 128), F32), pltpu.VMEM((216, 128), F32)],
        0,
        600_000,
    )


def place_grad(rim, x, y, v):
    low, high = stacked_depth(v.astype(F32))
    for half in range(2):
        lanes = slice(half * 128, half * 128 + 128)
        rim[x, y * 32 : y * 32 + 16, lanes] = low[half].astype(BF)
        rim[x, y * 32 + 16 : y * 32 + 32, lanes] = high[half].astype(BF)


def input_layers(rows, back_ref, total, store):
    for n in range(2):
        lanes = slice(n * 256, n * 256 + 256)
        acc = jnp.zeros((256, 256), F32)
        for i in range(3):
            for j in range(3):
                acc = acc + jnp.dot(
                    jnp.concatenate([rows(u, 2 - i, (2 - j) * 32) for u in range(2)], axis=0),
                    back_ref[i * 3 + j, :, lanes],
                    preferred_element_type=F32,
                )
        total[:, lanes] = acc
    for u in range(2):
        for y in range(4):
            at = u * 128 + y * 32
            for f in range(8):
                lanes = slice(f * 64, f * 64 + 64)
                pair = jnp.concatenate([total[at : at + 16, lanes], total[at + 16 : at + 32, lanes]], axis=1)
                store(f, u, y, pair.astype(BF))


def input_grad_inner(coords, pre_grad, y_before, y_after, back):
    def kernel(co, pre_ref, yb, ya, back_ref, out_ref, rim, total):
        y_low, y_high = co[4] > 0, co[4] < 7

        def place(x, carry):
            place_grad(rim, x, 0, masked(yb[x], y_low))
            place_grad(rim, x, 5, masked(ya[x], y_high))
            for y in range(4):
                place_grad(rim, x, y + 1, pre_ref[x, y])
            return carry

        lax.fori_loop(0, 8, place, 0)

        def multiply(h, carry):
            def store(f, u, y, block):
                out_ref[f, 2 * h + u, y] = block

            input_layers(lambda u, d, at: rim[2 * h + u + d, at : at + 128, :], back_ref, total, store)
            return carry

        lax.fori_loop(0, 3, multiply, 0)

    return call(
        kernel,
        shape((8, 6, 4, 16, 128)),
        [(coords, pltpu.SMEM)] + [(a, None) for a in (pre_grad, y_before, y_after, back)],
        [pltpu.VMEM((8, 192, 256), BF), pltpu.VMEM((256, 512), F32)],
        4_000_000_000,
        5_000_000,
    )


def input_grad_outer(coords, pre_grad, y_before, y_after, x_before, x_after, back, inner):
    def kernel(co, pre_ref, yb, ya, xb, xa, back_ref, inner_ref, out_ref, rim, total):
        y_low, y_high, x_low, x_high = co[4] > 0, co[4] < 7, co[5] > 0, co[5] < 3
        for y in range(6):
            beside = {0: y_low, 5: y_high}.get(y, True)
            place_grad(rim, 0, y, masked(xb[y], jnp.logical_and(x_low, beside)))
            place_grad(rim, 5, y, masked(xa[y], jnp.logical_and(x_high, beside)))
        for at, x in ((1, 0), (2, 1), (3, 6), (4, 7)):
            place_grad(rim, at, 0, masked(yb[x], y_low))
            place_grad(rim, at, 5, masked(ya[x], y_high))
            for y in range(4):
                place_grad(rim, at, y + 1, pre_ref[x, y])

        def store(f, u, y, block):
            out_ref[f, 7 * u, y] = block

        input_layers(lambda u, d, at: rim[3 * u + d, at : at + 128, :], back_ref, total, store)
        for f in range(8):
            out_ref[f, 1:7] = inner_ref[f]

    return call(
        kernel,
        shape((8,) + PIECE),
        [(coords, pltpu.SMEM)]
        + [(a, None) for a in (pre_grad, y_before, y_after, x_before, x_after, back, inner)],
        [pltpu.VMEM((6, 192, 256), BF), pltpu.VMEM((256, 512), F32)],
        2_000_000_000,
        5_000_000,
    )


def add_blocks(parts):
    def kernel(parts_ref, out_ref, wide):
        s = parts_ref[0].astype(F32)
        for f in range(1, 8):
            s = s + parts_ref[f].astype(F32)
        wide[...] = s.reshape(512, 128)
        from_pairs(wide, out_ref, range(8))

    return call(
        kernel,
        shape((8, 4, 2048)),
        [(parts, None)],
        [pltpu.VMEM((512, 128), F32)],
        0,
        1_200_000,
    )


def both_ways(last, first, axis, size):
    return (
        lax.ppermute(last, axis, [(i, (i + 1) % size) for i in range(size)]),
        lax.ppermute(first, axis, [((i + 1) % size, i) for i in range(size)]),
    )


def exchange(parts, axis):
    return lax.all_to_all(parts, axis, 0, 0)


def per_device(activations, weights, out_grad):
    filt, sx, sy = (lax.axis_index(a) for a in ("filt", "sx", "sy"))
    coords = jnp.stack([filt // 4, filt % 4, sx % 2, sx // 2, sy, sx, 0, 0]).astype(jnp.int32)
    cells = prepare_gather(activations[0, 0])
    cells, weights, out_grad = lax.optimization_barrier((cells, weights, out_grad))
    cells = exchange(cells, "filt")
    fore, back = prepare_weights(weights[0])
    grad = prepare_field(out_grad[0, 0])
    cells, fore, back, grad = lax.optimization_barrier((cells, fore, back, grad))
    y_before, y_after = both_ways(cells[:, 3], cells[:, 0], "sy", 8)
    x_last, x_first = gather_edges(cells, y_before, y_after)
    x_last, x_first, cells = lax.optimization_barrier((x_last, x_first, cells))
    x_before, x_after = both_ways(x_last, x_first, "sx", 4)
    field, out_inner, pre_inner = forward_inner(coords, cells, y_before, y_after, fore, grad)
    rim, outputs, pre_grad, g_first, g_last = forward_outer(
        coords, field, x_before, x_after, fore, grad, out_inner, pre_inner
    )

    gy_before, gy_after = both_ways(g_last, g_first, "sy", 8)
    keep, send = filter_grad(coords, field, rim, pre_grad)
    got = lax.ppermute(send, "sx", [(i, i ^ 1) for i in range(4)])
    stay, send = add_cores(coords, keep, got)
    send, pre_grad, gy_before, gy_after = lax.optimization_barrier((send, pre_grad, gy_before, gy_after))
    got = lax.ppermute(send, "sx", [(i, i ^ 2) for i in range(4)])
    gx_before, gx_after = both_ways(*grad_edges(pre_grad, gy_before, gy_after), "sx", 4)

    inner = input_grad_inner(coords, pre_grad, gy_before, gy_after, back)
    parts = input_grad_outer(coords, pre_grad, gy_before, gy_after, gx_before, gx_after, back, inner)
    parts, got = lax.optimization_barrier((parts, got))
    parts = exchange(parts, "filt")
    turned = add_far(coords, stay, got)
    regions = {0: turned[0]}
    for d in (4, 3, 5, 2, 6, 1, 7):
        regions[d] = lax.ppermute(turned[d], "sy", [(i, (i + d) % 8) for i in range(8)])
    weight_grad = add_regions([regions[d] for d in range(8)])
    input_grad = add_blocks(parts)
    return outputs[None, None], input_grad[None, None], weight_grad[None]


def solution(mesh):
    in_specs = (
        P("filt", None, "sx", "sy", None),
        P("filt", None, None),
        P("filt", None, "sx", "sy", None),
    )
    out_specs = (
        P("filt", None, "sx", "sy", None),
        P("filt", None, "sx", "sy", None),
        P("filt", None, ("sx", "sy")),
    )
    return jax.shard_map(
        per_device, mesh=mesh, in_specs=in_specs, out_specs=out_specs, check_vma=False
    )
```

```python
import math

import jax
import jax.numpy as jnp
from jax import lax
from jax.experimental import pallas as pl
from jax.experimental.pallas import tpu as pltpu
from jax.sharding import PartitionSpec as P

BF = jnp.bfloat16
F32 = jnp.float32
LEAK = 0.2
SCALE = 1.0 / math.sqrt(32768.0)
URGENT = 20_000_000_000
COST = [20_000_000_000, 4_000_000_000, 500_000_000, 5_000_000_000]
PIECE = (8, 4, 16, 128)


def call(kernel, outs, ins, scratch=(), flops=0, nbytes=0):
    return pl.pallas_call(
        kernel,
        out_shape=outs,
        in_specs=[
            pl.BlockSpec(memory_space=pltpu.VMEM if space is None else space)
            for _, space in ins
        ],
        out_specs=jax.tree.map(
            lambda out: pl.BlockSpec(
                memory_space=pltpu.VMEM if isinstance(out, jax.ShapeDtypeStruct) else pl.ANY
            ),
            outs,
        ),
        scratch_shapes=list(scratch),
        compiler_params=pltpu.CompilerParams(vmem_limit_bytes=14 << 20),
        cost_estimate=pl.CostEstimate(flops=flops, bytes_accessed=nbytes, transcendentals=0),
    )(*[array for array, _ in ins])


def shape(dims, dtype=BF):
    return jax.ShapeDtypeStruct(dims, dtype)


def down(v):
    rows = lax.broadcasted_iota(jnp.int32, v.shape, 0)
    return jnp.where(rows == 0, 0.0, pltpu.roll(v, 1, 0))


def up(v):
    rows = lax.broadcasted_iota(jnp.int32, v.shape, 0)
    return jnp.where(rows == v.shape[0] - 1, 0.0, pltpu.roll(v, v.shape[0] - 1, 0))


def to_pairs(field_ref, pair_ref, wide):
    for x in range(8):
        rows = field_ref[x].astype(F32)
        for t in range(16):
            wide[pl.ds(x * 64 + t, 4, stride=16), :] = rows[:, t * 128 : (t + 1) * 128]
    pair_ref[...] = wide[...].reshape(PIECE).astype(BF)


def from_pairs(wide, field_ref, layers):
    for n, x in enumerate(layers):
        parts = [wide[pl.ds(n * 64 + t, 4, stride=16), :] for t in range(16)]
        field_ref[x] = jnp.concatenate(parts, axis=1).astype(BF)


def prepare_field(field):
    def kernel(field_ref, pair_ref, wide):
        to_pairs(field_ref, pair_ref, wide)

    return call(
        kernel, shape(PIECE), [(field, None)], [pltpu.VMEM((512, 128), F32)], 0, 400_000
    )


def prepare_gather(field):
    def kernel(field_ref, out_ref, wide):
        for x in range(8):
            rows = field_ref[x].astype(F32)
            for t in range(16):
                wide[pl.ds(x * 16 + t, 4, stride=128), :] = rows[:, t * 128 : (t + 1) * 128]
        for y in range(4):
            row = wide[y * 128 : y * 128 + 128, :].reshape(8, 16, 128).astype(BF)
            for f in range(8):
                out_ref[f, y] = row

    return call(
        kernel,
        shape((8, 4, 8, 16, 128)),
        [(field, None)],
        [pltpu.VMEM((512, 128), F32)],
        0,
        1_300_000,
    )


def gather_sides(cells, prepared):
    def kernel(cells_ref, prepared_ref, last_ref, first_ref, sems):
        copies = [
            pltpu.make_async_copy(cells_ref.at[:, 3], last_ref, sems.at[0]),
            pltpu.make_async_copy(cells_ref.at[:, 0], first_ref, sems.at[1]),
        ]
        for copy in copies:
            copy.start()
        for copy in copies:
            copy.wait()

    out = shape((8, 8, 16, 128))
    ins = [(cells, pl.ANY), (prepared, None)]
    return call(kernel, (out, out), ins, [pltpu.SemaphoreType.DMA((2,))], 0, 1_000_000)


def gather_edges(coords, cells, y_before, y_after):
    def kernel(co, cells_ref, yb, ya, near_ref, far_ref):
        def give(last_ref, first_ref):
            for out_ref, x in ((last_ref, 7), (first_ref, 0)):
                for f in range(8):
                    out_ref[f, 0] = yb[f, x]
                    out_ref[f, 5] = ya[f, x]
                    for y in range(4):
                        out_ref[f, y + 1] = cells_ref[f, y, x]

        pl.when(co[2] == 0)(lambda: give(near_ref, far_ref))
        pl.when(co[2] == 1)(lambda: give(far_ref, near_ref))

    out = shape((8, 6, 16, 128))
    ins = [(coords, pltpu.SMEM)] + [(a, None) for a in (cells, y_before, y_after)]
    return call(kernel, (out, out), ins, (), 0, 400_000)


def grad_edges(coords, pre_grad, y_before, y_after):
    def kernel(co, pre_ref, yb, ya, near_ref, far_ref):
        for out_ref, x in ((near_ref, 7 - 7 * co[2]), (far_ref, 7 * co[2])):
            out_ref[0] = yb[x]
            out_ref[1:5] = pre_ref[x]
            out_ref[5] = ya[x]

    out = shape((6, 16, 128))
    ins = [(coords, pltpu.SMEM)] + [(a, None) for a in (pre_grad, y_before, y_after)]
    return call(kernel, (out, out), ins, (), 0, 0)


def prepare_weights(weights):
    def kernel(w_ref, fore_ref, back_out, done_ref, tall, even, odd, back_ref, sems):
        def spread(t, carry):
            lanes = pl.ds(pl.multiple_of(t * 128, 128), 128)
            tall[pl.ds(t, 27, stride=256), :] = w_ref[:, lanes].astype(F32)
            return carry

        lax.fori_loop(0, 256, spread, 0, unroll=8)

        def place(ij, carry):
            taps = [tall[pl.ds(pl.multiple_of((ij * 3 + k) * 256, 256), 256), :] for k in range(3)]
            zero = jnp.zeros((256, 64), F32)
            for par in range(2):
                lanes = slice(par * 64, par * 64 + 64)
                even[pl.ds(par, 256, stride=2), :] = jnp.concatenate(
                    [taps[0][:, lanes], taps[1][:, lanes]], axis=1
                )
                odd[pl.ds(par, 256, stride=2), :] = jnp.concatenate([taps[2][:, lanes], zero], axis=1)
            fore_ref[ij, :, 0:128] = even[...].astype(BF)
            fore_ref[ij, :, 128:256] = odd[...].astype(BF)
            for c in range(4):
                rows = slice(c * 128, c * 128 + 128)
                back_ref[ij, 0:128, rows] = even[rows, :].T.astype(BF)
                back_ref[ij, 128:256, rows] = odd[rows, :].T.astype(BF)
            copy_out(ij).start()
            return carry

        def copy_out(ij):
            return pltpu.make_async_copy(back_ref.at[ij], back_out.at[ij], sems.at[ij])

        def finish(ij, carry):
            copy_out(ij).wait()
            return carry

        lax.fori_loop(0, 9, place, 0)
        lax.fori_loop(0, 9, finish, 0)
        done_ref[...] = even[0:8, :]

    return call(
        kernel,
        (shape((9, 512, 256)), pltpu.HBM((9, 256, 512), BF), shape((8, 128), F32)),
        [(weights, None)],
        [
            pltpu.VMEM((27 * 256, 128), F32),
            pltpu.VMEM((512, 128), F32),
            pltpu.VMEM((512, 128), F32),
            pltpu.VMEM((9, 256, 512), BF),
            pltpu.SemaphoreType.DMA((9,)),
        ],
        0,
        8_000_000,
    )


def masked(v, inside):
    return jnp.where(inside, v, jnp.zeros_like(v))


def place_cell(field_ref, x, y, take):
    for q in range(4):
        a, b = take(2 * q), take(2 * q + 1)
        lanes = slice(q * 128, q * 128 + 128)
        field_ref[x, y * 32 : y * 32 + 16, lanes] = jnp.concatenate([a[:, :64], b[:, :64]], axis=1)
        field_ref[x, y * 32 + 16 : y * 32 + 32, lanes] = jnp.concatenate([a[:, 64:], b[:, 64:]], axis=1)


def convolved(rows, fore_ref):
    acc = jnp.zeros((256, 256), F32)
    for i in range(3):
        for j in range(3):
            acc = acc + jnp.dot(
                jnp.concatenate([rows(u, i, j * 32) for u in range(2)], axis=0),
                fore_ref[i * 3 + j],
                preferred_element_type=F32,
            )
    return acc


def finish_cell(total, start, grad):
    even, odd = total[pl.ds(start, 16), :], total[pl.ds(start + 16, 16), :]
    pre = (
        jnp.concatenate([down(odd[:, 0:64]), even[:, 0:64]], axis=1)
        + jnp.concatenate([even[:, 64:128], odd[:, 64:128]], axis=1)
        + jnp.concatenate([odd[:, 128:192], up(even[:, 128:192])], axis=1)
    )
    e = jnp.exp(-jnp.abs(pre))
    soft = jnp.maximum(pre, 0.0) + jnp.log1p(e)
    slope = jnp.where(pre >= 0, 1.0, e) / (1.0 + e)
    value = LEAK * pre + (1.0 - LEAK) * (soft - math.log(2.0))
    return value, (grad.astype(F32) * (LEAK + (1.0 - LEAK) * slope)).astype(BF)


def forward_inner(coords, cells, y_before, y_after, fore, grad):
    def kernel(co, cells_ref, yb, ya, fore_ref, grad_ref, field_ref, out_ref, pre_ref, total, wide):
        y_low, y_high = co[4] > 0, co[4] < 7

        def place(x, carry):
            place_cell(field_ref, x, 0, lambda f: masked(yb[f, x], y_low))
            place_cell(field_ref, x, 5, lambda f: masked(ya[f, x], y_high))
            for y in range(4):
                place_cell(field_ref, x, y + 1, lambda f: cells_ref[f, y, x])
            return carry

        lax.fori_loop(0, 8, place, 0)

        def multiply(h, carry):
            start = pl.multiple_of(h * 256, 256)
            total[pl.ds(start, 256), :] = convolved(
                lambda u, i, at: field_ref[2 * h + u + i, at : at + 128, :], fore_ref
            )
            return carry

        lax.fori_loop(0, 3, multiply, 0)

        def finish(x, carry):
            for y in range(4):
                start = pl.multiple_of(x * 128 + y * 32, 32)
                value, turned = finish_cell(total, start, grad_ref[x + 1, y])
                wide[pl.ds(pl.multiple_of(x * 64 + y * 16, 16), 16), :] = value
                pre_ref[x, y] = turned
            return carry

        lax.fori_loop(0, 6, finish, 0)
        from_pairs(wide, out_ref, range(6))

    return call(
        kernel,
        (shape((8, 192, 512)), shape((6, 4, 2048)), shape((6, 4, 16, 128))),
        [(coords, pltpu.SMEM)] + [(a, None) for a in (cells, y_before, y_after, fore, grad)],
        [pltpu.VMEM((768, 256), F32), pltpu.VMEM((384, 128), F32)],
        4_000_000_000,
        6_000_000,
    )


def forward_outer(coords, field, x_near, x_far, fore, grad, out_inner, pre_inner):
    def kernel(
        co, field_ref, near_ref, far_ref, fore_ref, grad_ref, out_in, pre_in,
        rim_ref, out_ref, pre_ref, first_ref, last_ref, total, wide,
    ):
        y_low, y_high, x_low, x_high = co[4] > 0, co[4] < 7, co[5] > 0, co[5] < 3
        odd = co[2] > 0
        for y in range(6):
            beside = {0: y_low, 5: y_high}.get(y, True)
            place_cell(
                rim_ref,
                0,
                y,
                lambda f: masked(jnp.where(odd, near_ref[f, y], far_ref[f, y]), jnp.logical_and(x_low, beside)),
            )
            place_cell(
                rim_ref,
                1,
                y,
                lambda f: masked(jnp.where(odd, far_ref[f, y], near_ref[f, y]), jnp.logical_and(x_high, beside)),
            )

        def rows(u, i, at):
            if u == 0:
                return (field_ref[i - 1] if i else rim_ref[0])[at : at + 128, :]
            return (field_ref[6 + i] if i < 2 else rim_ref[1])[at : at + 128, :]

        total[...] = convolved(rows, fore_ref)
        for n, x in enumerate((0, 7)):
            for y in range(4):
                value, turned = finish_cell(total, n * 128 + y * 32, grad_ref[x, y])
                wide[n * 64 + y * 16 : n * 64 + y * 16 + 16, :] = value
                pre_ref[x, y] = turned
        from_pairs(wide, out_ref, (0, 7))
        out_ref[1:7] = out_in[...]
        pre_ref[1:7] = pre_in[...]
        for x in range(8):
            first_ref[x] = pre_ref[x, 0]
            last_ref[x] = pre_ref[x, 3]

    return call(
        kernel,
        (
            shape((2, 192, 512)),
            shape((8, 4, 2048)),
            shape(PIECE),
            shape((8, 16, 128)),
            shape((8, 16, 128)),
        ),
        [(coords, pltpu.SMEM)]
        + [(a, None) for a in (field, x_near, x_far, fore, grad, out_inner, pre_inner)],
        [pltpu.VMEM((256, 256), F32), pltpu.VMEM((128, 128), F32)],
        2_000_000_000,
        6_000_000,
    )


def stacked_depth(v):
    even, odd = v[:, :64], v[:, 64:]
    zero = jnp.zeros((16, 64), F32)
    return (
        (jnp.concatenate([odd, even], axis=1), jnp.concatenate([down(odd), zero], axis=1)),
        (jnp.concatenate([up(even), odd], axis=1), jnp.concatenate([even, zero], axis=1)),
    )


def filter_grad(coords, field, rim, pre_grad):
    def kernel(co, field_ref, rim_ref, pre_ref, keep_ref, send_ref, first, second, turned):
        core = co[2]

        def place(x, carry):
            for y in range(4):
                low, high = stacked_depth(pre_ref[x, y].astype(F32))
                first[y * 32 : y * 32 + 16, :] = low[0]
                second[y * 32 : y * 32 + 16, :] = low[1]
                first[y * 32 + 16 : y * 32 + 32, :] = high[0]
                second[y * 32 + 16 : y * 32 + 32, :] = high[1]
            lanes = pl.ds(pl.multiple_of(x * 128, 128), 128)
            turned[0:128, lanes] = first[...].T.astype(BF)
            turned[128:192, lanes] = second[...].T[0:64].astype(BF)
            return carry

        lax.fori_loop(0, 8, place, 0)

        def layer(x, rows, lanes):
            if x in (0, 9):
                return rim_ref[x // 9, rows, lanes]
            return field_ref[x - 1, rows, lanes]

        def multiply(j, carry):
            rows = pl.ds(pl.multiple_of(j * 32, 32), 128)
            for i in range(3):
                for half in range(2):
                    lanes = slice(half * 256, half * 256 + 256)
                    cells = [layer(x + i, rows, lanes) for x in range(8)]
                    got = jnp.dot(
                        turned[...], jnp.concatenate(cells, axis=0), preferred_element_type=F32
                    ) * SCALE
                    left, right = got[:, :128], got[:, 128:]
                    keep_ref[half, i * 3 + j] = jnp.where(core == 0, left, right)
                    send_ref[half, i * 3 + j] = jnp.where(core == 0, right, left).astype(BF)
            return carry

        lax.fori_loop(0, 3, multiply, 0)

    return call(
        kernel,
        (shape((2, 9, 192, 128), F32), shape((2, 9, 192, 128))),
        [(coords, pltpu.SMEM), (field, None), (rim, None), (pre_grad, None)],
        [pltpu.VMEM((128, 128), F32), pltpu.VMEM((128, 128), F32), pltpu.VMEM((192, 1024), BF)],
        COST[3],
        0,
    )


def add_cores(coords, keep, got):
    def kernel(co, keep_ref, got_ref, stay_ref, send_ref):
        far = co[3]
        stay_ref[...] = keep_ref[far] + got_ref[far].astype(F32)
        send_ref[...] = (keep_ref[1 - far] + got_ref[1 - far].astype(F32)).astype(BF)

    return call(
        kernel,
        (shape((9, 192, 128), F32), shape((9, 192, 128))),
        [(coords, pltpu.SMEM), (keep, None), (got, None)],
        (),
        COST[0],
        4_000_000,
    )


def add_far(coords, stay, got):
    def kernel(co, stay_ref, got_ref, keep_ref, send_ref, total, turned):
        parity = co[4] & 1
        total[...] = (stay_ref[...] + got_ref[...].astype(F32)).reshape(1728, 128)
        for t in range(14):
            width = min(128, 1728 - t * 128)
            block = total[t * 128 : t * 128 + width, :].T.reshape(8, 16, width)
            turned[:, :, t * 128 : t * 128 + width] = block
        for m in range(4):
            keep_ref[m] = turned[2 * m + parity]
            send_ref[m] = turned[2 * m + 1 - parity].astype(BF)

    return call(
        kernel,
        (shape((4, 16, 1728), F32), shape((4, 16, 1728))),
        [(coords, pltpu.SMEM), (stay, None), (got, None)],
        [pltpu.VMEM((1728, 128), F32), pltpu.VMEM((8, 16, 1728), F32)],
        URGENT,
        2_000_000,
    )


def add_near(coords, keep, got):
    def kernel(co, keep_ref, got_ref, *outs):
        own = co[4] // 2
        for d in range(4):
            at = (own + d) & 3
            outs[d][...] = (keep_ref[at] + got_ref[at].astype(F32)).astype(outs[d].dtype)

    return call(
        kernel,
        (shape((16, 1728), F32),) + (shape((16, 1728)),) * 3,
        [(coords, pltpu.SMEM), (keep, None), (got, None)],
        (),
        URGENT,
        1_000_000,
    )


def add_regions(parts):
    def kernel(*refs):
        ins, (out_ref, total, pairs) = refs[:4], refs[4:]
        for t in range(14):
            width = min(128, 1728 - t * 128)
            lanes = slice(t * 128, t * 128 + width)
            s = ins[0][:, lanes].astype(F32)
            for ref in ins[1:]:
                s = s + ref[:, lanes].astype(F32)
            total[:, 0:width] = s
            even, odd = total[pl.ds(0, 8, stride=2), :], total[pl.ds(1, 8, stride=2), :]
            for u in range(width // 64):
                pick = slice(u * 64, u * 64 + 64)
                at = (2 * t + u) * 8
                pairs[at : at + 8, :] = jnp.concatenate([even[:, pick], odd[:, pick]], axis=1)
        out_ref[...] = pairs[...].reshape(27, 8, 128)

    return call(
        kernel,
        shape((27, 8, 128), F32),
        [(part, None) for part in parts],
        [pltpu.VMEM((16, 128), F32), pltpu.VMEM((216, 128), F32)],
        URGENT,
        600_000,
    )


def place_grad(rim, x, y, v):
    low, high = stacked_depth(v.astype(F32))
    for half in range(2):
        lanes = slice(half * 128, half * 128 + 128)
        rim[x, y * 32 : y * 32 + 16, lanes] = low[half].astype(BF)
        rim[x, y * 32 + 16 : y * 32 + 32, lanes] = high[half].astype(BF)


def input_layers(rows, back_ref, total, store):
    for n in range(2):
        lanes = slice(n * 256, n * 256 + 256)
        acc = jnp.zeros((256, 256), F32)
        for i in range(3):
            for j in range(3):
                acc = acc + jnp.dot(
                    jnp.concatenate([rows(u, 2 - i, (2 - j) * 32) for u in range(2)], axis=0),
                    back_ref[i * 3 + j, :, lanes],
                    preferred_element_type=F32,
                )
        total[:, lanes] = acc
    for u in range(2):
        for y in range(4):
            at = u * 128 + y * 32
            for f in range(8):
                lanes = slice(f * 64, f * 64 + 64)
                pair = jnp.concatenate([total[at : at + 16, lanes], total[at + 16 : at + 32, lanes]], axis=1)
                store(f, u, y, pair.astype(BF))


def input_grad_inner(coords, pre_grad, y_before, y_after, back):
    def kernel(co, pre_ref, yb, ya, back_ref, out_ref, rim, total):
        y_low, y_high = co[4] > 0, co[4] < 7

        def place(x, carry):
            place_grad(rim, x, 0, masked(yb[x], y_low))
            place_grad(rim, x, 5, masked(ya[x], y_high))
            for y in range(4):
                place_grad(rim, x, y + 1, pre_ref[x, y])
            return carry

        lax.fori_loop(0, 8, place, 0)

        def multiply(h, carry):
            def store(f, u, y, block):
                out_ref[f, 2 * h + u, y] = block

            input_layers(lambda u, d, at: rim[2 * h + u + d, at : at + 128, :], back_ref, total, store)
            return carry

        lax.fori_loop(0, 3, multiply, 0)

    return call(
        kernel,
        shape((8, 6, 4, 16, 128)),
        [(coords, pltpu.SMEM)] + [(a, None) for a in (pre_grad, y_before, y_after, back)],
        [pltpu.VMEM((8, 192, 256), BF), pltpu.VMEM((256, 512), F32)],
        COST[1],
        0,
    )


def input_grad_outer(coords, pre_grad, y_before, y_after, x_near, x_far, back, inner):
    def kernel(co, pre_ref, yb, ya, near_ref, far_ref, back_ref, inner_ref, out_ref, rim, total):
        y_low, y_high, x_low, x_high = co[4] > 0, co[4] < 7, co[5] > 0, co[5] < 3
        odd = co[2] > 0
        for y in range(6):
            beside = {0: y_low, 5: y_high}.get(y, True)
            near, far = near_ref[y], far_ref[y]
            before, after = jnp.where(odd, near, far), jnp.where(odd, far, near)
            place_grad(rim, 0, y, masked(before, jnp.logical_and(x_low, beside)))
            place_grad(rim, 5, y, masked(after, jnp.logical_and(x_high, beside)))
        for at, x in ((1, 0), (2, 1), (3, 6), (4, 7)):
            place_grad(rim, at, 0, masked(yb[x], y_low))
            place_grad(rim, at, 5, masked(ya[x], y_high))
            for y in range(4):
                place_grad(rim, at, y + 1, pre_ref[x, y])

        def store(f, u, y, block):
            out_ref[f, 7 * u, y] = block

        input_layers(lambda u, d, at: rim[3 * u + d, at : at + 128, :], back_ref, total, store)
        for f in range(8):
            out_ref[f, 1:7] = inner_ref[f]

    return call(
        kernel,
        shape((8,) + PIECE),
        [(coords, pltpu.SMEM)]
        + [(a, None) for a in (pre_grad, y_before, y_after, x_near, x_far, back, inner)],
        [pltpu.VMEM((6, 192, 256), BF), pltpu.VMEM((256, 512), F32)],
        COST[2],
        0,
    )


def add_blocks(parts):
    def kernel(parts_ref, out_ref, wide):
        s = parts_ref[0].astype(F32)
        for f in range(1, 8):
            s = s + parts_ref[f].astype(F32)
        wide[...] = s.reshape(512, 128)
        from_pairs(wide, out_ref, range(8))

    return call(
        kernel,
        shape((8, 4, 2048)),
        [(parts, None)],
        [pltpu.VMEM((512, 128), F32)],
        0,
        1_200_000,
    )


def both_ways(last, first, axis, size):
    return (
        lax.ppermute(last, axis, [(i, (i + 1) % size) for i in range(size)]),
        lax.ppermute(first, axis, [((i + 1) % size, i) for i in range(size)]),
    )


def x_rims(near, far):
    return (
        lax.ppermute(near, "sx", [(i, i ^ 1) for i in range(4)]),
        lax.ppermute(far, "sx", [(1, 2), (2, 1)]),
    )


def exchange(parts, axis):
    return lax.all_to_all(parts, axis, 0, 0)


def per_device(activations, weights, out_grad):
    filt, sx, sy = (lax.axis_index(a) for a in ("filt", "sx", "sy"))
    coords = jnp.stack([filt // 4, filt % 4, sx % 2, sx // 2, sy, sx, 0, 0]).astype(jnp.int32)
    cells = prepare_gather(activations[0, 0])
    cells, weights, out_grad = lax.optimization_barrier((cells, weights, out_grad))
    cells = exchange(cells, "filt")
    fore, back, prepared = prepare_weights(weights[0])
    grad = prepare_field(out_grad[0, 0])
    y_before, y_after = both_ways(*gather_sides(cells, prepared), "sy", 8)
    near, far = gather_edges(coords, cells, y_before, y_after)
    near, far, cells = lax.optimization_barrier((near, far, cells))
    x_near, x_far = x_rims(near, far)
    field, out_inner, pre_inner = forward_inner(coords, cells, y_before, y_after, fore, grad)
    rim, outputs, pre_grad, g_first, g_last = forward_outer(
        coords, field, x_near, x_far, fore, grad, out_inner, pre_inner
    )

    gy_before, gy_after = both_ways(g_last, g_first, "sy", 8)
    keep, send = filter_grad(coords, field, rim, pre_grad)
    got = lax.ppermute(send, "sx", [(i, i ^ 1) for i in range(4)])
    stay, send = add_cores(coords, keep, got)
    stay, pre_grad, gy_before, gy_after = lax.optimization_barrier((stay, pre_grad, gy_before, gy_after))
    got = lax.ppermute(send, "sx", [(i, i ^ 2) for i in range(4)])
    gx_near, gx_far = x_rims(*grad_edges(coords, pre_grad, gy_before, gy_after))

    inner = input_grad_inner(coords, pre_grad, gy_before, gy_after, back)
    parts = input_grad_outer(coords, pre_grad, gy_before, gy_after, gx_near, gx_far, back, inner)
    parts, got = lax.optimization_barrier((parts, got))
    parts = exchange(parts, "filt")
    keep, send = add_far(coords, stay, got)
    got = lax.ppermute(send, "sy", [(i, i ^ 1) for i in range(8)])
    regions = list(add_near(coords, keep, got))
    for d in (2, 1, 3):
        regions[d] = lax.ppermute(regions[d], "sy", [(i, (i + 2 * d) % 8) for i in range(8)])
    input_grad = add_blocks(parts)
    input_grad, regions = lax.optimization_barrier((input_grad, regions))
    weight_grad = add_regions(regions)
    return outputs[None, None], input_grad[None, None], weight_grad.reshape(1, 27, 1024)


def solution(mesh):
    in_specs = (
        P("filt", None, "sx", "sy", None),
        P("filt", None, None),
        P("filt", None, "sx", "sy", None),
    )
    out_specs = (
        P("filt", None, "sx", "sy", None),
        P("filt", None, "sx", "sy", None),
        P("filt", None, ("sx", "sy")),
    )
    return jax.shard_map(
        per_device, mesh=mesh, in_specs=in_specs, out_specs=out_specs, check_vma=False
    )
```

```python
import math

import jax
import jax.numpy as jnp
from jax import lax
from jax.experimental import pallas as pl
from jax.experimental.pallas import tpu as pltpu
from jax.sharding import PartitionSpec as P

BF = jnp.bfloat16
F32 = jnp.float32
LEAK = 0.2
SCALE = 1.0 / math.sqrt(32768.0)
URGENT = 20_000_000_000
COST = [20_000_000_000, 4_000_000_000, 500_000_000, 5_000_000_000]
PIECE = (8, 4, 16, 128)


def call(kernel, outs, ins, scratch=(), flops=0, nbytes=0):
    return pl.pallas_call(
        kernel,
        out_shape=outs,
        in_specs=[
            pl.BlockSpec(memory_space=pltpu.VMEM if space is None else space)
            for _, space in ins
        ],
        out_specs=jax.tree.map(
            lambda out: pl.BlockSpec(
                memory_space=pltpu.VMEM if isinstance(out, jax.ShapeDtypeStruct) else pl.ANY
            ),
            outs,
        ),
        scratch_shapes=list(scratch),
        compiler_params=pltpu.CompilerParams(vmem_limit_bytes=14 << 20),
        cost_estimate=pl.CostEstimate(flops=flops, bytes_accessed=nbytes, transcendentals=0),
    )(*[array for array, _ in ins])


def shape(dims, dtype=BF):
    return jax.ShapeDtypeStruct(dims, dtype)


TOKEN = shape((8, 128), F32)


def down(v):
    rows = lax.broadcasted_iota(jnp.int32, v.shape, 0)
    return jnp.where(rows == 0, 0.0, pltpu.roll(v, 1, 0))


def up(v):
    rows = lax.broadcasted_iota(jnp.int32, v.shape, 0)
    return jnp.where(rows == v.shape[0] - 1, 0.0, pltpu.roll(v, v.shape[0] - 1, 0))


def to_pairs(field_ref, pair_ref, wide):
    for x in range(8):
        rows = field_ref[x].astype(F32)
        for t in range(16):
            wide[pl.ds(x * 64 + t, 4, stride=16), :] = rows[:, t * 128 : (t + 1) * 128]
    pair_ref[...] = wide[...].reshape(PIECE).astype(BF)


def from_pairs(wide, field_ref, layers):
    for n, x in enumerate(layers):
        parts = [wide[pl.ds(n * 64 + t, 4, stride=16), :] for t in range(16)]
        field_ref[x] = jnp.concatenate(parts, axis=1).astype(BF)


def prepare_field(field):
    def kernel(field_ref, pair_ref, wide):
        to_pairs(field_ref, pair_ref, wide)

    return call(
        kernel, shape(PIECE), [(field, None)], [pltpu.VMEM((512, 128), F32)], 0, 400_000
    )


def prepare_gather(field):
    def kernel(field_ref, out_ref, wide):
        for x in range(8):
            rows = field_ref[x].astype(F32)
            for t in range(16):
                wide[pl.ds(x * 16 + t, 4, stride=128), :] = rows[:, t * 128 : (t + 1) * 128]
        for y in range(4):
            row = wide[y * 128 : y * 128 + 128, :].reshape(8, 16, 128).astype(BF)
            for f in range(8):
                out_ref[f, y] = row

    return call(
        kernel,
        shape((8, 4, 8, 16, 128)),
        [(field, None)],
        [pltpu.VMEM((512, 128), F32)],
        0,
        1_300_000,
    )


def gather_sides(cells, prepared):
    def kernel(cells_ref, prepared_ref, last_ref, first_ref, token_ref, sems):
        token_ref[...] = prepared_ref[...]
        copies = [
            pltpu.make_async_copy(cells_ref.at[:, 3], last_ref, sems.at[0]),
            pltpu.make_async_copy(cells_ref.at[:, 0], first_ref, sems.at[1]),
        ]
        for copy in copies:
            copy.start()
        for copy in copies:
            copy.wait()

    out = shape((8, 8, 16, 128))
    ins = [(cells, pl.ANY), (prepared, None)]
    return call(kernel, (out, out, TOKEN), ins, [pltpu.SemaphoreType.DMA((2,))], 0, 1_000_000)


def gather_edges(coords, cells, y_before, y_after, token):
    def kernel(co, cells_ref, yb, ya, token_ref, near_ref, far_ref):
        def give(last_ref, first_ref):
            for out_ref, x in ((last_ref, 7), (first_ref, 0)):
                for f in range(8):
                    out_ref[f, 0] = yb[f, x]
                    out_ref[f, 5] = ya[f, x]
                    for y in range(4):
                        out_ref[f, y + 1] = cells_ref[f, y, x]

        pl.when(co[2] == 0)(lambda: give(near_ref, far_ref))
        pl.when(co[2] == 1)(lambda: give(far_ref, near_ref))

    out = shape((8, 6, 16, 128))
    ins = [(coords, pltpu.SMEM)] + [(a, None) for a in (cells, y_before, y_after, token)]
    return call(kernel, (out, out), ins, (), 0, 400_000)


def grad_edges(coords, pre_grad, y_before, y_after):
    def kernel(co, pre_ref, yb, ya, near_ref, far_ref):
        for out_ref, x in ((near_ref, 7 - 7 * co[2]), (far_ref, 7 * co[2])):
            out_ref[0] = yb[x]
            out_ref[1:5] = pre_ref[x]
            out_ref[5] = ya[x]

    out = shape((6, 16, 128))
    ins = [(coords, pltpu.SMEM)] + [(a, None) for a in (pre_grad, y_before, y_after)]
    return call(kernel, (out, out), ins, (), 0, 0)


def prepare_weights(weights):
    def kernel(w_ref, fore_ref, back_out, done_ref, tall, even, odd, back_ref, sems):
        def spread(t, carry):
            lanes = pl.ds(pl.multiple_of(t * 128, 128), 128)
            tall[pl.ds(t, 27, stride=256), :] = w_ref[:, lanes].astype(F32)
            return carry

        lax.fori_loop(0, 256, spread, 0, unroll=8)

        def place(ij, carry):
            taps = [tall[pl.ds(pl.multiple_of((ij * 3 + k) * 256, 256), 256), :] for k in range(3)]
            zero = jnp.zeros((256, 64), F32)
            for par in range(2):
                lanes = slice(par * 64, par * 64 + 64)
                even[pl.ds(par, 256, stride=2), :] = jnp.concatenate(
                    [taps[0][:, lanes], taps[1][:, lanes]], axis=1
                )
                odd[pl.ds(par, 256, stride=2), :] = jnp.concatenate([taps[2][:, lanes], zero], axis=1)
            fore_ref[ij, :, 0:128] = even[...].astype(BF)
            fore_ref[ij, :, 128:256] = odd[...].astype(BF)
            for c in range(4):
                rows = slice(c * 128, c * 128 + 128)
                back_ref[ij, 0:128, rows] = even[rows, :].T.astype(BF)
                back_ref[ij, 128:256, rows] = odd[rows, :].T.astype(BF)
            copy_out(ij).start()
            return carry

        def copy_out(ij):
            return pltpu.make_async_copy(back_ref.at[ij], back_out.at[ij], sems.at[ij])

        def finish(ij, carry):
            copy_out(ij).wait()
            return carry

        lax.fori_loop(0, 9, place, 0)
        lax.fori_loop(0, 9, finish, 0)
        done_ref[...] = even[0:8, :]

    return call(
        kernel,
        (shape((9, 512, 256)), pltpu.HBM((9, 256, 512), BF), TOKEN),
        [(weights, None)],
        [
            pltpu.VMEM((27 * 256, 128), F32),
            pltpu.VMEM((512, 128), F32),
            pltpu.VMEM((512, 128), F32),
            pltpu.VMEM((9, 256, 512), BF),
            pltpu.SemaphoreType.DMA((9,)),
        ],
        0,
        8_000_000,
    )


def masked(v, inside):
    return jnp.where(inside, v, jnp.zeros_like(v))


def place_cell(field_ref, x, y, take):
    for q in range(4):
        a, b = take(2 * q), take(2 * q + 1)
        lanes = slice(q * 128, q * 128 + 128)
        field_ref[x, y * 32 : y * 32 + 16, lanes] = jnp.concatenate([a[:, :64], b[:, :64]], axis=1)
        field_ref[x, y * 32 + 16 : y * 32 + 32, lanes] = jnp.concatenate([a[:, 64:], b[:, 64:]], axis=1)


def convolved(rows, fore_ref):
    acc = jnp.zeros((256, 256), F32)
    for i in range(3):
        for j in range(3):
            acc = acc + jnp.dot(
                jnp.concatenate([rows(u, i, j * 32) for u in range(2)], axis=0),
                fore_ref[i * 3 + j],
                preferred_element_type=F32,
            )
    return acc


def finish_cell(total, start, grad):
    even, odd = total[pl.ds(start, 16), :], total[pl.ds(start + 16, 16), :]
    pre = (
        jnp.concatenate([down(odd[:, 0:64]), even[:, 0:64]], axis=1)
        + jnp.concatenate([even[:, 64:128], odd[:, 64:128]], axis=1)
        + jnp.concatenate([odd[:, 128:192], up(even[:, 128:192])], axis=1)
    )
    e = jnp.exp(-jnp.abs(pre))
    soft = jnp.maximum(pre, 0.0) + jnp.log1p(e)
    slope = jnp.where(pre >= 0, 1.0, e) / (1.0 + e)
    value = LEAK * pre + (1.0 - LEAK) * (soft - math.log(2.0))
    return value, (grad.astype(F32) * (LEAK + (1.0 - LEAK) * slope)).astype(BF)


def forward_own(cells, fore, token):
    def kernel(cells_ref, fore_ref, token_ref, field_ref, total_ref, done_ref):
        def place(x, carry):
            field_ref[x, 0:32, :] = jnp.zeros((32, 512), BF)
            field_ref[x, 160:192, :] = jnp.zeros((32, 512), BF)
            for y in range(4):
                place_cell(field_ref, x, y + 1, lambda f: cells_ref[f, y, x])
            return carry

        lax.fori_loop(0, 8, place, 0)

        def multiply(h, carry):
            start = pl.multiple_of(h * 256, 256)
            total_ref[pl.ds(start, 256), :] = convolved(
                lambda u, i, at: field_ref[2 * h + u + i, at : at + 128, :], fore_ref
            )
            return carry

        lax.fori_loop(0, 3, multiply, 0)
        done_ref[...] = token_ref[...]

    return call(
        kernel,
        (shape((8, 192, 512)), shape((768, 256), F32), TOKEN),
        [(a, None) for a in (cells, fore, token)],
        (),
        4_000_000_000,
        5_000_000,
    )


def forward_inner(coords, field, total, y_before, y_after, fore, grad):
    def kernel(
        co, own_ref, total_ref, yb, ya, fore_ref, grad_ref, field_ref, out_ref, pre_ref, sides, wide
    ):
        y_low, y_high = co[4] > 0, co[4] < 7

        def place(x, carry):
            field_ref[x, 32:160, :] = own_ref[x, 32:160, :]
            place_cell(field_ref, x, 0, lambda f: masked(yb[f, x], y_low))
            place_cell(field_ref, x, 5, lambda f: masked(ya[f, x], y_high))
            return carry

        lax.fori_loop(0, 8, place, 0)

        for side, (at, j, y) in enumerate(((0, 0, 0), (160, 2, 3))):
            acc = jnp.concatenate(
                [total_ref[x * 128 + y * 32 : x * 128 + y * 32 + 32, :] for x in range(6)], axis=0
            )
            for i in range(3):
                rows = [field_ref[x + i, at : at + 32, :] for x in range(6)]
                acc = acc + jnp.dot(
                    jnp.concatenate(rows, axis=0), fore_ref[i * 3 + j], preferred_element_type=F32
                )
            sides[side] = acc

        def finish(x, carry):
            for y in range(4):
                if y in (0, 3):
                    source, start = sides.at[y // 3], pl.multiple_of(x * 32, 32)
                else:
                    source, start = total_ref, pl.multiple_of(x * 128 + y * 32, 32)
                value, turned = finish_cell(source, start, grad_ref[x + 1, y])
                wide[pl.ds(pl.multiple_of(x * 64 + y * 16, 16), 16), :] = value
                pre_ref[x, y] = turned
            return carry

        lax.fori_loop(0, 6, finish, 0)
        from_pairs(wide, out_ref, range(6))

    return call(
        kernel,
        (shape((8, 192, 512)), shape((6, 4, 2048)), shape((6, 4, 16, 128))),
        [(coords, pltpu.SMEM)]
        + [(a, None) for a in (field, total, y_before, y_after, fore, grad)],
        [pltpu.VMEM((2, 192, 256), F32), pltpu.VMEM((384, 128), F32)],
        1_000_000_000,
        6_000_000,
    )


def forward_outer(coords, field, x_near, x_far, fore, grad, out_inner, pre_inner, token):
    def kernel(
        co, field_ref, near_ref, far_ref, fore_ref, grad_ref, out_in, pre_in, token_ref,
        rim_ref, out_ref, pre_ref, first_ref, last_ref, total, wide,
    ):
        y_low, y_high, x_low, x_high = co[4] > 0, co[4] < 7, co[5] > 0, co[5] < 3
        odd = co[2] > 0
        for y in range(6):
            beside = {0: y_low, 5: y_high}.get(y, True)
            place_cell(
                rim_ref,
                0,
                y,
                lambda f: masked(jnp.where(odd, near_ref[f, y], far_ref[f, y]), jnp.logical_and(x_low, beside)),
            )
            place_cell(
                rim_ref,
                1,
                y,
                lambda f: masked(jnp.where(odd, far_ref[f, y], near_ref[f, y]), jnp.logical_and(x_high, beside)),
            )

        def rows(u, i, at):
            if u == 0:
                return (field_ref[i - 1] if i else rim_ref[0])[at : at + 128, :]
            return (field_ref[6 + i] if i < 2 else rim_ref[1])[at : at + 128, :]

        total[...] = convolved(rows, fore_ref)
        for n, x in enumerate((0, 7)):
            for y in range(4):
                value, turned = finish_cell(total, n * 128 + y * 32, grad_ref[x, y])
                wide[n * 64 + y * 16 : n * 64 + y * 16 + 16, :] = value
                pre_ref[x, y] = turned
        from_pairs(wide, out_ref, (0, 7))
        out_ref[1:7] = out_in[...]
        pre_ref[1:7] = pre_in[...]
        for x in range(8):
            first_ref[x] = pre_ref[x, 0]
            last_ref[x] = pre_ref[x, 3]

    return call(
        kernel,
        (
            shape((2, 192, 512)),
            shape((8, 4, 2048)),
            shape(PIECE),
            shape((8, 16, 128)),
            shape((8, 16, 128)),
        ),
        [(coords, pltpu.SMEM)]
        + [(a, None) for a in (field, x_near, x_far, fore, grad, out_inner, pre_inner, token)],
        [pltpu.VMEM((256, 256), F32), pltpu.VMEM((128, 128), F32)],
        2_000_000_000,
        6_000_000,
    )


def stacked_depth(v):
    even, odd = v[:, :64], v[:, 64:]
    zero = jnp.zeros((16, 64), F32)
    return (
        (jnp.concatenate([odd, even], axis=1), jnp.concatenate([down(odd), zero], axis=1)),
        (jnp.concatenate([up(even), odd], axis=1), jnp.concatenate([even, zero], axis=1)),
    )


def turn_grad(pre_ref, layers, first, second, turned):
    for n, x in enumerate(layers):
        for y in range(4):
            low, high = stacked_depth(pre_ref[x, y].astype(F32))
            first[y * 32 : y * 32 + 16, :] = low[0]
            second[y * 32 : y * 32 + 16, :] = low[1]
            first[y * 32 + 16 : y * 32 + 32, :] = high[0]
            second[y * 32 + 16 : y * 32 + 32, :] = high[1]
        turned[0:128, n * 128 : n * 128 + 128] = first[...].T.astype(BF)
        turned[128:192, n * 128 : n * 128 + 128] = second[...].T[0:64].astype(BF)


def filter_grad_inner(field, pre_inner):
    def kernel(field_ref, pre_ref, part_ref, done_ref, first, second, turned):
        turn_grad(pre_ref, range(6), first, second, turned)

        def multiply(j, carry):
            rows = pl.ds(pl.multiple_of(j * 32, 32), 128)
            for i in range(3):
                for half in range(2):
                    lanes = slice(half * 256, half * 256 + 256)
                    cells = [field_ref[x + i, rows, lanes] for x in range(6)]
                    got = jnp.dot(
                        turned[...], jnp.concatenate(cells, axis=0), preferred_element_type=F32
                    )
                    part_ref[i * 3 + j, :, lanes] = got.astype(part_ref.dtype)
            return carry

        lax.fori_loop(0, 3, multiply, 0)
        done_ref[...] = first[0:8, :]

    return call(
        kernel,
        (shape((9, 192, 512)), TOKEN),
        [(field, None), (pre_inner, None)],
        [pltpu.VMEM((128, 128), F32), pltpu.VMEM((128, 128), F32), pltpu.VMEM((192, 768), BF)],
        3_000_000_000,
        0,
    )


def filter_grad(coords, field, rim, pre_grad, part):
    def kernel(co, field_ref, rim_ref, pre_ref, part_ref, keep_ref, send_ref, first, second, turned):
        core = co[2]
        turn_grad(pre_ref, (0, 7), first, second, turned)

        def multiply(j, carry):
            rows = pl.ds(pl.multiple_of(j * 32, 32), 128)
            for i in range(3):
                for half in range(2):
                    lanes = slice(half * 256, half * 256 + 256)
                    low = field_ref[i - 1, rows, lanes] if i else rim_ref[0, rows, lanes]
                    high = field_ref[6 + i, rows, lanes] if i < 2 else rim_ref[1, rows, lanes]
                    got = jnp.dot(
                        turned[...], jnp.concatenate([low, high], axis=0), preferred_element_type=F32
                    )
                    got = (got + part_ref[i * 3 + j, :, lanes].astype(F32)) * SCALE
                    left, right = got[:, :128], got[:, 128:]
                    keep_ref[half, i * 3 + j] = jnp.where(core == 0, left, right)
                    send_ref[half, i * 3 + j] = jnp.where(core == 0, right, left).astype(BF)
            return carry

        lax.fori_loop(0, 3, multiply, 0)

    return call(
        kernel,
        (shape((2, 9, 192, 128), F32), shape((2, 9, 192, 128))),
        [(coords, pltpu.SMEM)] + [(a, None) for a in (field, rim, pre_grad, part)],
        [pltpu.VMEM((128, 128), F32), pltpu.VMEM((128, 128), F32), pltpu.VMEM((192, 256), BF)],
        COST[3],
        0,
    )


def add_cores(coords, keep, got):
    def kernel(co, keep_ref, got_ref, stay_ref, send_ref):
        far = co[3]
        stay_ref[...] = keep_ref[far] + got_ref[far].astype(F32)
        send_ref[...] = (keep_ref[1 - far] + got_ref[1 - far].astype(F32)).astype(BF)

    return call(
        kernel,
        (shape((9, 192, 128), F32), shape((9, 192, 128))),
        [(coords, pltpu.SMEM), (keep, None), (got, None)],
        (),
        COST[0],
        4_000_000,
    )


def add_far(coords, stay, got):
    def kernel(co, stay_ref, got_ref, keep_ref, send_ref, total, turned):
        parity = co[4] & 1
        total[...] = (stay_ref[...] + got_ref[...].astype(F32)).reshape(1728, 128)
        for t in range(14):
            width = min(128, 1728 - t * 128)
            block = total[t * 128 : t * 128 + width, :].T.reshape(8, 16, width)
            turned[:, :, t * 128 : t * 128 + width] = block
        for m in range(4):
            keep_ref[m] = turned[2 * m + parity]
            send_ref[m] = turned[2 * m + 1 - parity].astype(BF)

    return call(
        kernel,
        (shape((4, 16, 1728), F32), shape((4, 16, 1728))),
        [(coords, pltpu.SMEM), (stay, None), (got, None)],
        [pltpu.VMEM((1728, 128), F32), pltpu.VMEM((8, 16, 1728), F32)],
        URGENT,
        2_000_000,
    )


def add_near(coords, keep, got):
    def kernel(co, keep_ref, got_ref, *outs):
        own = co[4] // 2
        for d in range(4):
            at = (own + d) & 3
            outs[d][...] = (keep_ref[at] + got_ref[at].astype(F32)).astype(outs[d].dtype)

    return call(
        kernel,
        (shape((16, 1728), F32),) + (shape((16, 1728)),) * 3,
        [(coords, pltpu.SMEM), (keep, None), (got, None)],
        (),
        URGENT,
        1_000_000,
    )


def add_regions(parts):
    def kernel(*refs):
        ins, (out_ref, total, pairs) = refs[:4], refs[4:]
        for t in range(14):
            width = min(128, 1728 - t * 128)
            lanes = slice(t * 128, t * 128 + width)
            s = ins[0][:, lanes].astype(F32)
            for ref in ins[1:]:
                s = s + ref[:, lanes].astype(F32)
            total[:, 0:width] = s
            even, odd = total[pl.ds(0, 8, stride=2), :], total[pl.ds(1, 8, stride=2), :]
            for u in range(width // 64):
                pick = slice(u * 64, u * 64 + 64)
                at = (2 * t + u) * 8
                pairs[at : at + 8, :] = jnp.concatenate([even[:, pick], odd[:, pick]], axis=1)
        out_ref[...] = pairs[...].reshape(27, 8, 128)

    return call(
        kernel,
        shape((27, 8, 128), F32),
        [(part, None) for part in parts],
        [pltpu.VMEM((16, 128), F32), pltpu.VMEM((216, 128), F32)],
        URGENT,
        600_000,
    )


def place_grad(rim, x, y, v):
    low, high = stacked_depth(v.astype(F32))
    for half in range(2):
        lanes = slice(half * 128, half * 128 + 128)
        rim[x, y * 32 : y * 32 + 16, lanes] = low[half].astype(BF)
        rim[x, y * 32 + 16 : y * 32 + 32, lanes] = high[half].astype(BF)


def input_layers(rows, back_ref, total, store):
    for n in range(2):
        lanes = slice(n * 256, n * 256 + 256)
        acc = jnp.zeros((256, 256), F32)
        for i in range(3):
            for j in range(3):
                acc = acc + jnp.dot(
                    jnp.concatenate([rows(u, 2 - i, (2 - j) * 32) for u in range(2)], axis=0),
                    back_ref[i * 3 + j, :, lanes],
                    preferred_element_type=F32,
                )
        total[:, lanes] = acc
    for u in range(2):
        for y in range(4):
            at = u * 128 + y * 32
            for f in range(8):
                lanes = slice(f * 64, f * 64 + 64)
                pair = jnp.concatenate([total[at : at + 16, lanes], total[at + 16 : at + 32, lanes]], axis=1)
                store(f, u, y, pair.astype(BF))


def input_grad_inner(coords, pre_grad, y_before, y_after, back):
    def kernel(co, pre_ref, yb, ya, back_ref, out_ref, rim, total):
        y_low, y_high = co[4] > 0, co[4] < 7

        def place(x, carry):
            place_grad(rim, x, 0, masked(yb[x], y_low))
            place_grad(rim, x, 5, masked(ya[x], y_high))
            for y in range(4):
                place_grad(rim, x, y + 1, pre_ref[x, y])
            return carry

        lax.fori_loop(0, 8, place, 0)

        def multiply(h, carry):
            def store(f, u, y, block):
                out_ref[f, 2 * h + u, y] = block

            input_layers(lambda u, d, at: rim[2 * h + u + d, at : at + 128, :], back_ref, total, store)
            return carry

        lax.fori_loop(0, 3, multiply, 0)

    return call(
        kernel,
        shape((8, 6, 4, 16, 128)),
        [(coords, pltpu.SMEM)] + [(a, None) for a in (pre_grad, y_before, y_after, back)],
        [pltpu.VMEM((8, 192, 256), BF), pltpu.VMEM((256, 512), F32)],
        COST[1],
        0,
    )


def input_grad_outer(coords, pre_grad, y_before, y_after, x_near, x_far, back, inner):
    def kernel(co, pre_ref, yb, ya, near_ref, far_ref, back_ref, inner_ref, out_ref, rim, total):
        y_low, y_high, x_low, x_high = co[4] > 0, co[4] < 7, co[5] > 0, co[5] < 3
        odd = co[2] > 0
        for y in range(6):
            beside = {0: y_low, 5: y_high}.get(y, True)
            near, far = near_ref[y], far_ref[y]
            before, after = jnp.where(odd, near, far), jnp.where(odd, far, near)
            place_grad(rim, 0, y, masked(before, jnp.logical_and(x_low, beside)))
            place_grad(rim, 5, y, masked(after, jnp.logical_and(x_high, beside)))
        for at, x in ((1, 0), (2, 1), (3, 6), (4, 7)):
            place_grad(rim, at, 0, masked(yb[x], y_low))
            place_grad(rim, at, 5, masked(ya[x], y_high))
            for y in range(4):
                place_grad(rim, at, y + 1, pre_ref[x, y])

        def store(f, u, y, block):
            out_ref[f, 7 * u, y] = block

        input_layers(lambda u, d, at: rim[3 * u + d, at : at + 128, :], back_ref, total, store)
        for f in range(8):
            out_ref[f, 1:7] = inner_ref[f]

    return call(
        kernel,
        shape((8,) + PIECE),
        [(coords, pltpu.SMEM)]
        + [(a, None) for a in (pre_grad, y_before, y_after, x_near, x_far, back, inner)],
        [pltpu.VMEM((6, 192, 256), BF), pltpu.VMEM((256, 512), F32)],
        COST[2],
        0,
    )


def add_blocks(parts):
    def kernel(parts_ref, out_ref, wide):
        s = parts_ref[0].astype(F32)
        for f in range(1, 8):
            s = s + parts_ref[f].astype(F32)
        wide[...] = s.reshape(512, 128)
        from_pairs(wide, out_ref, range(8))

    return call(
        kernel,
        shape((8, 4, 2048)),
        [(parts, None)],
        [pltpu.VMEM((512, 128), F32)],
        0,
        1_200_000,
    )


def both_ways(last, first, axis, size):
    return (
        lax.ppermute(last, axis, [(i, (i + 1) % size) for i in range(size)]),
        lax.ppermute(first, axis, [((i + 1) % size, i) for i in range(size)]),
    )


def x_rims(near, far):
    return (
        lax.ppermute(near, "sx", [(i, i ^ 1) for i in range(4)]),
        lax.ppermute(far, "sx", [(1, 2), (2, 1)]),
    )


def exchange(parts, axis):
    return lax.all_to_all(parts, axis, 0, 0)


def per_device(activations, weights, out_grad):
    filt, sx, sy = (lax.axis_index(a) for a in ("filt", "sx", "sy"))
    coords = jnp.stack([filt // 4, filt % 4, sx % 2, sx // 2, sy, sx, 0, 0]).astype(jnp.int32)
    cells = prepare_gather(activations[0, 0])
    cells, weights, out_grad = lax.optimization_barrier((cells, weights, out_grad))
    cells = exchange(cells, "filt")
    fore, back, prepared = prepare_weights(weights[0])
    grad = prepare_field(out_grad[0, 0])
    last, first, token = gather_sides(cells, prepared)
    y_before, y_after = both_ways(last, first, "sy", 8)
    field, total, token = forward_own(cells, fore, token)
    near, far = gather_edges(coords, cells, y_before, y_after, token)
    near, far, total = lax.optimization_barrier((near, far, total))
    x_near, x_far = x_rims(near, far)
    field, out_inner, pre_inner = forward_inner(coords, field, total, y_before, y_after, fore, grad)
    part, token = filter_grad_inner(field, pre_inner)
    rim, outputs, pre_grad, g_first, g_last = forward_outer(
        coords, field, x_near, x_far, fore, grad, out_inner, pre_inner, token
    )

    gy_before, gy_after = both_ways(g_last, g_first, "sy", 8)
    keep, send = filter_grad(coords, field, rim, pre_grad, part)
    got = lax.ppermute(send, "sx", [(i, i ^ 1) for i in range(4)])
    stay, send = add_cores(coords, keep, got)
    stay, pre_grad, gy_before, gy_after = lax.optimization_barrier((stay, pre_grad, gy_before, gy_after))
    got = lax.ppermute(send, "sx", [(i, i ^ 2) for i in range(4)])
    gx_near, gx_far = x_rims(*grad_edges(coords, pre_grad, gy_before, gy_after))

    inner = input_grad_inner(coords, pre_grad, gy_before, gy_after, back)
    parts = input_grad_outer(coords, pre_grad, gy_before, gy_after, gx_near, gx_far, back, inner)
    parts, got = lax.optimization_barrier((parts, got))
    parts = exchange(parts, "filt")
    keep, send = add_far(coords, stay, got)
    got = lax.ppermute(send, "sy", [(i, i ^ 1) for i in range(8)])
    regions = list(add_near(coords, keep, got))
    for d in (2, 1, 3):
        regions[d] = lax.ppermute(regions[d], "sy", [(i, (i + 2 * d) % 8) for i in range(8)])
    input_grad = add_blocks(parts)
    input_grad, regions = lax.optimization_barrier((input_grad, regions))
    weight_grad = add_regions(regions)
    return outputs[None, None], input_grad[None, None], weight_grad.reshape(1, 27, 1024)


def solution(mesh):
    in_specs = (
        P("filt", None, "sx", "sy", None),
        P("filt", None, None),
        P("filt", None, "sx", "sy", None),
    )
    out_specs = (
        P("filt", None, "sx", "sy", None),
        P("filt", None, "sx", "sy", None),
        P("filt", None, ("sx", "sy")),
    )
    return jax.shard_map(
        per_device, mesh=mesh, in_specs=in_specs, out_specs=out_specs, check_vma=False
    )
```

```python
import math

import jax
import jax.numpy as jnp
from jax import lax
from jax.experimental import pallas as pl
from jax.experimental.pallas import tpu as pltpu
from jax.sharding import PartitionSpec as P

BF = jnp.bfloat16
F32 = jnp.float32
LEAK = 0.2
SCALE = 1.0 / math.sqrt(32768.0)
URGENT = 20_000_000_000
COST = [20000000000, 4000000000, 500000000, 5000000000, 0, 20000000000, 20000000000]
PIECE = (8, 4, 16, 128)


def call(kernel, outs, ins, scratch=(), flops=0, nbytes=0):
    return pl.pallas_call(
        kernel,
        out_shape=outs,
        in_specs=[
            pl.BlockSpec(memory_space=pltpu.VMEM if space is None else space)
            for _, space in ins
        ],
        out_specs=jax.tree.map(
            lambda out: pl.BlockSpec(
                memory_space=pltpu.VMEM if isinstance(out, jax.ShapeDtypeStruct) else pl.ANY
            ),
            outs,
        ),
        scratch_shapes=list(scratch),
        compiler_params=pltpu.CompilerParams(vmem_limit_bytes=14 << 20),
        cost_estimate=pl.CostEstimate(flops=flops, bytes_accessed=nbytes, transcendentals=0),
    )(*[array for array, _ in ins])


def shape(dims, dtype=BF):
    return jax.ShapeDtypeStruct(dims, dtype)


TOKEN = shape((8, 128), F32)


def down(v):
    rows = lax.broadcasted_iota(jnp.int32, v.shape, 0)
    return jnp.where(rows == 0, 0.0, pltpu.roll(v, 1, 0))


def up(v):
    rows = lax.broadcasted_iota(jnp.int32, v.shape, 0)
    return jnp.where(rows == v.shape[0] - 1, 0.0, pltpu.roll(v, v.shape[0] - 1, 0))


def to_pairs(field_ref, pair_ref, wide):
    for x in range(8):
        rows = field_ref[x].astype(F32)
        for t in range(16):
            wide[pl.ds(x * 64 + t, 4, stride=16), :] = rows[:, t * 128 : (t + 1) * 128]
    pair_ref[...] = wide[...].reshape(PIECE).astype(BF)


def from_pairs(wide, field_ref, layers):
    for n, x in enumerate(layers):
        parts = [wide[pl.ds(n * 64 + t, 4, stride=16), :] for t in range(16)]
        field_ref[x] = jnp.concatenate(parts, axis=1).astype(BF)


def prepare_field(field):
    def kernel(field_ref, pair_ref, wide):
        to_pairs(field_ref, pair_ref, wide)

    return call(
        kernel, shape(PIECE), [(field, None)], [pltpu.VMEM((512, 128), F32)], 0, 400_000
    )


def prepare_gather(field):
    def kernel(field_ref, out_ref, wide):
        for x in range(8):
            rows = field_ref[x].astype(F32)
            for t in range(16):
                wide[pl.ds(x * 16 + t, 4, stride=128), :] = rows[:, t * 128 : (t + 1) * 128]
        for y in range(4):
            row = wide[y * 128 : y * 128 + 128, :].reshape(8, 16, 128).astype(BF)
            for f in range(8):
                out_ref[f, y] = row

    return call(
        kernel,
        shape((8, 4, 8, 16, 128)),
        [(field, None)],
        [pltpu.VMEM((512, 128), F32)],
        0,
        1_300_000,
    )


def gather_sides(cells, prepared):
    def kernel(cells_ref, prepared_ref, last_ref, first_ref, token_ref, sems):
        token_ref[...] = prepared_ref[...]
        copies = [
            pltpu.make_async_copy(cells_ref.at[:, 3], last_ref, sems.at[0]),
            pltpu.make_async_copy(cells_ref.at[:, 0], first_ref, sems.at[1]),
        ]
        for copy in copies:
            copy.start()
        for copy in copies:
            copy.wait()

    out = shape((8, 8, 16, 128))
    ins = [(cells, pl.ANY), (prepared, None)]
    return call(kernel, (out, out, TOKEN), ins, [pltpu.SemaphoreType.DMA((2,))], 0, 1_000_000)


def gather_edges(coords, cells, y_before, y_after, token):
    def kernel(co, cells_ref, yb, ya, token_ref, near_ref, far_ref):
        def give(last_ref, first_ref):
            for out_ref, x in ((last_ref, 7), (first_ref, 0)):
                for f in range(8):
                    out_ref[f, 0] = yb[f, x]
                    out_ref[f, 5] = ya[f, x]
                    for y in range(4):
                        out_ref[f, y + 1] = cells_ref[f, y, x]

        pl.when(co[2] == 0)(lambda: give(near_ref, far_ref))
        pl.when(co[2] == 1)(lambda: give(far_ref, near_ref))

    out = shape((8, 6, 16, 128))
    ins = [(coords, pltpu.SMEM)] + [(a, None) for a in (cells, y_before, y_after, token)]
    return call(kernel, (out, out), ins, (), 0, 400_000)


def grad_edges(coords, pre_grad, y_before, y_after):
    def kernel(co, pre_ref, yb, ya, near_ref, far_ref):
        for out_ref, x in ((near_ref, 7 - 7 * co[2]), (far_ref, 7 * co[2])):
            out_ref[0] = yb[x]
            out_ref[1:5] = pre_ref[x]
            out_ref[5] = ya[x]

    out = shape((6, 16, 128))
    ins = [(coords, pltpu.SMEM)] + [(a, None) for a in (pre_grad, y_before, y_after)]
    return call(kernel, (out, out), ins, (), 0, 0)


def prepare_weights(weights):
    def kernel(w_ref, fore_ref, back_out, done_ref, tall, even, odd, back_ref, sems):
        def spread(t, carry):
            lanes = pl.ds(pl.multiple_of(t * 128, 128), 128)
            tall[pl.ds(t, 27, stride=256), :] = w_ref[:, lanes].astype(F32)
            return carry

        lax.fori_loop(0, 256, spread, 0, unroll=8)

        def place(ij, carry):
            taps = [tall[pl.ds(pl.multiple_of((ij * 3 + k) * 256, 256), 256), :] for k in range(3)]
            zero = jnp.zeros((256, 64), F32)
            for par in range(2):
                lanes = slice(par * 64, par * 64 + 64)
                even[pl.ds(par, 256, stride=2), :] = jnp.concatenate(
                    [taps[0][:, lanes], taps[1][:, lanes]], axis=1
                )
                odd[pl.ds(par, 256, stride=2), :] = jnp.concatenate([taps[2][:, lanes], zero], axis=1)
            fore_ref[ij, :, 0:128] = even[...].astype(BF)
            fore_ref[ij, :, 128:256] = odd[...].astype(BF)
            for c in range(4):
                rows = slice(c * 128, c * 128 + 128)
                back_ref[ij, 0:128, rows] = even[rows, :].T.astype(BF)
                back_ref[ij, 128:256, rows] = odd[rows, :].T.astype(BF)
            copy_out(ij).start()
            return carry

        def copy_out(ij):
            return pltpu.make_async_copy(back_ref.at[ij], back_out.at[ij], sems.at[ij])

        def finish(ij, carry):
            copy_out(ij).wait()
            return carry

        lax.fori_loop(0, 9, place, 0)
        lax.fori_loop(0, 9, finish, 0)
        done_ref[...] = even[0:8, :]

    return call(
        kernel,
        (shape((9, 512, 256)), pltpu.HBM((9, 256, 512), BF), TOKEN),
        [(weights, None)],
        [
            pltpu.VMEM((27 * 256, 128), F32),
            pltpu.VMEM((512, 128), F32),
            pltpu.VMEM((512, 128), F32),
            pltpu.VMEM((9, 256, 512), BF),
            pltpu.SemaphoreType.DMA((9,)),
        ],
        0,
        8_000_000,
    )


def masked(v, inside):
    return jnp.where(inside, v, jnp.zeros_like(v))


def place_cell(field_ref, x, y, take):
    for q in range(4):
        a, b = take(2 * q), take(2 * q + 1)
        lanes = slice(q * 128, q * 128 + 128)
        field_ref[x, y * 32 : y * 32 + 16, lanes] = jnp.concatenate([a[:, :64], b[:, :64]], axis=1)
        field_ref[x, y * 32 + 16 : y * 32 + 32, lanes] = jnp.concatenate([a[:, 64:], b[:, 64:]], axis=1)


def convolved(rows, fore_ref):
    acc = jnp.zeros((256, 256), F32)
    for i in range(3):
        for j in range(3):
            acc = acc + jnp.dot(
                jnp.concatenate([rows(u, i, j * 32) for u in range(2)], axis=0),
                fore_ref[i * 3 + j],
                preferred_element_type=F32,
            )
    return acc


def finish_cell(total, start, grad):
    even, odd = total[pl.ds(start, 16), :], total[pl.ds(start + 16, 16), :]
    pre = (
        jnp.concatenate([down(odd[:, 0:64]), even[:, 0:64]], axis=1)
        + jnp.concatenate([even[:, 64:128], odd[:, 64:128]], axis=1)
        + jnp.concatenate([odd[:, 128:192], up(even[:, 128:192])], axis=1)
    )
    e = jnp.exp(-jnp.abs(pre))
    soft = jnp.maximum(pre, 0.0) + jnp.log1p(e)
    slope = jnp.where(pre >= 0, 1.0, e) / (1.0 + e)
    value = LEAK * pre + (1.0 - LEAK) * (soft - math.log(2.0))
    return value, (grad.astype(F32) * (LEAK + (1.0 - LEAK) * slope)).astype(BF)


def forward_own(cells, fore, token):
    def kernel(cells_ref, fore_ref, token_ref, field_ref, total_ref, done_ref):
        def place(x, carry):
            field_ref[x, 0:32, :] = jnp.zeros((32, 512), BF)
            field_ref[x, 160:192, :] = jnp.zeros((32, 512), BF)
            for y in range(4):
                place_cell(field_ref, x, y + 1, lambda f: cells_ref[f, y, x])
            return carry

        lax.fori_loop(0, 8, place, 0)

        def multiply(h, carry):
            start = pl.multiple_of(h * 256, 256)
            total_ref[pl.ds(start, 256), :] = convolved(
                lambda u, i, at: field_ref[2 * h + u + i, at : at + 128, :], fore_ref
            )
            return carry

        lax.fori_loop(0, 3, multiply, 0)
        done_ref[...] = token_ref[...]

    return call(
        kernel,
        (shape((8, 192, 512)), shape((768, 256), F32), TOKEN),
        [(a, None) for a in (cells, fore, token)],
        (),
        4_000_000_000,
        5_000_000,
    )


def forward_inner(coords, field, total, y_before, y_after, fore, grad):
    def kernel(
        co, own_ref, total_ref, yb, ya, fore_ref, grad_ref, field_ref, out_ref, pre_ref, sides, wide
    ):
        y_low, y_high = co[4] > 0, co[4] < 7

        def place(x, carry):
            field_ref[x, 32:160, :] = own_ref[x, 32:160, :]
            place_cell(field_ref, x, 0, lambda f: masked(yb[f, x], y_low))
            place_cell(field_ref, x, 5, lambda f: masked(ya[f, x], y_high))
            return carry

        lax.fori_loop(0, 8, place, 0)

        for side, (at, j, y) in enumerate(((0, 0, 0), (160, 2, 3))):
            acc = jnp.concatenate(
                [total_ref[x * 128 + y * 32 : x * 128 + y * 32 + 32, :] for x in range(6)], axis=0
            )
            for i in range(3):
                rows = [field_ref[x + i, at : at + 32, :] for x in range(6)]
                acc = acc + jnp.dot(
                    jnp.concatenate(rows, axis=0), fore_ref[i * 3 + j], preferred_element_type=F32
                )
            sides[side] = acc

        def finish(x, carry):
            for y in range(4):
                if y in (0, 3):
                    source, start = sides.at[y // 3], pl.multiple_of(x * 32, 32)
                else:
                    source, start = total_ref, pl.multiple_of(x * 128 + y * 32, 32)
                value, turned = finish_cell(source, start, grad_ref[x + 1, y])
                wide[pl.ds(pl.multiple_of(x * 64 + y * 16, 16), 16), :] = value
                pre_ref[x, y] = turned
            return carry

        lax.fori_loop(0, 6, finish, 0)
        from_pairs(wide, out_ref, range(6))

    return call(
        kernel,
        (shape((8, 192, 512)), shape((6, 4, 2048)), shape((6, 4, 16, 128))),
        [(coords, pltpu.SMEM)]
        + [(a, None) for a in (field, total, y_before, y_after, fore, grad)],
        [pltpu.VMEM((2, 192, 256), F32), pltpu.VMEM((384, 128), F32)],
        1_000_000_000,
        6_000_000,
    )


def forward_outer(coords, field, x_near, x_far, fore, grad, out_inner, pre_inner, token):
    def kernel(
        co, field_ref, near_ref, far_ref, fore_ref, grad_ref, out_in, pre_in, token_ref,
        rim_ref, out_ref, pre_ref, first_ref, last_ref, total, wide,
    ):
        y_low, y_high, x_low, x_high = co[4] > 0, co[4] < 7, co[5] > 0, co[5] < 3
        odd = co[2] > 0
        for y in range(6):
            beside = {0: y_low, 5: y_high}.get(y, True)
            place_cell(
                rim_ref,
                0,
                y,
                lambda f: masked(jnp.where(odd, near_ref[f, y], far_ref[f, y]), jnp.logical_and(x_low, beside)),
            )
            place_cell(
                rim_ref,
                1,
                y,
                lambda f: masked(jnp.where(odd, far_ref[f, y], near_ref[f, y]), jnp.logical_and(x_high, beside)),
            )

        def rows(u, i, at):
            if u == 0:
                return (field_ref[i - 1] if i else rim_ref[0])[at : at + 128, :]
            return (field_ref[6 + i] if i < 2 else rim_ref[1])[at : at + 128, :]

        total[...] = convolved(rows, fore_ref)
        for n, x in enumerate((0, 7)):
            for y in range(4):
                value, turned = finish_cell(total, n * 128 + y * 32, grad_ref[x, y])
                wide[n * 64 + y * 16 : n * 64 + y * 16 + 16, :] = value
                pre_ref[x, y] = turned
        from_pairs(wide, out_ref, (0, 7))
        out_ref[1:7] = out_in[...]
        pre_ref[1:7] = pre_in[...]
        for x in range(8):
            first_ref[x] = pre_ref[x, 0]
            last_ref[x] = pre_ref[x, 3]

    return call(
        kernel,
        (
            shape((2, 192, 512)),
            shape((8, 4, 2048)),
            shape(PIECE),
            shape((8, 16, 128)),
            shape((8, 16, 128)),
        ),
        [(coords, pltpu.SMEM)]
        + [(a, None) for a in (field, x_near, x_far, fore, grad, out_inner, pre_inner, token)],
        [pltpu.VMEM((256, 256), F32), pltpu.VMEM((128, 128), F32)],
        2_000_000_000,
        6_000_000,
    )


def stacked_depth(v):
    even, odd = v[:, :64], v[:, 64:]
    zero = jnp.zeros((16, 64), F32)
    return (
        (jnp.concatenate([odd, even], axis=1), jnp.concatenate([down(odd), zero], axis=1)),
        (jnp.concatenate([up(even), odd], axis=1), jnp.concatenate([even, zero], axis=1)),
    )


def turn_grad(pre_ref, layers, first, second, turned):
    for n, x in enumerate(layers):
        for y in range(4):
            low, high = stacked_depth(pre_ref[x, y].astype(F32))
            first[y * 32 : y * 32 + 16, :] = low[0]
            second[y * 32 : y * 32 + 16, :] = low[1]
            first[y * 32 + 16 : y * 32 + 32, :] = high[0]
            second[y * 32 + 16 : y * 32 + 32, :] = high[1]
        turned[0:128, n * 128 : n * 128 + 128] = first[...].T.astype(BF)
        turned[128:192, n * 128 : n * 128 + 128] = second[...].T[0:64].astype(BF)


def filter_grad_inner(field, pre_inner):
    def kernel(field_ref, pre_ref, part_ref, done_ref, first, second, turned):
        turn_grad(pre_ref, range(6), first, second, turned)

        def multiply(j, carry):
            rows = pl.ds(pl.multiple_of(j * 32, 32), 128)
            for i in range(3):
                for half in range(2):
                    lanes = slice(half * 256, half * 256 + 256)
                    cells = [field_ref[x + i, rows, lanes] for x in range(6)]
                    got = jnp.dot(
                        turned[...], jnp.concatenate(cells, axis=0), preferred_element_type=F32
                    )
                    part_ref[i * 3 + j, :, lanes] = got.astype(part_ref.dtype)
            return carry

        lax.fori_loop(0, 3, multiply, 0)
        done_ref[...] = first[0:8, :]

    return call(
        kernel,
        (shape((9, 192, 512)), TOKEN),
        [(field, None), (pre_inner, None)],
        [pltpu.VMEM((128, 128), F32), pltpu.VMEM((128, 128), F32), pltpu.VMEM((192, 768), BF)],
        3_000_000_000,
        0,
    )


def filter_grad(coords, field, rim, pre_grad, part):
    def kernel(co, field_ref, rim_ref, pre_ref, part_ref, keep_ref, send_ref, first, second, turned):
        core = co[2]
        turn_grad(pre_ref, (0, 7), first, second, turned)

        def multiply(j, carry):
            rows = pl.ds(pl.multiple_of(j * 32, 32), 128)
            for i in range(3):
                for half in range(2):
                    lanes = slice(half * 256, half * 256 + 256)
                    low = field_ref[i - 1, rows, lanes] if i else rim_ref[0, rows, lanes]
                    high = field_ref[6 + i, rows, lanes] if i < 2 else rim_ref[1, rows, lanes]
                    got = jnp.dot(
                        turned[...], jnp.concatenate([low, high], axis=0), preferred_element_type=F32
                    )
                    got = (got + part_ref[i * 3 + j, :, lanes].astype(F32)) * SCALE
                    left, right = got[:, :128], got[:, 128:]
                    keep_ref[half, i * 3 + j] = jnp.where(core == 0, left, right)
                    send_ref[half, i * 3 + j] = jnp.where(core == 0, right, left).astype(BF)
            return carry

        lax.fori_loop(0, 3, multiply, 0)

    return call(
        kernel,
        (shape((2, 9, 192, 128), F32), shape((2, 9, 192, 128))),
        [(coords, pltpu.SMEM)] + [(a, None) for a in (field, rim, pre_grad, part)],
        [pltpu.VMEM((128, 128), F32), pltpu.VMEM((128, 128), F32), pltpu.VMEM((192, 256), BF)],
        COST[3],
        0,
    )


def add_cores(coords, keep, got):
    def kernel(co, keep_ref, got_ref, stay_ref, send_ref):
        far = co[3]
        stay_ref[...] = keep_ref[far] + got_ref[far].astype(F32)
        send_ref[...] = (keep_ref[1 - far] + got_ref[1 - far].astype(F32)).astype(BF)

    return call(
        kernel,
        (shape((9, 192, 128), F32), shape((9, 192, 128))),
        [(coords, pltpu.SMEM), (keep, None), (got, None)],
        (),
        COST[0],
        4_000_000,
    )


def add_far(coords, stay, got):
    def kernel(co, stay_ref, got_ref, keep_ref, send_ref, total, turned):
        parity = co[4] & 1
        total[...] = (stay_ref[...] + got_ref[...].astype(F32)).reshape(1728, 128)
        for t in range(14):
            width = min(128, 1728 - t * 128)
            block = total[t * 128 : t * 128 + width, :].T.reshape(8, 16, width)
            turned[:, :, t * 128 : t * 128 + width] = block
        for m in range(4):
            keep_ref[m] = turned[2 * m + parity]
            send_ref[m] = turned[2 * m + 1 - parity].astype(BF)

    return call(
        kernel,
        (shape((4, 16, 1728), F32), shape((4, 16, 1728))),
        [(coords, pltpu.SMEM), (stay, None), (got, None)],
        [pltpu.VMEM((1728, 128), F32), pltpu.VMEM((8, 16, 1728), F32)],
        COST[6],
        2_000_000,
    )


def add_near(coords, keep, got):
    def kernel(co, keep_ref, got_ref, *outs):
        own = co[4] // 2
        for d in range(4):
            at = (own + d) & 3
            outs[d][...] = (keep_ref[at] + got_ref[at].astype(F32)).astype(outs[d].dtype)

    return call(
        kernel,
        (shape((16, 1728), F32),) + (shape((16, 1728)),) * 3,
        [(coords, pltpu.SMEM), (keep, None), (got, None)],
        (),
        COST[5],
        1_000_000,
    )


def last_sums(regions, parts):
    def kernel(r0, r1, r2, r3, parts_ref, filter_ref, input_ref, total, pairs, wide):
        s = parts_ref[0].astype(F32)
        for f in range(1, 8):
            s = s + parts_ref[f].astype(F32)
        wide[...] = s.reshape(512, 128)
        from_pairs(wide, input_ref, range(8))
        for t in range(14):
            width = min(128, 1728 - t * 128)
            lanes = slice(t * 128, t * 128 + width)
            s = r0[:, lanes].astype(F32)
            for ref in (r1, r2, r3):
                s = s + ref[:, lanes].astype(F32)
            total[:, 0:width] = s
            even, odd = total[pl.ds(0, 8, stride=2), :], total[pl.ds(1, 8, stride=2), :]
            for u in range(width // 64):
                pick = slice(u * 64, u * 64 + 64)
                at = (2 * t + u) * 8
                pairs[at : at + 8, :] = jnp.concatenate([even[:, pick], odd[:, pick]], axis=1)
        filter_ref[...] = pairs[...].reshape(27, 8, 128)

    return call(
        kernel,
        (shape((27, 8, 128), F32), shape((8, 4, 2048))),
        [(part, None) for part in regions] + [(parts, None)],
        [pltpu.VMEM((16, 128), F32), pltpu.VMEM((216, 128), F32), pltpu.VMEM((512, 128), F32)],
        COST[4],
        1_800_000,
    )


def place_grad(rim, x, y, v):
    low, high = stacked_depth(v.astype(F32))
    for half in range(2):
        lanes = slice(half * 128, half * 128 + 128)
        rim[x, y * 32 : y * 32 + 16, lanes] = low[half].astype(BF)
        rim[x, y * 32 + 16 : y * 32 + 32, lanes] = high[half].astype(BF)


def input_layers(rows, back_ref, total, store):
    for n in range(2):
        lanes = slice(n * 256, n * 256 + 256)
        acc = jnp.zeros((256, 256), F32)
        for i in range(3):
            for j in range(3):
                acc = acc + jnp.dot(
                    jnp.concatenate([rows(u, 2 - i, (2 - j) * 32) for u in range(2)], axis=0),
                    back_ref[i * 3 + j, :, lanes],
                    preferred_element_type=F32,
                )
        total[:, lanes] = acc
    for u in range(2):
        for y in range(4):
            at = u * 128 + y * 32
            for f in range(8):
                lanes = slice(f * 64, f * 64 + 64)
                pair = jnp.concatenate([total[at : at + 16, lanes], total[at + 16 : at + 32, lanes]], axis=1)
                store(f, u, y, pair.astype(BF))


def input_grad_inner(coords, pre_grad, y_before, y_after, back):
    def kernel(co, pre_ref, yb, ya, back_ref, out_ref, rim, total):
        y_low, y_high = co[4] > 0, co[4] < 7

        def place(x, carry):
            place_grad(rim, x, 0, masked(yb[x], y_low))
            place_grad(rim, x, 5, masked(ya[x], y_high))
            for y in range(4):
                place_grad(rim, x, y + 1, pre_ref[x, y])
            return carry

        lax.fori_loop(0, 8, place, 0)

        def multiply(h, carry):
            def store(f, u, y, block):
                out_ref[f, 2 * h + u, y] = block

            input_layers(lambda u, d, at: rim[2 * h + u + d, at : at + 128, :], back_ref, total, store)
            return carry

        lax.fori_loop(0, 3, multiply, 0)

    return call(
        kernel,
        shape((8, 6, 4, 16, 128)),
        [(coords, pltpu.SMEM)] + [(a, None) for a in (pre_grad, y_before, y_after, back)],
        [pltpu.VMEM((8, 192, 256), BF), pltpu.VMEM((256, 512), F32)],
        COST[1],
        0,
    )


def input_grad_outer(coords, pre_grad, y_before, y_after, x_near, x_far, back, inner):
    def kernel(co, pre_ref, yb, ya, near_ref, far_ref, back_ref, inner_ref, out_ref, rim, total):
        y_low, y_high, x_low, x_high = co[4] > 0, co[4] < 7, co[5] > 0, co[5] < 3
        odd = co[2] > 0
        for y in range(6):
            beside = {0: y_low, 5: y_high}.get(y, True)
            near, far = near_ref[y], far_ref[y]
            before, after = jnp.where(odd, near, far), jnp.where(odd, far, near)
            place_grad(rim, 0, y, masked(before, jnp.logical_and(x_low, beside)))
            place_grad(rim, 5, y, masked(after, jnp.logical_and(x_high, beside)))
        for at, x in ((1, 0), (2, 1), (3, 6), (4, 7)):
            place_grad(rim, at, 0, masked(yb[x], y_low))
            place_grad(rim, at, 5, masked(ya[x], y_high))
            for y in range(4):
                place_grad(rim, at, y + 1, pre_ref[x, y])

        def store(f, u, y, block):
            out_ref[f, 7 * u, y] = block

        input_layers(lambda u, d, at: rim[3 * u + d, at : at + 128, :], back_ref, total, store)
        for f in range(8):
            out_ref[f, 1:7] = inner_ref[f]

    return call(
        kernel,
        shape((8,) + PIECE),
        [(coords, pltpu.SMEM)]
        + [(a, None) for a in (pre_grad, y_before, y_after, x_near, x_far, back, inner)],
        [pltpu.VMEM((6, 192, 256), BF), pltpu.VMEM((256, 512), F32)],
        COST[2],
        0,
    )


def both_ways(last, first, axis, size):
    return (
        lax.ppermute(last, axis, [(i, (i + 1) % size) for i in range(size)]),
        lax.ppermute(first, axis, [((i + 1) % size, i) for i in range(size)]),
    )


def x_rims(near, far):
    return (
        lax.ppermute(near, "sx", [(i, i ^ 1) for i in range(4)]),
        lax.ppermute(far, "sx", [(1, 2), (2, 1)]),
    )


def exchange(parts, axis):
    return lax.all_to_all(parts, axis, 0, 0)


def per_device(activations, weights, out_grad):
    filt, sx, sy = (lax.axis_index(a) for a in ("filt", "sx", "sy"))
    coords = jnp.stack([filt // 4, filt % 4, sx % 2, sx // 2, sy, sx, 0, 0]).astype(jnp.int32)
    cells = prepare_gather(activations[0, 0])
    cells, weights, out_grad = lax.optimization_barrier((cells, weights, out_grad))
    cells = exchange(cells, "filt")
    fore, back, prepared = prepare_weights(weights[0])
    grad = prepare_field(out_grad[0, 0])
    last, first, token = gather_sides(cells, prepared)
    y_before, y_after = both_ways(last, first, "sy", 8)
    field, total, token = forward_own(cells, fore, token)
    near, far = gather_edges(coords, cells, y_before, y_after, token)
    near, far, total = lax.optimization_barrier((near, far, total))
    x_near, x_far = x_rims(near, far)
    field, out_inner, pre_inner = forward_inner(coords, field, total, y_before, y_after, fore, grad)
    part, token = filter_grad_inner(field, pre_inner)
    rim, outputs, pre_grad, g_first, g_last = forward_outer(
        coords, field, x_near, x_far, fore, grad, out_inner, pre_inner, token
    )

    gy_before, gy_after = both_ways(g_last, g_first, "sy", 8)
    keep, send = filter_grad(coords, field, rim, pre_grad, part)
    got = lax.ppermute(send, "sx", [(i, i ^ 1) for i in range(4)])
    stay, send = add_cores(coords, keep, got)
    stay, pre_grad, gy_before, gy_after = lax.optimization_barrier((stay, pre_grad, gy_before, gy_after))
    got = lax.ppermute(send, "sx", [(i, i ^ 2) for i in range(4)])
    gx_near, gx_far = x_rims(*grad_edges(coords, pre_grad, gy_before, gy_after))

    inner = input_grad_inner(coords, pre_grad, gy_before, gy_after, back)
    parts = input_grad_outer(coords, pre_grad, gy_before, gy_after, gx_near, gx_far, back, inner)
    parts, got = lax.optimization_barrier((parts, got))
    parts = exchange(parts, "filt")
    keep, send = add_far(coords, stay, got)
    got = lax.ppermute(send, "sy", [(i, i ^ 1) for i in range(8)])
    regions = list(add_near(coords, keep, got))
    for d in (2, 1, 3):
        regions[d] = lax.ppermute(regions[d], "sy", [(i, (i + 2 * d) % 8) for i in range(8)])
    weight_grad, input_grad = last_sums(regions, parts)
    return outputs[None, None], input_grad[None, None], weight_grad.reshape(1, 27, 1024)


def solution(mesh):
    in_specs = (
        P("filt", None, "sx", "sy", None),
        P("filt", None, None),
        P("filt", None, "sx", "sy", None),
    )
    out_specs = (
        P("filt", None, "sx", "sy", None),
        P("filt", None, "sx", "sy", None),
        P("filt", None, ("sx", "sy")),
    )
    return jax.shard_map(
        per_device, mesh=mesh, in_specs=in_specs, out_specs=out_specs, check_vma=False
    )
```

```python
import math

import jax
import jax.numpy as jnp
from jax import lax
from jax.experimental import pallas as pl
from jax.experimental.pallas import tpu as pltpu
from jax.sharding import PartitionSpec as P

BF = jnp.bfloat16
F32 = jnp.float32
LEAK = 0.2
SCALE = 1.0 / math.sqrt(32768.0)
URGENT = 20_000_000_000
COST = [20000000000, 4000000000, 500000000, 5000000000, 0, 20000000000, 20000000000]
PIECE = (8, 4, 16, 128)


def call(kernel, outs, ins, scratch=(), flops=0, nbytes=0):
    return pl.pallas_call(
        kernel,
        out_shape=outs,
        in_specs=[
            pl.BlockSpec(memory_space=pltpu.VMEM if space is None else space)
            for _, space in ins
        ],
        out_specs=jax.tree.map(
            lambda out: pl.BlockSpec(
                memory_space=pltpu.VMEM if isinstance(out, jax.ShapeDtypeStruct) else pl.ANY
            ),
            outs,
        ),
        scratch_shapes=list(scratch),
        compiler_params=pltpu.CompilerParams(vmem_limit_bytes=14 << 20),
        cost_estimate=pl.CostEstimate(flops=flops, bytes_accessed=nbytes, transcendentals=0),
    )(*[array for array, _ in ins])


def shape(dims, dtype=BF):
    return jax.ShapeDtypeStruct(dims, dtype)


TOKEN = shape((8, 128), F32)


def down(v):
    rows = lax.broadcasted_iota(jnp.int32, v.shape, 0)
    return jnp.where(rows == 0, 0.0, pltpu.roll(v, 1, 0))


def up(v):
    rows = lax.broadcasted_iota(jnp.int32, v.shape, 0)
    return jnp.where(rows == v.shape[0] - 1, 0.0, pltpu.roll(v, v.shape[0] - 1, 0))


def to_pairs(field_ref, pair_ref, wide):
    for x in range(8):
        rows = field_ref[x].astype(F32)
        for t in range(16):
            wide[pl.ds(x * 64 + t, 4, stride=16), :] = rows[:, t * 128 : (t + 1) * 128]
    pair_ref[...] = wide[0:512, :].reshape(PIECE).astype(BF)


def from_pairs(wide, field_ref, layers):
    for n, x in enumerate(layers):
        parts = [wide[pl.ds(n * 64 + t, 4, stride=16), :] for t in range(16)]
        field_ref[x] = jnp.concatenate(parts, axis=1).astype(BF)


def prepare_field(field):
    def kernel(field_ref, pair_ref, wide):
        to_pairs(field_ref, pair_ref, wide)

    return call(
        kernel, shape(PIECE), [(field, None)], [pltpu.VMEM((576, 128), F32)], 0, 400_000
    )


def prepare_gather(field):
    def kernel(field_ref, out_ref, wide):
        for x in range(8):
            rows = field_ref[x].astype(F32)
            for t in range(16):
                wide[pl.ds(x * 16 + t, 4, stride=128), :] = rows[:, t * 128 : (t + 1) * 128]
        for y in range(4):
            row = wide[y * 128 : y * 128 + 128, :].reshape(8, 16, 128).astype(BF)
            for f in range(8):
                out_ref[f, y] = row

    return call(
        kernel,
        shape((8, 4, 8, 16, 128)),
        [(field, None)],
        [pltpu.VMEM((1024, 128), F32)],
        0,
        1_300_000,
    )


def gather_sides(cells, prepared):
    def kernel(cells_ref, prepared_ref, last_ref, first_ref, token_ref, sems):
        token_ref[...] = prepared_ref[...]
        copies = [
            pltpu.make_async_copy(cells_ref.at[:, 3], last_ref, sems.at[0]),
            pltpu.make_async_copy(cells_ref.at[:, 0], first_ref, sems.at[1]),
        ]
        for copy in copies:
            copy.start()
        for copy in copies:
            copy.wait()

    out = shape((8, 8, 16, 128))
    ins = [(cells, pl.ANY), (prepared, None)]
    return call(kernel, (out, out, TOKEN), ins, [pltpu.SemaphoreType.DMA((2,))], 0, 1_000_000)


def gather_edges(coords, cells, y_before, y_after, token):
    def kernel(co, cells_ref, yb, ya, token_ref, near_ref, far_ref):
        def give(last_ref, first_ref):
            for out_ref, x in ((last_ref, 7), (first_ref, 0)):
                for f in range(8):
                    out_ref[f, 0] = yb[f, x]
                    out_ref[f, 5] = ya[f, x]
                    for y in range(4):
                        out_ref[f, y + 1] = cells_ref[f, y, x]

        pl.when(co[2] == 0)(lambda: give(near_ref, far_ref))
        pl.when(co[2] == 1)(lambda: give(far_ref, near_ref))

    out = shape((8, 6, 16, 128))
    ins = [(coords, pltpu.SMEM)] + [(a, None) for a in (cells, y_before, y_after, token)]
    return call(kernel, (out, out), ins, (), 0, 400_000)


def grad_edges(coords, pre_grad, y_before, y_after):
    def kernel(co, pre_ref, yb, ya, near_ref, far_ref):
        for out_ref, x in ((near_ref, 7 - 7 * co[2]), (far_ref, 7 * co[2])):
            out_ref[0] = yb[x]
            out_ref[1:5] = pre_ref[x]
            out_ref[5] = ya[x]

    out = shape((6, 16, 128))
    ins = [(coords, pltpu.SMEM)] + [(a, None) for a in (pre_grad, y_before, y_after)]
    return call(kernel, (out, out), ins, (), 0, 0)


def prepare_weights(weights):
    def kernel(w_ref, fore_ref, back_out, done_ref, tall, even, odd, back_ref, sems):
        def spread(t, carry):
            lanes = pl.ds(pl.multiple_of(t * 128, 128), 128)
            tall[pl.ds(t, 27, stride=256), :] = w_ref[:, lanes].astype(F32)
            return carry

        lax.fori_loop(0, 256, spread, 0, unroll=8)

        def place(ij, carry):
            taps = [tall[pl.ds(pl.multiple_of((ij * 3 + k) * 256, 256), 256), :] for k in range(3)]
            zero = jnp.zeros((256, 64), F32)
            for par in range(2):
                lanes = slice(par * 64, par * 64 + 64)
                even[pl.ds(par, 256, stride=2), :] = jnp.concatenate(
                    [taps[0][:, lanes], taps[1][:, lanes]], axis=1
                )
                odd[pl.ds(par, 256, stride=2), :] = jnp.concatenate([taps[2][:, lanes], zero], axis=1)
            fore_ref[ij, :, 0:128] = even[...].astype(BF)
            fore_ref[ij, :, 128:256] = odd[...].astype(BF)
            for c in range(4):
                rows = slice(c * 128, c * 128 + 128)
                back_ref[ij, 0:128, rows] = even[rows, :].T.astype(BF)
                back_ref[ij, 128:256, rows] = odd[rows, :].T.astype(BF)
            copy_out(ij).start()
            return carry

        def copy_out(ij):
            return pltpu.make_async_copy(back_ref.at[ij], back_out.at[ij], sems.at[ij])

        def finish(ij, carry):
            copy_out(ij).wait()
            return carry

        lax.fori_loop(0, 9, place, 0)
        lax.fori_loop(0, 9, finish, 0)
        done_ref[...] = even[0:8, :]

    return call(
        kernel,
        (shape((9, 512, 256)), pltpu.HBM((9, 256, 512), BF), TOKEN),
        [(weights, None)],
        [
            pltpu.VMEM((32 * 256, 128), F32),
            pltpu.VMEM((512, 128), F32),
            pltpu.VMEM((512, 128), F32),
            pltpu.VMEM((9, 256, 512), BF),
            pltpu.SemaphoreType.DMA((9,)),
        ],
        0,
        8_000_000,
    )


def masked(v, inside):
    return jnp.where(inside, v, jnp.zeros_like(v))


def place_cell(field_ref, x, y, take):
    for q in range(4):
        a, b = take(2 * q), take(2 * q + 1)
        lanes = slice(q * 128, q * 128 + 128)
        field_ref[x, y * 32 : y * 32 + 16, lanes] = jnp.concatenate([a[:, :64], b[:, :64]], axis=1)
        field_ref[x, y * 32 + 16 : y * 32 + 32, lanes] = jnp.concatenate([a[:, 64:], b[:, 64:]], axis=1)


def convolved(rows, fore_ref):
    acc = jnp.zeros((256, 256), F32)
    for i in range(3):
        for j in range(3):
            acc = acc + jnp.dot(
                jnp.concatenate([rows(u, i, j * 32) for u in range(2)], axis=0),
                fore_ref[i * 3 + j],
                preferred_element_type=F32,
            )
    return acc


def finish_cell(total, start, grad):
    even, odd = total[pl.ds(start, 16), :], total[pl.ds(start + 16, 16), :]
    pre = (
        jnp.concatenate([down(odd[:, 0:64]), even[:, 0:64]], axis=1)
        + jnp.concatenate([even[:, 64:128], odd[:, 64:128]], axis=1)
        + jnp.concatenate([odd[:, 128:192], up(even[:, 128:192])], axis=1)
    )
    e = jnp.exp(-jnp.abs(pre))
    soft = jnp.maximum(pre, 0.0) + jnp.log1p(e)
    slope = jnp.where(pre >= 0, 1.0, e) / (1.0 + e)
    value = LEAK * pre + (1.0 - LEAK) * (soft - math.log(2.0))
    return value, (grad.astype(F32) * (LEAK + (1.0 - LEAK) * slope)).astype(BF)


def forward_own(cells, fore, token):
    def kernel(cells_ref, fore_ref, token_ref, field_ref, total_ref, done_ref):
        def place(x, carry):
            field_ref[x, 0:32, :] = jnp.zeros((32, 512), BF)
            field_ref[x, 160:192, :] = jnp.zeros((32, 512), BF)
            for y in range(4):
                place_cell(field_ref, x, y + 1, lambda f: cells_ref[f, y, x])
            return carry

        lax.fori_loop(0, 8, place, 0)

        def multiply(h, carry):
            start = pl.multiple_of(h * 256, 256)
            total_ref[pl.ds(start, 256), :] = convolved(
                lambda u, i, at: field_ref[2 * h + u + i, at : at + 128, :], fore_ref
            )
            return carry

        lax.fori_loop(0, 3, multiply, 0)
        done_ref[...] = token_ref[...]

    return call(
        kernel,
        (shape((8, 192, 512)), shape((768, 256), F32), TOKEN),
        [(a, None) for a in (cells, fore, token)],
        (),
        4_000_000_000,
        5_000_000,
    )


def forward_inner(coords, field, total, y_before, y_after, fore, grad):
    def kernel(
        co, own_ref, total_ref, yb, ya, fore_ref, grad_ref, field_ref, out_ref, pre_ref, sides, wide
    ):
        y_low, y_high = co[4] > 0, co[4] < 7

        def place(x, carry):
            field_ref[x, 32:160, :] = own_ref[x, 32:160, :]
            place_cell(field_ref, x, 0, lambda f: masked(yb[f, x], y_low))
            place_cell(field_ref, x, 5, lambda f: masked(ya[f, x], y_high))
            return carry

        lax.fori_loop(0, 8, place, 0)

        for side, (at, j, y) in enumerate(((0, 0, 0), (160, 2, 3))):
            acc = jnp.concatenate(
                [total_ref[x * 128 + y * 32 : x * 128 + y * 32 + 32, :] for x in range(6)], axis=0
            )
            for i in range(3):
                rows = [field_ref[x + i, at : at + 32, :] for x in range(6)]
                acc = acc + jnp.dot(
                    jnp.concatenate(rows, axis=0), fore_ref[i * 3 + j], preferred_element_type=F32
                )
            sides[side] = acc

        def finish(x, carry):
            for y in range(4):
                if y in (0, 3):
                    source, start = sides.at[y // 3], pl.multiple_of(x * 32, 32)
                else:
                    source, start = total_ref, pl.multiple_of(x * 128 + y * 32, 32)
                value, turned = finish_cell(source, start, grad_ref[x + 1, y])
                wide[pl.ds(pl.multiple_of(x * 64 + y * 16, 16), 16), :] = value
                pre_ref[x, y] = turned
            return carry

        lax.fori_loop(0, 6, finish, 0)
        from_pairs(wide, out_ref, range(6))

    return call(
        kernel,
        (shape((8, 192, 512)), shape((6, 4, 2048)), shape((6, 4, 16, 128))),
        [(coords, pltpu.SMEM)]
        + [(a, None) for a in (field, total, y_before, y_after, fore, grad)],
        [pltpu.VMEM((2, 192, 256), F32), pltpu.VMEM((448, 128), F32)],
        1_000_000_000,
        6_000_000,
    )


def forward_outer(coords, field, x_near, x_far, fore, grad, out_inner, pre_inner, token):
    def kernel(
        co, field_ref, near_ref, far_ref, fore_ref, grad_ref, out_in, pre_in, token_ref,
        rim_ref, out_ref, pre_ref, first_ref, last_ref, total, wide,
    ):
        y_low, y_high, x_low, x_high = co[4] > 0, co[4] < 7, co[5] > 0, co[5] < 3
        odd = co[2] > 0
        for y in range(6):
            beside = {0: y_low, 5: y_high}.get(y, True)
            place_cell(
                rim_ref,
                0,
                y,
                lambda f: masked(jnp.where(odd, near_ref[f, y], far_ref[f, y]), jnp.logical_and(x_low, beside)),
            )
            place_cell(
                rim_ref,
                1,
                y,
                lambda f: masked(jnp.where(odd, far_ref[f, y], near_ref[f, y]), jnp.logical_and(x_high, beside)),
            )

        def rows(u, i, at):
            if u == 0:
                return (field_ref[i - 1] if i else rim_ref[0])[at : at + 128, :]
            return (field_ref[6 + i] if i < 2 else rim_ref[1])[at : at + 128, :]

        total[...] = convolved(rows, fore_ref)
        for n, x in enumerate((0, 7)):
            for y in range(4):
                value, turned = finish_cell(total, n * 128 + y * 32, grad_ref[x, y])
                wide[n * 64 + y * 16 : n * 64 + y * 16 + 16, :] = value
                pre_ref[x, y] = turned
        from_pairs(wide, out_ref, (0, 7))
        out_ref[1:7] = out_in[...]
        pre_ref[1:7] = pre_in[...]
        for x in range(8):
            first_ref[x] = pre_ref[x, 0]
            last_ref[x] = pre_ref[x, 3]

    return call(
        kernel,
        (
            shape((2, 192, 512)),
            shape((8, 4, 2048)),
            shape(PIECE),
            shape((8, 16, 128)),
            shape((8, 16, 128)),
        ),
        [(coords, pltpu.SMEM)]
        + [(a, None) for a in (field, x_near, x_far, fore, grad, out_inner, pre_inner, token)],
        [pltpu.VMEM((256, 256), F32), pltpu.VMEM((192, 128), F32)],
        2_000_000_000,
        6_000_000,
    )


def stacked_depth(v):
    even, odd = v[:, :64], v[:, 64:]
    zero = jnp.zeros((16, 64), F32)
    return (
        (jnp.concatenate([odd, even], axis=1), jnp.concatenate([down(odd), zero], axis=1)),
        (jnp.concatenate([up(even), odd], axis=1), jnp.concatenate([even, zero], axis=1)),
    )


def turn_grad(pre_ref, layers, first, second, turned):
    for n, x in enumerate(layers):
        for y in range(4):
            low, high = stacked_depth(pre_ref[x, y].astype(F32))
            first[y * 32 : y * 32 + 16, :] = low[0]
            second[y * 32 : y * 32 + 16, :] = low[1]
            first[y * 32 + 16 : y * 32 + 32, :] = high[0]
            second[y * 32 + 16 : y * 32 + 32, :] = high[1]
        turned[0:128, n * 128 : n * 128 + 128] = first[...].T.astype(BF)
        turned[128:192, n * 128 : n * 128 + 128] = second[...].T[0:64].astype(BF)


def filter_grad_inner(field, pre_inner):
    def kernel(field_ref, pre_ref, part_ref, done_ref, first, second, turned):
        turn_grad(pre_ref, range(6), first, second, turned)

        def multiply(j, carry):
            rows = pl.ds(pl.multiple_of(j * 32, 32), 128)
            for i in range(3):
                for half in range(2):
                    lanes = slice(half * 256, half * 256 + 256)
                    cells = [field_ref[x + i, rows, lanes] for x in range(6)]
                    got = jnp.dot(
                        turned[...], jnp.concatenate(cells, axis=0), preferred_element_type=F32
                    )
                    part_ref[i * 3 + j, :, lanes] = got.astype(part_ref.dtype)
            return carry

        lax.fori_loop(0, 3, multiply, 0)
        done_ref[...] = first[0:8, :]

    return call(
        kernel,
        (shape((9, 192, 512)), TOKEN),
        [(field, None), (pre_inner, None)],
        [pltpu.VMEM((128, 128), F32), pltpu.VMEM((128, 128), F32), pltpu.VMEM((192, 768), BF)],
        3_000_000_000,
        0,
    )


def filter_grad(coords, field, rim, pre_grad, part):
    def kernel(co, field_ref, rim_ref, pre_ref, part_ref, keep_ref, send_ref, first, second, turned):
        core = co[2]
        turn_grad(pre_ref, (0, 7), first, second, turned)

        def multiply(j, carry):
            rows = pl.ds(pl.multiple_of(j * 32, 32), 128)
            for i in range(3):
                for half in range(2):
                    lanes = slice(half * 256, half * 256 + 256)
                    low = field_ref[i - 1, rows, lanes] if i else rim_ref[0, rows, lanes]
                    high = field_ref[6 + i, rows, lanes] if i < 2 else rim_ref[1, rows, lanes]
                    got = jnp.dot(
                        turned[...], jnp.concatenate([low, high], axis=0), preferred_element_type=F32
                    )
                    got = (got + part_ref[i * 3 + j, :, lanes].astype(F32)) * SCALE
                    left, right = got[:, :128], got[:, 128:]
                    keep_ref[half, i * 3 + j] = jnp.where(core == 0, left, right)
                    send_ref[half, i * 3 + j] = jnp.where(core == 0, right, left).astype(BF)
            return carry

        lax.fori_loop(0, 3, multiply, 0)

    return call(
        kernel,
        (shape((2, 9, 192, 128), F32), shape((2, 9, 192, 128))),
        [(coords, pltpu.SMEM)] + [(a, None) for a in (field, rim, pre_grad, part)],
        [pltpu.VMEM((128, 128), F32), pltpu.VMEM((128, 128), F32), pltpu.VMEM((192, 256), BF)],
        COST[3],
        0,
    )


def add_cores(coords, keep, got):
    def kernel(co, keep_ref, got_ref, stay_ref, send_ref):
        far = co[3]
        stay_ref[...] = keep_ref[far] + got_ref[far].astype(F32)
        send_ref[...] = (keep_ref[1 - far] + got_ref[1 - far].astype(F32)).astype(BF)

    return call(
        kernel,
        (shape((9, 192, 128), F32), shape((9, 192, 128))),
        [(coords, pltpu.SMEM), (keep, None), (got, None)],
        (),
        COST[0],
        4_000_000,
    )


def add_far(coords, stay, got):
    def kernel(co, stay_ref, got_ref, keep_ref, send_ref, total, turned):
        parity = co[4] & 1
        total[...] = (stay_ref[...] + got_ref[...].astype(F32)).reshape(1728, 128)
        for t in range(14):
            width = min(128, 1728 - t * 128)
            block = total[t * 128 : t * 128 + width, :].T.reshape(8, 16, width)
            turned[:, :, t * 128 : t * 128 + width] = block
        for m in range(4):
            keep_ref[m] = turned[2 * m + parity]
            send_ref[m] = turned[2 * m + 1 - parity].astype(BF)

    return call(
        kernel,
        (shape((4, 16, 1728), F32), shape((4, 16, 1728))),
        [(coords, pltpu.SMEM), (stay, None), (got, None)],
        [pltpu.VMEM((1728, 128), F32), pltpu.VMEM((8, 16, 1728), F32)],
        COST[6],
        2_000_000,
    )


def add_near(coords, keep, got):
    def kernel(co, keep_ref, got_ref, *outs):
        own = co[4] // 2
        for d in range(4):
            at = (own + d) & 3
            outs[d][...] = (keep_ref[at] + got_ref[at].astype(F32)).astype(outs[d].dtype)

    return call(
        kernel,
        (shape((16, 1728), F32),) + (shape((16, 1728)),) * 3,
        [(coords, pltpu.SMEM), (keep, None), (got, None)],
        (),
        COST[5],
        1_000_000,
    )


def last_sums(regions, parts):
    def kernel(r0, r1, r2, r3, parts_ref, filter_ref, input_ref, total, pairs, wide):
        s = parts_ref[0].astype(F32)
        for f in range(1, 8):
            s = s + parts_ref[f].astype(F32)
        wide[0:512, :] = s.reshape(512, 128)
        from_pairs(wide, input_ref, range(8))
        for t in range(14):
            width = min(128, 1728 - t * 128)
            lanes = slice(t * 128, t * 128 + width)
            s = r0[:, lanes].astype(F32)
            for ref in (r1, r2, r3):
                s = s + ref[:, lanes].astype(F32)
            total[:, 0:width] = s
            even, odd = total[pl.ds(0, 8, stride=2), :], total[pl.ds(1, 8, stride=2), :]
            for u in range(width // 64):
                pick = slice(u * 64, u * 64 + 64)
                at = (2 * t + u) * 8
                pairs[at : at + 8, :] = jnp.concatenate([even[:, pick], odd[:, pick]], axis=1)
        filter_ref[...] = pairs[...].reshape(27, 8, 128)

    return call(
        kernel,
        (shape((27, 8, 128), F32), shape((8, 4, 2048))),
        [(part, None) for part in regions] + [(parts, None)],
        [pltpu.VMEM((16, 128), F32), pltpu.VMEM((216, 128), F32), pltpu.VMEM((576, 128), F32)],
        COST[4],
        1_800_000,
    )


def place_grad(rim, x, y, v):
    low, high = stacked_depth(v.astype(F32))
    for half in range(2):
        lanes = slice(half * 128, half * 128 + 128)
        rim[x, y * 32 : y * 32 + 16, lanes] = low[half].astype(BF)
        rim[x, y * 32 + 16 : y * 32 + 32, lanes] = high[half].astype(BF)


def input_layers(rows, back_ref, total, store):
    for n in range(2):
        lanes = slice(n * 256, n * 256 + 256)
        acc = jnp.zeros((256, 256), F32)
        for i in range(3):
            for j in range(3):
                acc = acc + jnp.dot(
                    jnp.concatenate([rows(u, 2 - i, (2 - j) * 32) for u in range(2)], axis=0),
                    back_ref[i * 3 + j, :, lanes],
                    preferred_element_type=F32,
                )
        total[:, lanes] = acc
    for u in range(2):
        for y in range(4):
            at = u * 128 + y * 32
            for f in range(8):
                lanes = slice(f * 64, f * 64 + 64)
                pair = jnp.concatenate([total[at : at + 16, lanes], total[at + 16 : at + 32, lanes]], axis=1)
                store(f, u, y, pair.astype(BF))


def input_grad_inner(coords, pre_grad, y_before, y_after, back):
    def kernel(co, pre_ref, yb, ya, back_ref, out_ref, rim, total):
        y_low, y_high = co[4] > 0, co[4] < 7

        def place(x, carry):
            place_grad(rim, x, 0, masked(yb[x], y_low))
            place_grad(rim, x, 5, masked(ya[x], y_high))
            for y in range(4):
                place_grad(rim, x, y + 1, pre_ref[x, y])
            return carry

        lax.fori_loop(0, 8, place, 0)

        def multiply(h, carry):
            def store(f, u, y, block):
                out_ref[f, 2 * h + u, y] = block

            input_layers(lambda u, d, at: rim[2 * h + u + d, at : at + 128, :], back_ref, total, store)
            return carry

        lax.fori_loop(0, 3, multiply, 0)

    return call(
        kernel,
        shape((8, 6, 4, 16, 128)),
        [(coords, pltpu.SMEM)] + [(a, None) for a in (pre_grad, y_before, y_after, back)],
        [pltpu.VMEM((8, 192, 256), BF), pltpu.VMEM((256, 512), F32)],
        COST[1],
        0,
    )


def input_grad_outer(coords, pre_grad, y_before, y_after, x_near, x_far, back, inner):
    def kernel(co, pre_ref, yb, ya, near_ref, far_ref, back_ref, inner_ref, out_ref, rim, total):
        y_low, y_high, x_low, x_high = co[4] > 0, co[4] < 7, co[5] > 0, co[5] < 3
        odd = co[2] > 0
        for y in range(6):
            beside = {0: y_low, 5: y_high}.get(y, True)
            near, far = near_ref[y], far_ref[y]
            before, after = jnp.where(odd, near, far), jnp.where(odd, far, near)
            place_grad(rim, 0, y, masked(before, jnp.logical_and(x_low, beside)))
            place_grad(rim, 5, y, masked(after, jnp.logical_and(x_high, beside)))
        for at, x in ((1, 0), (2, 1), (3, 6), (4, 7)):
            place_grad(rim, at, 0, masked(yb[x], y_low))
            place_grad(rim, at, 5, masked(ya[x], y_high))
            for y in range(4):
                place_grad(rim, at, y + 1, pre_ref[x, y])

        def store(f, u, y, block):
            out_ref[f, 7 * u, y] = block

        input_layers(lambda u, d, at: rim[3 * u + d, at : at + 128, :], back_ref, total, store)
        for f in range(8):
            out_ref[f, 1:7] = inner_ref[f]

    return call(
        kernel,
        shape((8,) + PIECE),
        [(coords, pltpu.SMEM)]
        + [(a, None) for a in (pre_grad, y_before, y_after, x_near, x_far, back, inner)],
        [pltpu.VMEM((6, 192, 256), BF), pltpu.VMEM((256, 512), F32)],
        COST[2],
        0,
    )


def both_ways(last, first, axis, size):
    return (
        lax.ppermute(last, axis, [(i, (i + 1) % size) for i in range(size)]),
        lax.ppermute(first, axis, [((i + 1) % size, i) for i in range(size)]),
    )


def x_rims(near, far):
    return (
        lax.ppermute(near, "sx", [(i, i ^ 1) for i in range(4)]),
        lax.ppermute(far, "sx", [(1, 2), (2, 1)]),
    )


def exchange(parts, axis):
    return lax.all_to_all(parts, axis, 0, 0)


def per_device(activations, weights, out_grad):
    filt, sx, sy = (lax.axis_index(a) for a in ("filt", "sx", "sy"))
    coords = jnp.stack([filt // 4, filt % 4, sx % 2, sx // 2, sy, sx, 0, 0]).astype(jnp.int32)
    cells = prepare_gather(activations[0, 0])
    cells, weights, out_grad = lax.optimization_barrier((cells, weights, out_grad))
    cells = exchange(cells, "filt")
    fore, back, prepared = prepare_weights(weights[0])
    grad = prepare_field(out_grad[0, 0])
    last, first, token = gather_sides(cells, prepared)
    y_before, y_after = both_ways(last, first, "sy", 8)
    field, total, token = forward_own(cells, fore, token)
    near, far = gather_edges(coords, cells, y_before, y_after, token)
    near, far, total = lax.optimization_barrier((near, far, total))
    x_near, x_far = x_rims(near, far)
    field, out_inner, pre_inner = forward_inner(coords, field, total, y_before, y_after, fore, grad)
    part, token = filter_grad_inner(field, pre_inner)
    rim, outputs, pre_grad, g_first, g_last = forward_outer(
        coords, field, x_near, x_far, fore, grad, out_inner, pre_inner, token
    )

    gy_before, gy_after = both_ways(g_last, g_first, "sy", 8)
    keep, send = filter_grad(coords, field, rim, pre_grad, part)
    got = lax.ppermute(send, "sx", [(i, i ^ 1) for i in range(4)])
    stay, send = add_cores(coords, keep, got)
    stay, pre_grad, gy_before, gy_after = lax.optimization_barrier((stay, pre_grad, gy_before, gy_after))
    got = lax.ppermute(send, "sx", [(i, i ^ 2) for i in range(4)])
    gx_near, gx_far = x_rims(*grad_edges(coords, pre_grad, gy_before, gy_after))

    inner = input_grad_inner(coords, pre_grad, gy_before, gy_after, back)
    parts = input_grad_outer(coords, pre_grad, gy_before, gy_after, gx_near, gx_far, back, inner)
    parts, got = lax.optimization_barrier((parts, got))
    parts = exchange(parts, "filt")
    keep, send = add_far(coords, stay, got)
    got = lax.ppermute(send, "sy", [(i, i ^ 1) for i in range(8)])
    regions = list(add_near(coords, keep, got))
    for d in (2, 1, 3):
        regions[d] = lax.ppermute(regions[d], "sy", [(i, (i + 2 * d) % 8) for i in range(8)])
    weight_grad, input_grad = last_sums(regions, parts)
    return outputs[None, None], input_grad[None, None], weight_grad.reshape(1, 27, 1024)


def solution(mesh):
    in_specs = (
        P("filt", None, "sx", "sy", None),
        P("filt", None, None),
        P("filt", None, "sx", "sy", None),
    )
    out_specs = (
        P("filt", None, "sx", "sy", None),
        P("filt", None, "sx", "sy", None),
        P("filt", None, ("sx", "sy")),
    )
    return jax.shard_map(
        per_device, mesh=mesh, in_specs=in_specs, out_specs=out_specs, check_vma=False
    )
```

```python
import math

import jax
import jax.numpy as jnp
from jax import lax
from jax.experimental import pallas as pl
from jax.experimental.pallas import tpu as pltpu
from jax.sharding import PartitionSpec as P

BF = jnp.bfloat16
F32 = jnp.float32
LEAK = 0.2
SCALE = 1.0 / math.sqrt(32768.0)
URGENT = 20_000_000_000
COST = [20000000000, 4000000000, 500000000, 5000000000, 0, 20000000000, 20000000000]
PIECE = (8, 4, 16, 128)


def call(kernel, outs, ins, scratch=(), flops=0, nbytes=0):
    return pl.pallas_call(
        kernel,
        out_shape=outs,
        in_specs=[
            pl.BlockSpec(memory_space=pltpu.VMEM if space is None else space)
            for _, space in ins
        ],
        out_specs=jax.tree.map(
            lambda out: pl.BlockSpec(
                memory_space=pltpu.VMEM if isinstance(out, jax.ShapeDtypeStruct) else pl.ANY
            ),
            outs,
        ),
        scratch_shapes=list(scratch),
        compiler_params=pltpu.CompilerParams(vmem_limit_bytes=14 << 20),
        cost_estimate=pl.CostEstimate(flops=flops, bytes_accessed=nbytes, transcendentals=0),
    )(*[array for array, _ in ins])


def shape(dims, dtype=BF):
    return jax.ShapeDtypeStruct(dims, dtype)


TOKEN = shape((8, 128), F32)


def down(v):
    rows = lax.broadcasted_iota(jnp.int32, v.shape, 0)
    return jnp.where(rows == 0, 0.0, pltpu.roll(v, 1, 0))


def up(v):
    rows = lax.broadcasted_iota(jnp.int32, v.shape, 0)
    return jnp.where(rows == v.shape[0] - 1, 0.0, pltpu.roll(v, v.shape[0] - 1, 0))


def to_pairs(field_ref, pair_ref, wide):
    for x in range(8):
        rows = field_ref[x].astype(F32)
        for t in range(16):
            wide[pl.ds(x * 64 + t, 4, stride=16), :] = rows[:, t * 128 : (t + 1) * 128]
    pair_ref[...] = wide[0:512, :].reshape(PIECE).astype(BF)


def from_pairs(wide, field_ref, layers):
    for n, x in enumerate(layers):
        parts = [wide[pl.ds(n * 64 + t, 4, stride=16), :] for t in range(16)]
        field_ref[x] = jnp.concatenate(parts, axis=1).astype(BF)


def prepare_field(field):
    def kernel(field_ref, pair_ref, wide):
        to_pairs(field_ref, pair_ref, wide)

    return call(
        kernel, shape(PIECE), [(field, None)], [pltpu.VMEM((576, 128), F32)], 0, 400_000
    )


def prepare_gather(field):
    def kernel(field_ref, out_ref, wide):
        for x in range(8):
            rows = field_ref[x].astype(F32)
            for t in range(16):
                wide[pl.ds(x * 16 + t, 4, stride=128), :] = rows[:, t * 128 : (t + 1) * 128]
        for y in range(4):
            row = wide[y * 128 : y * 128 + 128, :].reshape(8, 16, 128).astype(BF)
            for f in range(8):
                out_ref[f, y] = row

    return call(
        kernel,
        shape((8, 4, 8, 16, 128)),
        [(field, None)],
        [pltpu.VMEM((1024, 128), F32)],
        0,
        1_300_000,
    )


def gather_sides(cells, prepared):
    def kernel(cells_ref, prepared_ref, last_ref, first_ref, token_ref, sems):
        token_ref[...] = prepared_ref[...]
        copies = [
            pltpu.make_async_copy(cells_ref.at[:, 3], last_ref, sems.at[0]),
            pltpu.make_async_copy(cells_ref.at[:, 0], first_ref, sems.at[1]),
        ]
        for copy in copies:
            copy.start()
        for copy in copies:
            copy.wait()

    out = shape((8, 8, 16, 128))
    ins = [(cells, pl.ANY), (prepared, None)]
    return call(kernel, (out, out, TOKEN), ins, [pltpu.SemaphoreType.DMA((2,))], 0, 1_000_000)


def gather_edges(coords, cells, y_before, y_after, token):
    def kernel(co, cells_ref, yb, ya, token_ref, near_ref, far_ref):
        def give(last_ref, first_ref):
            for out_ref, x in ((last_ref, 7), (first_ref, 0)):
                for f in range(8):
                    out_ref[f, 0] = yb[f, x]
                    out_ref[f, 5] = ya[f, x]
                    for y in range(4):
                        out_ref[f, y + 1] = cells_ref[f, y, x]

        pl.when(co[2] == 0)(lambda: give(near_ref, far_ref))
        pl.when(co[2] == 1)(lambda: give(far_ref, near_ref))

    out = shape((8, 6, 16, 128))
    ins = [(coords, pltpu.SMEM)] + [(a, None) for a in (cells, y_before, y_after, token)]
    return call(kernel, (out, out), ins, (), 0, 400_000)


def grad_edges(coords, pre_grad, y_before, y_after):
    def kernel(co, pre_ref, yb, ya, near_ref, far_ref):
        for out_ref, x in ((near_ref, 7 - 7 * co[2]), (far_ref, 7 * co[2])):
            out_ref[0] = yb[x]
            out_ref[1:5] = pre_ref[x]
            out_ref[5] = ya[x]

    out = shape((6, 16, 128))
    ins = [(coords, pltpu.SMEM)] + [(a, None) for a in (pre_grad, y_before, y_after)]
    return call(kernel, (out, out), ins, (), 0, 0)


def prepare_weights(weights):
    def kernel(w_ref, fore_ref, back_out, done_ref, tall, even, odd, back_ref, sems):
        def spread(t, carry):
            lanes = pl.ds(pl.multiple_of(t * 128, 128), 128)
            tall[pl.ds(t, 27, stride=256), :] = w_ref[:, lanes].astype(F32)
            return carry

        lax.fori_loop(0, 256, spread, 0, unroll=8)

        def place(ij, carry):
            taps = [tall[pl.ds(pl.multiple_of((ij * 3 + k) * 256, 256), 256), :] for k in range(3)]
            zero = jnp.zeros((256, 64), F32)
            for par in range(2):
                lanes = slice(par * 64, par * 64 + 64)
                even[pl.ds(par, 256, stride=2), :] = jnp.concatenate(
                    [taps[0][:, lanes], taps[1][:, lanes]], axis=1
                )
                odd[pl.ds(par, 256, stride=2), :] = jnp.concatenate([taps[2][:, lanes], zero], axis=1)
            fore_ref[ij, :, 0:128] = even[...].astype(BF)
            fore_ref[ij, :, 128:256] = odd[...].astype(BF)
            for c in range(4):
                rows = slice(c * 128, c * 128 + 128)
                back_ref[ij, 0:128, rows] = even[rows, :].T.astype(BF)
                back_ref[ij, 128:256, rows] = odd[rows, :].T.astype(BF)
            copy_out(ij).start()
            return carry

        def copy_out(ij):
            return pltpu.make_async_copy(back_ref.at[ij], back_out.at[ij], sems.at[ij])

        def finish(ij, carry):
            copy_out(ij).wait()
            return carry

        lax.fori_loop(0, 9, place, 0)
        lax.fori_loop(0, 9, finish, 0)
        done_ref[...] = even[0:8, :]

    return call(
        kernel,
        (shape((9, 512, 256)), pltpu.HBM((9, 256, 512), BF), TOKEN),
        [(weights, None)],
        [
            pltpu.VMEM((32 * 256, 128), F32),
            pltpu.VMEM((512, 128), F32),
            pltpu.VMEM((512, 128), F32),
            pltpu.VMEM((9, 256, 512), BF),
            pltpu.SemaphoreType.DMA((9,)),
        ],
        0,
        8_000_000,
    )


def masked(v, inside):
    return jnp.where(inside, v, jnp.zeros_like(v))


def place_cell(field_ref, x, y, take):
    for q in range(4):
        a, b = take(2 * q), take(2 * q + 1)
        lanes = slice(q * 128, q * 128 + 128)
        field_ref[x, y * 32 : y * 32 + 16, lanes] = jnp.concatenate([a[:, :64], b[:, :64]], axis=1)
        field_ref[x, y * 32 + 16 : y * 32 + 32, lanes] = jnp.concatenate([a[:, 64:], b[:, 64:]], axis=1)


def convolved(rows, fore_ref):
    acc = jnp.zeros((256, 256), F32)
    for i in range(3):
        for j in range(3):
            acc = acc + jnp.dot(
                jnp.concatenate([rows(u, i, j * 32) for u in range(2)], axis=0),
                fore_ref[i * 3 + j],
                preferred_element_type=F32,
            )
    return acc


def finish_cell(total, start, grad):
    even, odd = total[pl.ds(start, 16), :], total[pl.ds(start + 16, 16), :]
    pre = (
        jnp.concatenate([down(odd[:, 0:64]), even[:, 0:64]], axis=1)
        + jnp.concatenate([even[:, 64:128], odd[:, 64:128]], axis=1)
        + jnp.concatenate([odd[:, 128:192], up(even[:, 128:192])], axis=1)
    )
    e = jnp.exp(-jnp.abs(pre))
    soft = jnp.maximum(pre, 0.0) + jnp.log1p(e)
    slope = jnp.where(pre >= 0, 1.0, e) / (1.0 + e)
    value = LEAK * pre + (1.0 - LEAK) * (soft - math.log(2.0))
    return value, (grad.astype(F32) * (LEAK + (1.0 - LEAK) * slope)).astype(BF)


def forward_own(cells, fore, token):
    def kernel(cells_ref, fore_ref, token_ref, field_ref, total_ref, done_ref):
        def place(x, carry):
            field_ref[x, 0:32, :] = jnp.zeros((32, 512), BF)
            field_ref[x, 160:192, :] = jnp.zeros((32, 512), BF)
            for y in range(4):
                place_cell(field_ref, x, y + 1, lambda f: cells_ref[f, y, x])
            return carry

        lax.fori_loop(0, 8, place, 0)

        def multiply(h, carry):
            start = pl.multiple_of(h * 256, 256)
            total_ref[pl.ds(start, 256), :] = convolved(
                lambda u, i, at: field_ref[2 * h + u + i, at : at + 128, :], fore_ref
            )
            return carry

        lax.fori_loop(0, 3, multiply, 0)
        done_ref[...] = token_ref[...]

    return call(
        kernel,
        (shape((8, 192, 512)), shape((768, 256), F32), TOKEN),
        [(a, None) for a in (cells, fore, token)],
        (),
        4_000_000_000,
        5_000_000,
    )


def forward_inner(coords, field, total, y_before, y_after, fore, grad):
    def kernel(
        co, own_ref, total_ref, yb, ya, fore_ref, grad_ref, field_ref, out_ref, pre_ref, sides, wide
    ):
        y_low, y_high = co[4] > 0, co[4] < 7

        def place(x, carry):
            field_ref[x, 32:160, :] = own_ref[x, 32:160, :]
            place_cell(field_ref, x, 0, lambda f: masked(yb[f, x], y_low))
            place_cell(field_ref, x, 5, lambda f: masked(ya[f, x], y_high))
            return carry

        lax.fori_loop(0, 8, place, 0)

        for side, (at, j, y) in enumerate(((0, 0, 0), (160, 2, 3))):
            acc = jnp.concatenate(
                [total_ref[x * 128 + y * 32 : x * 128 + y * 32 + 32, :] for x in range(6)], axis=0
            )
            for i in range(3):
                rows = [field_ref[x + i, at : at + 32, :] for x in range(6)]
                acc = acc + jnp.dot(
                    jnp.concatenate(rows, axis=0), fore_ref[i * 3 + j], preferred_element_type=F32
                )
            sides[side] = acc

        def finish(x, carry):
            for y in range(4):
                if y in (0, 3):
                    source, start = sides.at[y // 3], pl.multiple_of(x * 32, 32)
                else:
                    source, start = total_ref, pl.multiple_of(x * 128 + y * 32, 32)
                value, turned = finish_cell(source, start, grad_ref[x + 1, y])
                wide[pl.ds(pl.multiple_of(x * 64 + y * 16, 16), 16), :] = value
                pre_ref[x, y] = turned
            return carry

        lax.fori_loop(0, 6, finish, 0)
        from_pairs(wide, out_ref, range(6))

    return call(
        kernel,
        (shape((8, 192, 512)), shape((6, 4, 2048)), shape((6, 4, 16, 128))),
        [(coords, pltpu.SMEM)]
        + [(a, None) for a in (field, total, y_before, y_after, fore, grad)],
        [pltpu.VMEM((2, 192, 256), F32), pltpu.VMEM((448, 128), F32)],
        1_000_000_000,
        6_000_000,
    )


def forward_outer(coords, field, x_near, x_far, fore, grad, out_inner, pre_inner, token):
    def kernel(
        co, field_ref, near_ref, far_ref, fore_ref, grad_ref, out_in, pre_in, token_ref,
        rim_ref, out_ref, pre_ref, first_ref, last_ref, total, wide,
    ):
        y_low, y_high, x_low, x_high = co[4] > 0, co[4] < 7, co[5] > 0, co[5] < 3
        odd = co[2] > 0
        for y in range(6):
            beside = {0: y_low, 5: y_high}.get(y, True)
            place_cell(
                rim_ref,
                0,
                y,
                lambda f: masked(jnp.where(odd, near_ref[f, y], far_ref[f, y]), jnp.logical_and(x_low, beside)),
            )
            place_cell(
                rim_ref,
                1,
                y,
                lambda f: masked(jnp.where(odd, far_ref[f, y], near_ref[f, y]), jnp.logical_and(x_high, beside)),
            )

        def rows(u, i, at):
            if u == 0:
                return (field_ref[i - 1] if i else rim_ref[0])[at : at + 128, :]
            return (field_ref[6 + i] if i < 2 else rim_ref[1])[at : at + 128, :]

        total[...] = convolved(rows, fore_ref)
        for n, x in enumerate((0, 7)):
            for y in range(4):
                value, turned = finish_cell(total, n * 128 + y * 32, grad_ref[x, y])
                wide[n * 64 + y * 16 : n * 64 + y * 16 + 16, :] = value
                pre_ref[x, y] = turned
        from_pairs(wide, out_ref, (0, 7))
        out_ref[1:7] = out_in[...]
        pre_ref[1:7] = pre_in[...]
        for x in range(8):
            first_ref[x] = pre_ref[x, 0]
            last_ref[x] = pre_ref[x, 3]

    return call(
        kernel,
        (
            shape((2, 192, 512)),
            shape((8, 4, 2048)),
            shape(PIECE),
            shape((8, 16, 128)),
            shape((8, 16, 128)),
        ),
        [(coords, pltpu.SMEM)]
        + [(a, None) for a in (field, x_near, x_far, fore, grad, out_inner, pre_inner, token)],
        [pltpu.VMEM((256, 256), F32), pltpu.VMEM((192, 128), F32)],
        2_000_000_000,
        6_000_000,
    )


def stacked_depth(v):
    even, odd = v[:, :64], v[:, 64:]
    zero = jnp.zeros((16, 64), F32)
    return (
        (jnp.concatenate([odd, even], axis=1), jnp.concatenate([down(odd), zero], axis=1)),
        (jnp.concatenate([up(even), odd], axis=1), jnp.concatenate([even, zero], axis=1)),
    )


def turn_grad(pre_ref, layers, first, second, turned):
    for n, x in enumerate(layers):
        for y in range(4):
            low, high = stacked_depth(pre_ref[x, y].astype(F32))
            first[y * 32 : y * 32 + 16, :] = low[0]
            second[y * 32 : y * 32 + 16, :] = low[1]
            first[y * 32 + 16 : y * 32 + 32, :] = high[0]
            second[y * 32 + 16 : y * 32 + 32, :] = high[1]
        turned[0:128, n * 128 : n * 128 + 128] = first[...].T.astype(BF)
        turned[128:192, n * 128 : n * 128 + 128] = second[...].T[0:64].astype(BF)


def filter_grad_inner(field, pre_inner):
    def kernel(field_ref, pre_ref, part_ref, done_ref, first, second, turned):
        turn_grad(pre_ref, range(6), first, second, turned)

        def multiply(j, carry):
            rows = pl.ds(pl.multiple_of(j * 32, 32), 128)
            for i in range(3):
                for half in range(2):
                    lanes = slice(half * 256, half * 256 + 256)
                    cells = [field_ref[x + i, rows, lanes] for x in range(6)]
                    got = jnp.dot(
                        turned[...], jnp.concatenate(cells, axis=0), preferred_element_type=F32
                    )
                    part_ref[i * 3 + j, :, lanes] = got.astype(part_ref.dtype)
            return carry

        lax.fori_loop(0, 3, multiply, 0)
        done_ref[...] = first[0:8, :]

    return call(
        kernel,
        (shape((9, 192, 512)), TOKEN),
        [(field, None), (pre_inner, None)],
        [pltpu.VMEM((128, 128), F32), pltpu.VMEM((128, 128), F32), pltpu.VMEM((192, 768), BF)],
        3_000_000_000,
        0,
    )


def filter_grad(coords, field, rim, pre_grad, part):
    def kernel(co, field_ref, rim_ref, pre_ref, part_ref, keep_ref, send_ref, first, second, turned):
        core = co[2]
        turn_grad(pre_ref, (0, 7), first, second, turned)

        def multiply(j, carry):
            rows = pl.ds(pl.multiple_of(j * 32, 32), 128)
            for i in range(3):
                for half in range(2):
                    lanes = slice(half * 256, half * 256 + 256)
                    low = field_ref[i - 1, rows, lanes] if i else rim_ref[0, rows, lanes]
                    high = field_ref[6 + i, rows, lanes] if i < 2 else rim_ref[1, rows, lanes]
                    got = jnp.dot(
                        turned[...], jnp.concatenate([low, high], axis=0), preferred_element_type=F32
                    )
                    got = (got + part_ref[i * 3 + j, :, lanes].astype(F32)) * SCALE
                    left, right = got[:, :128], got[:, 128:]
                    keep_ref[half, i * 3 + j] = jnp.where(core == 0, left, right)
                    send_ref[half, i * 3 + j] = jnp.where(core == 0, right, left).astype(BF)
            return carry

        lax.fori_loop(0, 3, multiply, 0)

    return call(
        kernel,
        (shape((2, 9, 192, 128), F32), shape((2, 9, 192, 128))),
        [(coords, pltpu.SMEM)] + [(a, None) for a in (field, rim, pre_grad, part)],
        [pltpu.VMEM((128, 128), F32), pltpu.VMEM((128, 128), F32), pltpu.VMEM((192, 256), BF)],
        COST[3],
        0,
    )


def add_cores(coords, keep, got):
    def kernel(co, keep_ref, got_ref, stay_ref, send_ref):
        far = co[3]
        stay_ref[...] = keep_ref[far] + got_ref[far].astype(F32)
        send_ref[...] = (keep_ref[1 - far] + got_ref[1 - far].astype(F32)).astype(BF)

    return call(
        kernel,
        (shape((9, 192, 128), F32), shape((9, 192, 128))),
        [(coords, pltpu.SMEM), (keep, None), (got, None)],
        (),
        COST[0],
        4_000_000,
    )


def add_far(coords, stay, got):
    def kernel(co, stay_ref, got_ref, keep_ref, send_ref, total, turned):
        parity = co[4] & 1
        total[...] = (stay_ref[...] + got_ref[...].astype(F32)).reshape(1728, 128)
        for t in range(14):
            width = min(128, 1728 - t * 128)
            block = total[t * 128 : t * 128 + width, :].T.reshape(8, 16, width)
            turned[:, :, t * 128 : t * 128 + width] = block
        for m in range(4):
            keep_ref[m] = turned[2 * m + parity]
            send_ref[m] = turned[2 * m + 1 - parity].astype(BF)

    return call(
        kernel,
        (shape((4, 16, 1728), F32), shape((4, 16, 1728))),
        [(coords, pltpu.SMEM), (stay, None), (got, None)],
        [pltpu.VMEM((1728, 128), F32), pltpu.VMEM((8, 16, 1728), F32)],
        COST[6],
        2_000_000,
    )


def add_near(coords, keep, got):
    def kernel(co, keep_ref, got_ref, *outs):
        own = co[4] // 2
        for d in range(4):
            at = (own + d) & 3
            outs[d][...] = (keep_ref[at] + got_ref[at].astype(F32)).astype(outs[d].dtype)

    return call(
        kernel,
        (shape((16, 1728), F32),) + (shape((16, 1728)),) * 3,
        [(coords, pltpu.SMEM), (keep, None), (got, None)],
        (),
        COST[5],
        1_000_000,
    )


def last_sums(regions, parts):
    def kernel(r0, r1, r2, r3, parts_ref, filter_ref, input_ref, total, pairs, wide):
        s = parts_ref[0].astype(F32)
        for f in range(1, 8):
            s = s + parts_ref[f].astype(F32)
        wide[0:512, :] = s.reshape(512, 128)
        from_pairs(wide, input_ref, range(8))
        for t in range(14):
            width = min(128, 1728 - t * 128)
            lanes = slice(t * 128, t * 128 + width)
            s = r0[:, lanes].astype(F32)
            for ref in (r1, r2, r3):
                s = s + ref[:, lanes].astype(F32)
            total[:, 0:width] = s
            even, odd = total[pl.ds(0, 8, stride=2), :], total[pl.ds(1, 8, stride=2), :]
            for u in range(width // 64):
                pick = slice(u * 64, u * 64 + 64)
                at = (2 * t + u) * 8
                pairs[at : at + 8, :] = jnp.concatenate([even[:, pick], odd[:, pick]], axis=1)
        filter_ref[...] = pairs[...].reshape(27, 8, 128)

    return call(
        kernel,
        (shape((27, 8, 128), F32), shape((8, 4, 2048))),
        [(part, None) for part in regions] + [(parts, None)],
        [pltpu.VMEM((16, 128), F32), pltpu.VMEM((216, 128), F32), pltpu.VMEM((576, 128), F32)],
        COST[4],
        1_800_000,
    )


def place_grad(rim, x, y, v):
    low, high = stacked_depth(v.astype(F32))
    for half in range(2):
        lanes = slice(half * 128, half * 128 + 128)
        rim[x, y * 32 : y * 32 + 16, lanes] = low[half].astype(BF)
        rim[x, y * 32 + 16 : y * 32 + 32, lanes] = high[half].astype(BF)


def input_layers(rows, back_ref, total, store):
    for n in range(2):
        lanes = slice(n * 256, n * 256 + 256)
        acc = jnp.zeros((256, 256), F32)
        for i in range(3):
            for j in range(3):
                acc = acc + jnp.dot(
                    jnp.concatenate([rows(u, 2 - i, (2 - j) * 32) for u in range(2)], axis=0),
                    back_ref[i * 3 + j, :, lanes],
                    preferred_element_type=F32,
                )
        total[:, lanes] = acc
    for u in range(2):
        for y in range(4):
            at = u * 128 + y * 32
            for f in range(8):
                lanes = slice(f * 64, f * 64 + 64)
                pair = jnp.concatenate([total[at : at + 16, lanes], total[at + 16 : at + 32, lanes]], axis=1)
                store(f, u, y, pair.astype(BF))


def input_grad_inner(coords, pre_grad, y_before, y_after, back):
    def kernel(co, pre_ref, yb, ya, back_ref, out_ref, rim, total):
        y_low, y_high = co[4] > 0, co[4] < 7

        def place(x, carry):
            place_grad(rim, x, 0, masked(yb[x], y_low))
            place_grad(rim, x, 5, masked(ya[x], y_high))
            for y in range(4):
                place_grad(rim, x, y + 1, pre_ref[x, y])
            return carry

        lax.fori_loop(0, 8, place, 0)

        def multiply(h, carry):
            def store(f, u, y, block):
                out_ref[f, 2 * h + u, y] = block

            input_layers(lambda u, d, at: rim[2 * h + u + d, at : at + 128, :], back_ref, total, store)
            return carry

        lax.fori_loop(0, 3, multiply, 0)

    return call(
        kernel,
        shape((8, 6, 4, 16, 128)),
        [(coords, pltpu.SMEM)] + [(a, None) for a in (pre_grad, y_before, y_after, back)],
        [pltpu.VMEM((8, 192, 256), BF), pltpu.VMEM((256, 512), F32)],
        COST[1],
        0,
    )


def input_grad_outer(coords, pre_grad, y_before, y_after, x_near, x_far, back, inner):
    def kernel(co, pre_ref, yb, ya, near_ref, far_ref, back_ref, inner_ref, out_ref, rim, total):
        y_low, y_high, x_low, x_high = co[4] > 0, co[4] < 7, co[5] > 0, co[5] < 3
        odd = co[2] > 0
        for y in range(6):
            beside = {0: y_low, 5: y_high}.get(y, True)
            near, far = near_ref[y], far_ref[y]
            before, after = jnp.where(odd, near, far), jnp.where(odd, far, near)
            place_grad(rim, 0, y, masked(before, jnp.logical_and(x_low, beside)))
            place_grad(rim, 5, y, masked(after, jnp.logical_and(x_high, beside)))
        for at, x in ((1, 0), (2, 1), (3, 6), (4, 7)):
            place_grad(rim, at, 0, masked(yb[x], y_low))
            place_grad(rim, at, 5, masked(ya[x], y_high))
            for y in range(4):
                place_grad(rim, at, y + 1, pre_ref[x, y])

        def store(f, u, y, block):
            out_ref[f, 7 * u, y] = block

        input_layers(lambda u, d, at: rim[3 * u + d, at : at + 128, :], back_ref, total, store)
        for f in range(8):
            out_ref[f, 1:7] = inner_ref[f]

    return call(
        kernel,
        shape((8,) + PIECE),
        [(coords, pltpu.SMEM)]
        + [(a, None) for a in (pre_grad, y_before, y_after, x_near, x_far, back, inner)],
        [pltpu.VMEM((6, 192, 256), BF), pltpu.VMEM((256, 512), F32)],
        COST[2],
        0,
    )


def both_ways(last, first, axis, size):
    return (
        lax.ppermute(last, axis, [(i, (i + 1) % size) for i in range(size)]),
        lax.ppermute(first, axis, [((i + 1) % size, i) for i in range(size)]),
    )


def x_rims(near, far):
    return (
        lax.ppermute(near, "sx", [(i, i ^ 1) for i in range(4)]),
        lax.ppermute(far, "sx", [(1, 2), (2, 1)]),
    )


def exchange(parts, axis):
    return lax.all_to_all(parts, axis, 0, 0)


def per_device(activations, weights, out_grad):
    filt, sx, sy = (lax.axis_index(a) for a in ("filt", "sx", "sy"))
    coords = jnp.stack([filt // 4, filt % 4, sx % 2, sx // 2, sy, sx, 0, 0]).astype(jnp.int32)
    cells = prepare_gather(activations[0, 0])
    cells, weights, out_grad = lax.optimization_barrier((cells, weights, out_grad))
    cells = exchange(cells, "filt")
    fore, back, prepared = prepare_weights(weights[0])
    grad = prepare_field(out_grad[0, 0])
    last, first, token = gather_sides(cells, prepared)
    y_before, y_after = both_ways(last, first, "sy", 8)
    field, total, token = forward_own(cells, fore, token)
    near, far = gather_edges(coords, cells, y_before, y_after, token)
    near, far, total = lax.optimization_barrier((near, far, total))
    x_near, x_far = x_rims(near, far)
    field, out_inner, pre_inner = forward_inner(coords, field, total, y_before, y_after, fore, grad)
    part, token = filter_grad_inner(field, pre_inner)
    rim, outputs, pre_grad, g_first, g_last = forward_outer(
        coords, field, x_near, x_far, fore, grad, out_inner, pre_inner, token
    )

    gy_before, gy_after = both_ways(g_last, g_first, "sy", 8)
    keep, send = filter_grad(coords, field, rim, pre_grad, part)
    got = lax.ppermute(send, "sx", [(i, i ^ 1) for i in range(4)])
    stay, send = add_cores(coords, keep, got)
    stay, pre_grad, gy_before, gy_after = lax.optimization_barrier((stay, pre_grad, gy_before, gy_after))
    got = lax.ppermute(send, "sx", [(i, i ^ 2) for i in range(4)])
    gx_near, gx_far = x_rims(*grad_edges(coords, pre_grad, gy_before, gy_after))

    inner = input_grad_inner(coords, pre_grad, gy_before, gy_after, back)
    parts = input_grad_outer(coords, pre_grad, gy_before, gy_after, gx_near, gx_far, back, inner)
    parts, got = lax.optimization_barrier((parts, got))
    parts = exchange(parts, "filt")
    keep, send = add_far(coords, stay, got)
    got = lax.ppermute(send, "sy", [(i, i ^ 1) for i in range(8)])
    regions = list(add_near(coords, keep, got))
    for d in (2, 3, 1):
        regions[d] = lax.ppermute(regions[d], "sy", [(i, (i + 2 * d) % 8) for i in range(8)])
    weight_grad, input_grad = last_sums(regions, parts)
    return outputs[None, None], input_grad[None, None], weight_grad.reshape(1, 27, 1024)


def solution(mesh):
    in_specs = (
        P("filt", None, "sx", "sy", None),
        P("filt", None, None),
        P("filt", None, "sx", "sy", None),
    )
    out_specs = (
        P("filt", None, "sx", "sy", None),
        P("filt", None, "sx", "sy", None),
        P("filt", None, ("sx", "sy")),
    )
    return jax.shard_map(
        per_device, mesh=mesh, in_specs=in_specs, out_specs=out_specs, check_vma=False
    )
```
